32 devices in a mesh: lat: 8 (over z, y), lon: 4 (over x, core).
Axes of the slice: x: 2, y: 2, z: 4, core: 2. Of those that a mesh axis runs over, the one named last changes fastest.
Arguments:
- tokens: bfloat16 [4, 192, 360, 256], P(None, 'lat', 'lon'), may hold values from -6 to 6
- cotangent: bfloat16 [4, 192, 360, 256], P(None, 'lat', 'lon'), may hold values from -6 to 6
- w_qkv: bfloat16 [256, 768], replicated, may hold values from -0.375 to 0.375
- q_bias: bfloat16 [256], replicated, may hold values from -4 to 4
- v_bias: bfloat16 [256], replicated, may hold values from -1.5 to 1.5
- w_proj: bfloat16 [256, 256], replicated, may hold values from -0.375 to 0.375
- b_proj: bfloat16 [256], replicated, may hold values from -1.5 to 1.5
- w_up: bfloat16 [256, 1024], replicated, may hold values from -0.375 to 0.375
- b_up: bfloat16 [1024], replicated, may hold values from -6 to 6
- w_down: bfloat16 [1024, 256], replicated, may hold values from -0.1875 to 0.1875
- b_down: bfloat16 [256], replicated, may hold values from -3 to 3
- w_mod: bfloat16 [256, 1024], replicated, may hold values from -0.375 to 0.375
- b_mod: bfloat16 [1024], replicated, may hold values from -4 to 4
- rel_table: bfloat16 [4, 3, 23, 11], replicated, may hold values from -6 to 6
- crop_rows: int32 [8], replicated, may hold values from 6 to 24, as said below
- lead_hours: int32 [1], replicated, may hold values from 1 to 240
Outputs:
- mixed: bfloat16 [4, 192, 360, 256], P(None, 'lat', 'lon')
- token_grad: bfloat16 [4, 192, 360, 256], P(None, 'lat', 'lon')
- grad_qkv: float32 [256, 768], replicated
- grad_q_bias: float32 [256], replicated
- grad_v_bias: float32 [256], replicated
- grad_proj: float32 [256, 256], replicated
- grad_proj_bias: float32 [256], replicated
- grad_up: float32 [256, 1024], replicated
- grad_up_bias: float32 [1024], replicated
- grad_down: float32 [1024, 256], replicated
- grad_down_bias: float32 [256], replicated
- grad_mod: float32 [256, 1024], replicated
- grad_mod_bias: float32 [1024], replicated
- grad_table: float32 [4, 3, 23, 11], replicated
The draws below stay inside these ranges and needn't reach their ends.
Inputs may be any that keep to these rules, and one draw needn't show every extreme that they name: In each latitude band of 24 rows the crop holds the band's last crop_rows rows; some band is whole and some holds a quarter of 24 rows.
All inputs are finite; a program needn't handle non-finite values.
Results may differ from the reference program's by a relative error of at most 0.012.
Values may be sent and summed in bfloat16 or wider, within the bound.
A program may use at most 384 MiB of HBM per device.

```python
import math
import jax
import jax.numpy as jnp
from jax import lax

D = 256
FF = 1024
HEADS = 4
LEVELS = 4
WZ = 2
WY = 12
WX = 6
LAT_DEV = 24
LON_DEV = 90
NY = 192
NX = 360
BANDS = 8


def draw_crop_rows(key, part):
    key = jax.random.fold_in(key, 11)
    first_key, second_key = jax.random.split(key)
    crop_counts = jax.random.randint(first_key, (BANDS,), LAT_DEV // 4, LAT_DEV + 1)
    order = jax.random.permutation(second_key, BANDS)
    crop_counts = crop_counts.at[order[0]].set(LAT_DEV).at[order[1]].set(LAT_DEV // 4)
    return crop_counts.astype(jnp.int32)


def shard_levels(own_key, extent, shards, smallest, largest):
    factor_of, own = 1.0, jax.random.fold_in(own_key, 6)
    for position, shards_of in shards:
        draws = jnp.exp(jax.random.uniform(jax.random.fold_in(own, position), (shards_of,), jnp.float32, smallest / len(shards), largest / len(shards)))
        factor_of = factor_of * jnp.repeat(draws, extent[position] // shards_of).reshape([-1 if axis == position else 1 for axis in range(len(extent))])
    return factor_of


def gaussian(own_key, extent, width, most, shards=(), kind=jnp.bfloat16):
    loudness = shard_levels(own_key, extent, shards, -0.22, 0.18) if shards else 1.0
    drawn = jax.random.normal(own_key, extent, jnp.float32) * width * loudness
    return jnp.minimum(jnp.maximum(drawn, -most), most).astype(kind)


def setup_inputs(seed: int = 0) -> dict:
    arg_keys = jax.random.split(jax.random.key(seed), 17)
    return {
        "tokens": gaussian(arg_keys[0], (LEVELS, NY, NX, D), 1.0, 6.0, ((1, 8), (2, 4))),
        "cotangent": gaussian(arg_keys[1], (LEVELS, NY, NX, D), 1.0, 6.0, ((1, 8), (2, 4))),
        "w_qkv": gaussian(arg_keys[2], (D, 3 * D), D ** -0.5, 0.375),
        "q_bias": gaussian(arg_keys[3], (D,), 0.3, 4.0),
        "v_bias": gaussian(arg_keys[4], (D,), 0.1, 1.5),
        "w_proj": gaussian(arg_keys[5], (D, D), D ** -0.5, 0.375),
        "b_proj": gaussian(arg_keys[6], (D,), 0.1, 1.5),
        "w_up": gaussian(arg_keys[7], (D, FF), D ** -0.5, 0.375),
        "b_up": gaussian(arg_keys[8], (FF,), 0.5, 6.0),
        "w_down": gaussian(arg_keys[9], (FF, D), FF ** -0.5, 0.1875),
        "b_down": gaussian(arg_keys[10], (D,), 0.2, 3.0),
        "w_mod": gaussian(arg_keys[11], (D, 4 * D), D ** -0.5, 0.375),
        "b_mod": gaussian(arg_keys[12], (4 * D,), 0.3, 4.0),
        "rel_table": gaussian(arg_keys[13], (HEADS, 2 * WZ - 1, 2 * WY - 1, 2 * WX - 1), 0.5, 6.0),
        "crop_rows": draw_crop_rows(jax.random.fold_in(arg_keys[16], 71), 0),
        "lead_hours": jax.random.randint(arg_keys[15], (1,), 1, 241).astype(jnp.int32),
    }


@jax.custom_vjp
def low(v):
    return lax.optimization_barrier(v.astype(jnp.bfloat16)).astype(jnp.float32)

@jax.custom_vjp
def low_back(v):
    return v

def low_keep(v):
    return (low(v), None)

def low_pass(kept, grad):
    return (grad,)

def back_keep(v):
    return (v, None)

def back_low(kept, grad):
    return (low(grad),)
low.defvjp(low_keep, low_pass)
low_back.defvjp(back_keep, back_low)
NORM_EPSILON = 1e-05
MASKED_SCORE = -1000000000.0
PRECISE = lax.Precision.HIGHEST

def matmul(left, right):
    return jnp.dot(left, right, precision=PRECISE, preferred_element_type=jnp.float32)

def layer_norm(values):
    center = values - lax.optimization_barrier(jnp.mean(values, axis=-1, keepdims=True))
    spread = lax.optimization_barrier(jnp.mean(center * center, axis=-1, keepdims=True))
    return center * lax.rsqrt(spread + NORM_EPSILON)

def modulate(values, scale_vec, shift_vec):
    return layer_norm(values) * (1.0 + scale_vec) + shift_vec

def lead_context(lead_hours, feat_width):
    half_width = feat_width // 2
    fraction = jnp.arange(half_width, dtype=jnp.float32) / half_width
    angles = lead_hours.astype(jnp.float32)[0] * jnp.exp(-math.log(1000.0) * fraction)
    return jnp.concatenate([jnp.sin(angles), jnp.cos(angles)])

def one_hot_offsets(span_len):
    places = jnp.arange(span_len)
    offsets = places[:, None] - places[None, :] + span_len - 1
    return (offsets[:, :, None] == jnp.arange(2 * span_len - 1)[None, None, :]).astype(jnp.float32)

def relative_bias(table_bias):
    head_count = table_bias.shape[0]
    span_z = (table_bias.shape[1] + 1) // 2
    span_y = (table_bias.shape[2] + 1) // 2
    span_x = (table_bias.shape[3] + 1) // 2
    biases = jnp.einsum('habc,ika,jlb,mnc->hijmkln', table_bias, one_hot_offsets(span_z), one_hot_offsets(span_y), one_hot_offsets(span_x), precision=PRECISE)
    window = span_z * span_y * span_x
    return biases.reshape(head_count, window, window)

def to_groups(grid_field, per_group):
    level_count, row_count, col_count, feat_width = grid_field.shape
    pieces = grid_field.reshape(level_count // WZ, WZ, row_count // WY, WY, col_count // WX, WX, feat_width)
    pieces = pieces.transpose(0, 2, 4, 1, 3, 5, 6)
    return pieces.reshape(-1, per_group * WZ * WY * WX, feat_width)

def from_groups(groups, full_shape):
    level_count, row_count, col_count, feat_width = full_shape
    pieces = groups.reshape(level_count // WZ, row_count // WY, col_count // WX, WZ, WY, WX, feat_width)
    return pieces.transpose(0, 3, 1, 4, 2, 5, 6).reshape(level_count, row_count, col_count, feat_width)

def reference(tokens, cotangent, w_qkv, q_bias, v_bias, w_proj, b_proj, w_up, b_up, w_down, b_down, w_mod, b_mod, rel_table, crop_rows, lead_hours):
    level_count, row_count, col_count, feat_width = tokens.shape
    per_group = LON_DEV // WX
    window = WZ * WY * WX
    shifts = (WZ // 2, WY // 2, WX // 2)
    row_ids = jnp.arange(row_count, dtype=jnp.int32)
    crop_here = crop_rows[row_ids // LAT_DEV]
    valid_rows = (row_ids % LAT_DEV >= LAT_DEV - crop_here).astype(jnp.int32)
    level_part = (jnp.arange(level_count, dtype=jnp.int32) == 0).astype(jnp.int32)
    row_part = (row_ids < shifts[1]).astype(jnp.int32)
    segment = jnp.broadcast_to(2 * level_part[:, None, None] + row_part[None, :, None], (level_count, row_count, col_count))
    validity = jnp.broadcast_to(valid_rows[None, :, None], (level_count, row_count, col_count))

    def grouped(grid_field):
        rolled = jnp.roll(grid_field, (-shifts[0], -shifts[1], -shifts[2]), axis=(0, 1, 2))
        return to_groups(rolled, per_group)
    seg_groups = grouped(segment[..., None]).reshape(-1, per_group, window)
    valid_groups = grouped(validity[..., None]).reshape(-1, per_group, window)
    context = jax.nn.silu(lead_context(lead_hours, feat_width))
    head_dim = feat_width // HEADS
    score_scale = head_dim ** (-0.5)

    def forward(inputs, weight_qkv, bias_q, bias_v, weight_proj, bias_proj, weight_up, bias_up, weight_down, bias_down, weight_mod, bias_mod, table_bias):
        modulation = matmul(context[None, :], weight_mod)[0] + bias_mod
        shift_one, scale_one, shift_two, scale_two = jnp.split(modulation, 4)
        biases = relative_bias(table_bias)
        qkv_shift = jnp.concatenate([bias_q, jnp.zeros_like(bias_q), bias_v])

        def group_block(pieces):
            group_tokens, group_seg, group_valid = pieces
            count_win = group_seg.shape[0]
            projected = low(low_back(matmul(group_tokens, weight_qkv) + qkv_shift))
            split_heads = projected.reshape(count_win, window, 3, HEADS, head_dim)
            queries = split_heads[:, :, 0]
            keys_win = split_heads[:, :, 1]
            values_win = split_heads[:, :, 2]
            raw_scores = jnp.einsum('wqhd,wkhd->whqk', queries, keys_win, precision=PRECISE) * score_scale + biases[None]
            same_part = group_seg[:, :, None] == group_seg[:, None, :]
            usable = (group_valid[:, None, :] > 0) | jnp.eye(window, dtype=jnp.bool_)[None]
            scores = low_back(jnp.where((same_part & usable)[:, None], raw_scores, MASKED_SCORE))
            weights = low(jax.nn.softmax(scores, axis=-1))
            attended = jnp.einsum('whqk,wkhd->wqhd', weights, values_win, precision=PRECISE).reshape(count_win * window, feat_width)
            attended = low(low_back(attended))
            branch = low_back(matmul(attended, weight_proj) + bias_proj)
            middle = group_tokens + modulate(branch, scale_one, shift_one)
            hidden_pre = low_back(matmul(low(middle), weight_up) + bias_up)
            hidden = low(jax.nn.gelu(hidden_pre, approximate=False))
            second = low_back(matmul(hidden, weight_down) + bias_down)
            return middle + modulate(second, scale_two, shift_two)
        result = lax.map(jax.checkpoint(group_block), (grouped(inputs), seg_groups, valid_groups))
        result = from_groups(result, inputs.shape)
        return jnp.roll(result, shifts, axis=(0, 1, 2))
    mixed_out, pullback = jax.vjp(forward, tokens.astype(jnp.float32), w_qkv.astype(jnp.float32), q_bias.astype(jnp.float32), v_bias.astype(jnp.float32), w_proj.astype(jnp.float32), b_proj.astype(jnp.float32), w_up.astype(jnp.float32), b_up.astype(jnp.float32), w_down.astype(jnp.float32), b_down.astype(jnp.float32), w_mod.astype(jnp.float32), b_mod.astype(jnp.float32), rel_table.astype(jnp.float32))
    gradients = pullback(cotangent.astype(jnp.float32))
    return (mixed_out.astype(jnp.bfloat16), gradients[0].astype(jnp.bfloat16), gradients[1], gradients[2], gradients[3], gradients[4], gradients[5], gradients[6], gradients[7], gradients[8], gradients[9], gradients[10], gradients[11], gradients[12])
```

```python
import functools
import math

import jax
import jax.numpy as jnp
from jax import lax
from jax.experimental import pallas as pl
from jax.experimental.pallas import tpu as pltpu
from jax.sharding import PartitionSpec as P

WZ = 2
WY = 12
WX = 6
WINDOW = WZ * WY * WX
HEADS = 4
BLOCK_WINDOWS = 3

NORM_EPSILON = 1e-05
MASKED_SCORE = -1000000000.0
PRECISE = lax.Precision.HIGHEST
F32 = jnp.float32
BF16 = jnp.bfloat16


def passed_along(block, axis, distance):
    devices = range(lax.axis_size(axis))
    route = [((i - distance) % len(devices), i) for i in devices]
    return lax.ppermute(block, axis, route)


def lead_context(lead_hours, feat_width):
    half_width = feat_width // 2
    fraction = jnp.arange(half_width, dtype=jnp.float32) / half_width
    angles = lead_hours.astype(jnp.float32)[0] * jnp.exp(-math.log(1000.0) * fraction)
    return jnp.concatenate([jnp.sin(angles), jnp.cos(angles)])


def one_hot_offsets(span_len):
    places = jnp.arange(span_len)
    offsets = places[:, None] - places[None, :] + span_len - 1
    return (offsets[:, :, None] == jnp.arange(2 * span_len - 1)[None, None, :]).astype(jnp.float32)


def relative_bias(table_bias):
    biases = jnp.einsum(
        "habc,ika,jlb,mnc->nklhmij",
        table_bias,
        one_hot_offsets(WZ),
        one_hot_offsets(WY),
        one_hot_offsets(WX),
        precision=PRECISE,
    )
    return biases.reshape(WINDOW, HEADS * WINDOW)


def to_windows(region):
    level_count, row_count, col_count, feat_width = region.shape
    rolled = jnp.roll(region, -(WZ // 2), axis=0)
    pieces = rolled.reshape(level_count // WZ, WZ, row_count // WY, WY, col_count, feat_width)
    return pieces.transpose(0, 2, 4, 1, 3, 5).reshape(-1, feat_width)


def from_windows(flat, level_count, row_count, col_count):
    feat_width = flat.shape[-1]
    pieces = flat.reshape(level_count // WZ, row_count // WY, col_count, WZ, WY, feat_width)
    region = pieces.transpose(0, 3, 1, 4, 2, 5).reshape(
        level_count, row_count, col_count, feat_width
    )
    return jnp.roll(region, WZ // 2, axis=0)


def extend(tile_field):
    row_count = tile_field.shape[1]
    col_count = tile_field.shape[2]
    arriving = passed_along(tile_field[:, :, col_count - WX // 2 :], "lon", 1)
    widened = jnp.concatenate([arriving, tile_field[:, :, : col_count - WX // 2]], axis=2)
    above_rows = passed_along(widened[:, row_count - WY // 2 :], "lat", 1)
    return jnp.concatenate([above_rows, widened[:, : row_count - WY // 2]], axis=1)


def fold(region):
    returned = passed_along(region[:, : WY // 2], "lat", -1)
    taller = jnp.concatenate([region[:, WY // 2 :], returned], axis=1)
    leftover = passed_along(taller[:, :, : WX // 2], "lon", -1)
    return jnp.concatenate([taller[:, :, WX // 2 :], leftover], axis=2)


def dot_nn(left, right):
    return lax.dot_general(left, right, (((1,), (0,)), ((), ())), preferred_element_type=F32)


def dot_nt(left, right):
    return lax.dot_general(left, right, (((1,), (1,)), ((), ())), preferred_element_type=F32)


def dot_tn(left, right):
    return lax.dot_general(left, right, (((0,), (0,)), ((), ())), preferred_element_type=F32)


def row_mean(values):
    return jnp.mean(values, axis=-1, keepdims=True)


def norm(values):
    center = values - row_mean(values)
    inverse = lax.rsqrt(row_mean(center * center) + NORM_EPSILON)
    return center * inverse, inverse


def norm_back(grad, normed, inverse):
    return inverse * (grad - row_mean(grad) - normed * row_mean(grad * normed))


def gelu_both(values):
    gauss_cdf = 0.5 * (1.0 + lax.erf(values * math.sqrt(0.5)))
    density = jnp.exp(values * values * -0.5) * (1.0 / math.sqrt(2.0 * math.pi))
    return values * gauss_cdf, gauss_cdf + values * density


def by_head(values):
    width = values.shape[-1] // HEADS
    lane_head = lax.broadcasted_iota(jnp.int32, values.shape, 1) // width
    zero = jnp.zeros_like(values)
    return jnp.concatenate([jnp.where(lane_head == h, values, zero) for h in range(HEADS)], axis=0)


def own_head(stacked):
    cells = stacked.shape[0] // HEADS
    width = stacked.shape[-1] // HEADS
    lane_head = lax.broadcasted_iota(jnp.int32, (cells, stacked.shape[-1]), 1) // width
    picked = stacked[:cells]
    for h in range(1, HEADS):
        picked = jnp.where(lane_head == h, stacked[h * cells : (h + 1) * cells], picked)
    return picked


def block_kernel(
    x_ref, g_ref, score_bias_ref, w_qkv_ref, qkv_shift_ref, w_proj_ref, w_up_ref, b_up_ref,
    w_down_ref, vec_ref,
    mixed_ref, token_grad_ref, grad_qkv_ref, grad_qkv_bias_ref, grad_proj_ref, grad_up_ref,
    grad_up_bias_ref, grad_down_ref, vec_grad_ref, score_sum_ref,
    qkv_ref, prob_ref, att_ref, dqkv_ref,
):
    @pl.when(pl.program_id(0) == 0)
    def _():
        for ref in (grad_qkv_ref, grad_qkv_bias_ref, grad_proj_ref, grad_up_ref,
                    grad_up_bias_ref, grad_down_ref, vec_grad_ref, score_sum_ref):
            ref[...] = jnp.zeros_like(ref)

    windows = x_ref.shape[0] // WINDOW
    width = x_ref.shape[1]
    score_scale = (width // HEADS) ** -0.5
    shift_one, scale_one, shift_two, scale_two, b_proj, b_down = [
        vec_ref[i : i + 1, :] for i in range(6)
    ]
    x = x_ref[...]
    qkv_ref[...] = (dot_nn(x, w_qkv_ref[...]) + qkv_shift_ref[...]).astype(BF16)
    for w in range(windows):
        cells = pl.ds(w * WINDOW, WINDOW)
        queries = by_head(qkv_ref[cells, :width] * BF16(score_scale))
        scores = dot_nt(qkv_ref[cells, width : 2 * width], queries) + score_bias_ref[0]
        top = jnp.max(scores, axis=0, keepdims=True)
        exps = jnp.exp(scores - top)
        prob = exps * (1.0 / jnp.sum(exps, axis=0, keepdims=True))
        prob_ref[w] = prob
        att_ref[cells, :] = own_head(
            dot_tn(prob.astype(BF16), qkv_ref[cells, 2 * width :])
        ).astype(BF16)

    att = att_ref[...]
    branch = dot_nn(att, w_proj_ref[...]) + b_proj
    norm_one, inverse_one = norm(branch)
    middle = x.astype(F32) + norm_one * (1.0 + scale_one) + shift_one
    middle_low = middle.astype(BF16)
    pre = dot_nn(middle_low, w_up_ref[...]) + b_up_ref[...]
    hidden, slope = gelu_both(pre)
    hidden = hidden.astype(BF16)
    second = dot_nn(hidden, w_down_ref[...]) + b_down
    norm_two, inverse_two = norm(second)
    mixed_ref[...] = (middle + norm_two * (1.0 + scale_two) + shift_two).astype(BF16)

    g = g_ref[...].astype(F32)
    second_low = norm_back(g * (1.0 + scale_two), norm_two, inverse_two).astype(BF16)
    grad_down_ref[...] += dot_tn(second_low, hidden)
    pre_grad = dot_nt(second_low, w_down_ref[...]) * slope
    pre_low = pre_grad.astype(BF16)
    grad_up_ref[...] += dot_tn(middle_low, pre_low)
    grad_up_bias_ref[...] += jnp.sum(pre_grad, axis=0, keepdims=True)
    middle_grad = g + dot_nt(pre_low, w_up_ref[...])
    branch_low = norm_back(middle_grad * (1.0 + scale_one), norm_one, inverse_one).astype(BF16)
    grad_proj_ref[...] += dot_tn(att, branch_low)
    att_ref[...] = dot_nt(branch_low, w_proj_ref[...]).astype(BF16)
    sums = [
        jnp.sum(v, axis=0, keepdims=True)
        for v in (
            middle_grad, middle_grad * norm_one, g, g * norm_two,
            branch_low.astype(F32), second_low.astype(F32),
        )
    ]
    vec_grad_ref[0:6, :] += jnp.concatenate(sums, axis=0)

    for w in range(windows):
        cells = pl.ds(w * WINDOW, WINDOW)
        queries = by_head(qkv_ref[cells, :width] * BF16(score_scale))
        out_grad = by_head(att_ref[cells, :])
        prob = prob_ref[w]
        prob_grad = dot_nt(qkv_ref[cells, 2 * width :], out_grad)
        score_grad = prob * (prob_grad - jnp.sum(prob_grad * prob, axis=0, keepdims=True))
        score_sum_ref[...] += score_grad
        score_grad = score_grad.astype(BF16)
        dqkv_ref[cells, :width] = (
            own_head(dot_tn(score_grad, qkv_ref[cells, width : 2 * width])) * score_scale
        ).astype(BF16)
        dqkv_ref[cells, width : 2 * width] = dot_nn(score_grad, queries).astype(BF16)
        dqkv_ref[cells, 2 * width :] = dot_nn(prob.astype(BF16), out_grad).astype(BF16)

    dqkv = dqkv_ref[...]
    grad_qkv_ref[...] += dot_tn(x, dqkv)
    grad_qkv_bias_ref[...] += jnp.sum(dqkv.astype(F32), axis=0, keepdims=True)
    token_grad_ref[...] = (middle_grad + dot_nt(dqkv, w_qkv_ref[...])).astype(BF16)


def block_call(x, g, score_bias, w_qkv, qkv_shift, w_proj, w_up, b_up, w_down, vecs):
    cell_count, width = x.shape
    hidden_width = w_up.shape[1]
    rows = BLOCK_WINDOWS * WINDOW
    steps = cell_count // rows
    per_group = steps // score_bias.shape[0]

    def whole(shape):
        return pl.BlockSpec(shape, lambda i: (0,) * len(shape))

    tile = pl.BlockSpec((rows, width), lambda i: (i, 0))
    outs = [
        (grad_shape, whole(grad_shape))
        for grad_shape in (
            (width, 3 * width), (1, 3 * width), (width, width), (width, hidden_width),
            (1, hidden_width), (width, hidden_width), (8, width), (WINDOW, HEADS * WINDOW),
        )
    ]
    return pl.pallas_call(
        block_kernel,
        grid=(steps,),
        in_specs=[
            tile, tile,
            pl.BlockSpec((1, WINDOW, HEADS * WINDOW), lambda i: (i // per_group, 0, 0)),
        ] + [whole(w.shape) for w in (w_qkv, qkv_shift, w_proj, w_up, b_up, w_down, vecs)],
        out_specs=[tile, tile] + [spec for _, spec in outs],
        out_shape=[jax.ShapeDtypeStruct(x.shape, BF16)] * 2
        + [jax.ShapeDtypeStruct(s, F32) for s, _ in outs],
        scratch_shapes=[
            pltpu.VMEM((rows, 3 * width), BF16),
            pltpu.VMEM((BLOCK_WINDOWS, WINDOW, HEADS * WINDOW), F32),
            pltpu.VMEM((rows, width), BF16),
            pltpu.VMEM((rows, 3 * width), BF16),
        ],
        compiler_params=pltpu.CompilerParams(vmem_limit_bytes=60 * 2**20),
    )(x, g, score_bias, w_qkv, qkv_shift, w_proj, w_up, b_up, w_down, vecs)


def on_device(
    tokens, cotangent, w_qkv, q_bias, v_bias, w_proj, b_proj, w_up, b_up, w_down, b_down,
    w_mod, b_mod, rel_table, crop_rows, lead_hours,
):
    level_count, row_count, col_count, feat_width = tokens.shape
    band_count = lax.axis_size("lat")
    context = jax.nn.silu(lead_context(lead_hours, feat_width))
    modulation = jnp.dot(
        context[None, :], w_mod.astype(F32), precision=PRECISE, preferred_element_type=F32
    )[0] + b_mod.astype(F32)
    vecs = jnp.concatenate(
        [
            modulation.reshape(4, feat_width),
            b_proj.astype(F32)[None],
            b_down.astype(F32)[None],
            jnp.zeros((2, feat_width), F32),
        ]
    )
    biases, bias_pull = jax.vjp(relative_bias, rel_table.astype(F32))

    first_row = lax.axis_index("lat") * row_count - WY // 2
    global_rows = jnp.mod(
        first_row + jnp.arange(row_count, dtype=jnp.int32), band_count * row_count
    )
    band_ids = global_rows // row_count
    crop_here = jnp.sum(
        jnp.where(
            band_ids[:, None] == jnp.arange(band_count, dtype=jnp.int32)[None, :],
            crop_rows[None, :],
            0,
        ),
        axis=1,
    )
    valid_rows = (global_rows % row_count >= row_count - crop_here).reshape(-1, WY)
    row_part = (global_rows < WY // 2).reshape(-1, WY)
    level_part = jnp.roll(jnp.arange(level_count) == 0, -(WZ // 2)).reshape(-1, WZ)
    group_shape = (level_part.shape[0], row_part.shape[0], WX, WZ, WY)
    part = 2 * level_part[:, None, None, :, None] + row_part[None, :, None, None, :]
    part = jnp.broadcast_to(part, group_shape).reshape(-1, WINDOW)
    valid = jnp.broadcast_to(valid_rows[None, :, None, None, :], group_shape).reshape(-1, WINDOW)
    allowed = (part[:, :, None] == part[:, None, :]) & (
        valid[:, :, None] | jnp.eye(WINDOW, dtype=jnp.bool_)[None]
    )
    masks = jnp.where(allowed, 0.0, MASKED_SCORE).astype(F32)
    score_bias = biases[None] + jnp.tile(masks, (1, 1, HEADS))

    qkv_shift = jnp.concatenate([q_bias, jnp.zeros_like(q_bias), v_bias]).astype(F32)[None]
    (
        mixed, token_grad, grad_qkv, grad_qkv_bias, grad_proj, grad_up, grad_up_bias, grad_down,
        vec_grad, score_sum,
    ) = block_call(
        to_windows(extend(tokens)), to_windows(extend(cotangent)), score_bias, w_qkv, qkv_shift,
        w_proj, w_up, b_up.astype(F32)[None], w_down, vecs,
    )
    mixed = fold(from_windows(mixed, level_count, row_count, col_count))
    token_grad = fold(from_windows(token_grad, level_count, row_count, col_count))
    grad_table = bias_pull(score_sum)[0]
    grad_qkv, grad_qkv_bias, grad_proj, grad_up, grad_up_bias, grad_down, vec_grad, grad_table = (
        lax.psum(
            (grad_qkv, grad_qkv_bias, grad_proj, grad_up, grad_up_bias, grad_down, vec_grad,
             grad_table),
            ("lat", "lon"),
        )
    )
    grad_mod_bias = vec_grad[:4].reshape(-1)
    grad_mod = context[:, None] * grad_mod_bias[None, :]
    return (
        mixed,
        token_grad,
        grad_qkv,
        grad_qkv_bias[0, :feat_width],
        grad_qkv_bias[0, 2 * feat_width :],
        grad_proj,
        vec_grad[4],
        grad_up,
        grad_up_bias[0],
        grad_down.T,
        vec_grad[5],
        grad_mod,
        grad_mod_bias,
        grad_table,
    )


def solution(mesh):
    split = P(None, "lat", "lon", None)
    return jax.shard_map(
        on_device,
        mesh=mesh,
        in_specs=(split, split) + (P(),) * 14,
        out_specs=(split, split) + (P(),) * 12,
        check_vma=False,
    )
```

```python
import functools
import math

import jax
import jax.numpy as jnp
from jax import lax
from jax.experimental import pallas as pl
from jax.experimental.pallas import tpu as pltpu
from jax.sharding import PartitionSpec as P

WZ = 2
WY = 12
WX = 6
CELLS = WZ * WY
WINDOW = CELLS * WX
HEADS = 4
SCORES = HEADS * WINDOW
HALF_Y = WY // 2
HALF_X = WX // 2
BLOCK_WINDOWS = 5
OFFSETS = (2 * WZ - 1) * (2 * WX - 1)
VECTORS = 16
TABLE_ROWS = 2 * WY
EDGE = HALF_X * CELLS
PACKED_COLS = 8

NORM_EPSILON = 1e-05
MASKED_SCORE = -1000000000.0
F32 = jnp.float32
BF16 = jnp.bfloat16
MESH = pl.DeviceIdType.MESH
ANY = pl.BlockSpec(memory_space=pl.ANY)
VMEM_LIMIT = 60 * 2**20


def dot_nn(left, right):
    return lax.dot_general(left, right, (((1,), (0,)), ((), ())), preferred_element_type=F32)


def dot_nt(left, right):
    return lax.dot_general(left, right, (((1,), (1,)), ((), ())), preferred_element_type=F32)


def dot_tn(left, right):
    return lax.dot_general(left, right, (((0,), (0,)), ((), ())), preferred_element_type=F32)


def iota(shape, axis):
    return lax.broadcasted_iota(jnp.int32, shape, axis)


def whole(shape, buffers=1):
    return pl.BlockSpec(
        shape, lambda *_: (0,) * len(shape), pipeline_mode=pl.Buffered(buffers)
    )


def shape_of(shape, dtype):
    return jax.ShapeDtypeStruct(shape, dtype)


def strips_kernel(tokens_ref, cotangent_ref, rows_ref, cols_ref):
    _, col_count, row_count, width = tokens_ref.shape
    for a, ref in enumerate((tokens_ref, cotangent_ref)):
        cols_ref[a, 0] = ref[0, col_count - HALF_X :].reshape(HALF_X * row_count, width)
        for start in range(0, col_count, PACKED_COLS):
            count = min(PACKED_COLS, col_count - start)
            block = ref[0, start : start + count].astype(F32)
            packed = jnp.concatenate(
                [block[c, row_count - HALF_Y :] for c in range(count)], axis=0
            )
            rows_ref[a, 0, start * HALF_Y : (start + count) * HALF_Y, :] = packed.astype(BF16)


def packed_rows(col_count):
    return -(-col_count * HALF_Y // 16) * 16


def cut_strips(tokens, cotangent):
    level_count, col_count, row_count, width = tokens.shape
    field = pl.BlockSpec((1, col_count, row_count, width), lambda i: (i, 0, 0, 0))

    def strip(count):
        return pl.BlockSpec((2, 1, count, width), lambda i: (0, i, 0, 0))

    counts = (packed_rows(col_count), HALF_X * row_count)
    return pl.pallas_call(
        strips_kernel,
        grid=(level_count,),
        in_specs=[field, field],
        out_specs=[strip(count) for count in counts],
        out_shape=[shape_of((2, level_count, count, width), BF16) for count in counts],
        compiler_params=pltpu.CompilerParams(vmem_limit_bytes=VMEM_LIMIT),
    )(tokens, cotangent)


def offset_pick(key_x, key_z):
    lane = iota((HEADS * OFFSETS, SCORES), 1)
    head, rest = lane // WINDOW, lane % WINDOW
    query_x, query_z = rest // CELLS, (rest % CELLS) // WY
    offset_z, offset_x = query_z - key_z + WZ - 1, query_x - key_x + WX - 1
    place = (offset_z * (2 * WX - 1) + offset_x) * HEADS + head
    return iota((HEADS * OFFSETS, SCORES), 0) == place


def setup_kernel(
    lead_ref, w_mod_ref, b_mod_ref, b_proj_ref, b_down_ref, q_bias_ref, v_bias_ref, b_up_ref,
    table_ref, bias_ref, vec_ref, context_ref,
):
    width = w_mod_ref.shape[0]
    half = width // 2
    lanes = context_ref.shape[1]
    fraction = iota((half, lanes), 0).astype(F32) / half
    angles = lead_ref[0].astype(F32) * jnp.exp(-math.log(1000.0) * fraction)
    waves = jnp.concatenate([jnp.sin(angles), jnp.cos(angles)], axis=0)
    context = waves * (1.0 / (1.0 + jnp.exp(-waves)))
    context_ref[...] = context
    for part in range(4):
        pieces = []
        for j in range(width // lanes):
            start = part * width + j * lanes
            pieces.append(
                jnp.sum(context * w_mod_ref[:, start : start + lanes].astype(F32), axis=0, keepdims=True)
            )
        vec_ref[part : part + 1, :] = jnp.concatenate(pieces, axis=1) + b_mod_ref[
            :, part * width : (part + 1) * width
        ].astype(F32)
    rows = [b_proj_ref[...], b_down_ref[...], q_bias_ref[...], jnp.zeros((1, width), BF16), v_bias_ref[...]]
    rows += [b_up_ref[:, j * width : (j + 1) * width] for j in range(4)]
    rows += [jnp.zeros((1, width), BF16)] * (VECTORS - 4 - len(rows))
    for i, row in enumerate(rows):
        vec_ref[4 + i : 5 + i, :] = row.astype(F32)

    offsets_y = 2 * WY - 1
    backwards = iota((TABLE_ROWS, offsets_y), 0) + iota((TABLE_ROWS, offsets_y), 1) == offsets_y - 1
    table = dot_nt(backwards.astype(BF16), table_ref[...]).astype(BF16)
    query_y = iota((WY, SCORES), 1) % WY
    for key_x in range(WX):
        for key_z in range(WZ):
            spread = dot_nn(table, offset_pick(key_x, key_z).astype(BF16))
            rows = spread[WY - 1 : 2 * WY - 1]
            for y in range(1, WY):
                rows = jnp.where(query_y == y, spread[WY - 1 - y : 2 * WY - 1 - y], rows)
            start = key_x * CELLS + key_z * WY
            bias_ref[start : start + WY, :] = rows


def set_up(lead_hours, w_mod, b_mod, b_proj, b_down, q_bias, v_bias, b_up, table):
    width = w_mod.shape[0]
    vmem = pl.BlockSpec(memory_space=pltpu.VMEM)
    vectors = [v[None] for v in (b_mod, b_proj, b_down, q_bias, v_bias, b_up)]
    return pl.pallas_call(
        setup_kernel,
        in_specs=[pl.BlockSpec(memory_space=pltpu.SMEM)] + [vmem] * 8,
        out_specs=[vmem] * 3,
        out_shape=[
            shape_of((WINDOW, SCORES), F32),
            shape_of((VECTORS, width), F32),
            shape_of((width, 128), F32),
        ],
        compiler_params=pltpu.CompilerParams(vmem_limit_bytes=VMEM_LIMIT),
    )(lead_hours, w_mod, *vectors, table)


def table_grad(score_sum_ref):
    query_y = iota((WY, SCORES), 1) % WY
    total = jnp.zeros((TABLE_ROWS, HEADS * OFFSETS), F32)
    for key_x in range(WX):
        for key_z in range(WZ):
            start = key_x * CELLS + key_z * WY
            rows = score_sum_ref[start : start + WY, :]
            spread = jnp.zeros((TABLE_ROWS, SCORES), F32)
            for y in range(WY):
                own = jnp.where(query_y == y, rows, 0.0)
                pads = (WY - 1 - y, TABLE_ROWS - (2 * WY - 1 - y))
                parts = [jnp.zeros((p, SCORES), F32) for p in pads]
                spread = spread + jnp.concatenate(
                    ([parts[0]] if pads[0] else []) + [own, parts[1]], axis=0
                )
            pick = offset_pick(key_x, key_z).astype(BF16)
            high = spread.astype(BF16)
            low = (spread - high.astype(F32)).astype(BF16)
            total = total + dot_nt(high, pick) + dot_nt(low, pick)
    return total


def row_mean(values):
    return jnp.mean(values, axis=-1, keepdims=True)


def norm(values):
    center = values - row_mean(values)
    inverse = lax.rsqrt(row_mean(center * center) + NORM_EPSILON)
    return center * inverse, inverse


def norm_back(grad, normed, inverse):
    return inverse * (grad - row_mean(grad) - normed * row_mean(grad * normed))


def gelu_both(values):
    gauss_cdf = 0.5 * (1.0 + lax.erf(values * math.sqrt(0.5)))
    density = jnp.exp(values * values * -0.5) * (1.0 / math.sqrt(2.0 * math.pi))
    return values * gauss_cdf, gauss_cdf + values * density


def by_head(values):
    width = values.shape[-1] // HEADS
    lane_head = iota(values.shape, 1) // width
    zero = jnp.zeros_like(values)
    return jnp.concatenate([jnp.where(lane_head == h, values, zero) for h in range(HEADS)], axis=0)


def own_head(stacked):
    cells = stacked.shape[0] // HEADS
    width = stacked.shape[-1] // HEADS
    lane_head = iota((cells, stacked.shape[-1]), 1) // width
    picked = stacked[:cells]
    for h in range(1, HEADS):
        picked = jnp.where(lane_head == h, stacked[h * cells : (h + 1) * cells], picked)
    return picked


def store_windows(field, z_pieces, out_ref):
    width = out_ref.shape[1]
    for c in range(HALF_X):
        out_ref[c * CELLS : (c + 1) * CELLS, :] = jnp.concatenate(
            [z_pieces(c, z) for z in range(WZ)], axis=0
        )
    own_cols = out_ref.shape[0] // CELLS - HALF_X
    for start in range(0, own_cols, PACKED_COLS):
        count = min(PACKED_COLS, own_cols - start)
        both = jnp.concatenate([field(start, count, z) for z in range(WZ)], axis=1)
        first = (start + HALF_X) * CELLS
        out_ref[first : first + count * CELLS, :] = both.reshape(count * CELLS, width)


def unpack_strip(rows, count):
    return jnp.stack([rows[c * HALF_Y : (c + 1) * HALF_Y] for c in range(count)], axis=0)


def mask_scores(bias, level_wraps, straddles, first_band, crop_own, crop_before, row_count):
    def parts(cell):
        z, y = (cell % CELLS) // WY, cell % WY
        part = 2 * jnp.where(z == WZ - 1, level_wraps, 0)
        if straddles:
            part = part + jnp.where(y >= HALF_Y, first_band, 0)
            own = y - HALF_Y >= row_count - crop_own
            before = row_count - HALF_Y + y >= row_count - crop_before
            valid = jnp.where(y >= HALF_Y, own.astype(jnp.int32), before.astype(jnp.int32))
        else:
            valid = (HALF_Y + y >= row_count - crop_own).astype(jnp.int32)
        return part, valid

    key = iota(bias.shape, 0)
    query = iota(bias.shape, 1) % WINDOW
    key_part, key_valid = parts(key)
    query_part, _ = parts(query)
    allowed = (key_part == query_part) & ((key_valid > 0) | (key == query))
    return jnp.where(allowed, bias, bias + MASKED_SCORE)


def block_kernel(straddles, first_pair, last, *refs):
    refs = list(refs)

    def take(count):
        taken, refs[:count] = refs[:count], []
        return taken

    (crop_ref,) = take(1)
    field_refs = [take(WZ), take(WZ)]
    col_refs = [take(WZ), take(WZ)]
    row_refs, corner_refs = ([take(WZ), take(WZ)], [take(WZ), take(WZ)]) if straddles else (None, None)
    bias_ref, vec_ref, w_qkv_ref, w_proj_ref, w_up_ref, w_down_ref = take(6)
    grad_in_ref, small_in_ref, scores_in_ref = take(3)
    out_ref, edge_ref, grad_ref, small_ref = take(4)
    (score_sum_ref,) = take(0 if last else 1) or (None,)
    (back_ref,) = take(1 if straddles else 0) or (None,)
    score_bias_ref, xw_ref, gw_ref, qkv_ref, prob_ref, att_ref, dqkv_ref = take(7)
    if last:
        (score_sum_ref,) = take(1)

    step = pl.program_id(0)
    width = vec_ref.shape[1]
    hidden_width = w_up_ref.shape[1]
    _, col_count, row_count, _ = field_refs[0][0].shape
    band_count = crop_ref.shape[0]
    score_scale = (width // HEADS) ** -0.5

    @pl.when(step == 0)
    def _():
        grad_ref[...] = grad_in_ref[...]
        small_ref[...] = small_in_ref[...]
        score_sum_ref[...] = scores_in_ref[...]

    band = lax.axis_index("lat")
    score_bias_ref[...] = mask_scores(
        bias_ref[...], (step + first_pair == 1).astype(jnp.int32), straddles,
        (band == 0).astype(jnp.int32), crop_ref[band],
        crop_ref[lax.rem(band + band_count - 1, band_count)], row_count,
    )

    for a, target in enumerate((xw_ref, gw_ref)):
        def field(start, count, z, a=a):
            rows = field_refs[a][z][0, start : start + count].astype(F32)
            if not straddles:
                return rows[:, HALF_Y : HALF_Y + WY]
            strip = row_refs[a][z][0, 0, start * HALF_Y : (start + count) * HALF_Y, :].astype(F32)
            return jnp.concatenate([unpack_strip(strip, count), rows[:, :HALF_Y]], axis=1)

        def western(c, z, a=a):
            own = slice(c * row_count, (c + 1) * row_count)
            rows = col_refs[a][z][0, 0, own, :].astype(F32)
            if not straddles:
                return rows[HALF_Y : HALF_Y + WY]
            before = corner_refs[a][z][0, 0, own, :].astype(F32)
            return jnp.concatenate([before[row_count - HALF_Y :], rows[:HALF_Y]], axis=0)

        store_windows(field, western, target)

    rows = BLOCK_WINDOWS * WINDOW
    shift_one, scale_one, shift_two, scale_two, b_proj, b_down = [
        vec_ref[i : i + 1, :] for i in range(6)
    ]
    qkv_shift = jnp.concatenate([vec_ref[i : i + 1, :] for i in range(6, 9)], axis=1)
    b_up = jnp.concatenate([vec_ref[i : i + 1, :] for i in range(9, 13)], axis=1)

    def add_grad(first, value):
        for j in range(value.shape[1] // width):
            grad_ref[(first + j) * width : (first + j + 1) * width, :] += value[
                :, j * width : (j + 1) * width
            ]

    def block(index, carry):
        here = pl.ds(pl.multiple_of(index * rows, 16), rows)
        x32 = xw_ref[here, :]
        x = x32.astype(BF16)
        qkv_ref[...] = (dot_nn(x, w_qkv_ref[...]) + qkv_shift).astype(BF16)
        for w in range(BLOCK_WINDOWS):
            cells = pl.ds(w * WINDOW, WINDOW)
            queries = by_head(qkv_ref[cells, :width] * BF16(score_scale))
            scores = dot_nt(qkv_ref[cells, width : 2 * width], queries) + score_bias_ref[...]
            top = jnp.max(scores, axis=0, keepdims=True)
            exps = jnp.exp(scores - top)
            prob = exps * (1.0 / jnp.sum(exps, axis=0, keepdims=True))
            prob_ref[w] = prob
            att_ref[cells, :] = own_head(
                dot_tn(prob.astype(BF16), qkv_ref[cells, 2 * width :])
            ).astype(BF16)

        att = att_ref[...]
        branch = dot_nn(att, w_proj_ref[...]) + b_proj
        norm_one, inverse_one = norm(branch)
        middle = x32 + norm_one * (1.0 + scale_one) + shift_one
        middle_low = middle.astype(BF16)
        pre = dot_nn(middle_low, w_up_ref[...]) + b_up
        hidden, slope = gelu_both(pre)
        hidden = hidden.astype(BF16)
        second = dot_nn(hidden, w_down_ref[...]) + b_down
        norm_two, inverse_two = norm(second)
        out_ref[0, 0, here, :] = (middle + norm_two * (1.0 + scale_two) + shift_two).astype(BF16)

        g = gw_ref[here, :]
        second_low = norm_back(g * (1.0 + scale_two), norm_two, inverse_two).astype(BF16)
        add_grad(8, dot_tn(second_low, hidden))
        pre_grad = dot_nt(second_low, w_down_ref[...]) * slope
        pre_low = pre_grad.astype(BF16)
        add_grad(4, dot_tn(middle_low, pre_low))
        middle_grad = g + dot_nt(pre_low, w_up_ref[...])
        branch_low = norm_back(middle_grad * (1.0 + scale_one), norm_one, inverse_one).astype(BF16)
        add_grad(3, dot_tn(att, branch_low))
        att_ref[...] = dot_nt(branch_low, w_proj_ref[...]).astype(BF16)

        for w in range(BLOCK_WINDOWS):
            cells = pl.ds(w * WINDOW, WINDOW)
            queries = by_head(qkv_ref[cells, :width] * BF16(score_scale))
            out_grad = by_head(att_ref[cells, :])
            prob = prob_ref[w]
            prob_grad = dot_nt(qkv_ref[cells, 2 * width :], out_grad)
            score_grad = prob * (prob_grad - jnp.sum(prob_grad * prob, axis=0, keepdims=True))
            score_sum_ref[...] += score_grad
            score_grad = score_grad.astype(BF16)
            dqkv_ref[cells, :width] = (
                own_head(dot_tn(score_grad, qkv_ref[cells, width : 2 * width])) * score_scale
            ).astype(BF16)
            dqkv_ref[cells, width : 2 * width] = dot_nn(score_grad, queries).astype(BF16)
            dqkv_ref[cells, 2 * width :] = dot_nn(prob.astype(BF16), out_grad).astype(BF16)

        dqkv = dqkv_ref[...]
        add_grad(0, dot_tn(x, dqkv))
        out_ref[1, 0, here, :] = (middle_grad + dot_nt(dqkv, w_qkv_ref[...])).astype(BF16)

        def column_sums(values):
            return jnp.sum(values, axis=0, keepdims=True)

        qkv_sums = column_sums(dqkv.astype(F32))
        up_sums = column_sums(pre_grad)
        sums = [
            column_sums(middle_grad), column_sums(middle_grad * norm_one), column_sums(g),
            column_sums(g * norm_two), column_sums(branch_low.astype(F32)),
            column_sums(second_low.astype(F32)),
        ]
        sums += [qkv_sums[:, j * width : (j + 1) * width] for j in range(3)]
        sums += [up_sums[:, j * width : (j + 1) * width] for j in range(hidden_width // width)]
        sums += [jnp.zeros((VECTORS - len(sums), width), F32)]
        small_ref[:VECTORS, :] += jnp.concatenate(sums, axis=0)
        return carry

    lax.fori_loop(0, col_count // WX // BLOCK_WINDOWS, block, 0)
    for a in range(2):
        edge_ref[a, 0] = out_ref[a, 0, :EDGE, :]
        if straddles:
            for start in range(0, col_count - HALF_X, PACKED_COLS):
                count = min(PACKED_COLS, col_count - HALF_X - start)
                first = (start + HALF_X) * CELLS
                cells = out_ref[a, 0, first : first + count * CELLS, :].astype(F32)
                for z in range(WZ):
                    pieces = [
                        cells[c * CELLS + z * WY : c * CELLS + z * WY + HALF_Y] for c in range(count)
                    ]
                    back_ref[a, z, start * HALF_Y : (start + count) * HALF_Y, :] = jnp.concatenate(
                        pieces, axis=0
                    ).astype(BF16)
    if last:
        @pl.when(step == pl.num_programs(0) - 1)
        def _():
            small_ref[VECTORS:, : HEADS * OFFSETS] = table_grad(score_sum_ref)


def block_call(straddles, first_pair, pair_count, last, crop_rows, fields, halos, constants, sums):
    level_count, col_count, row_count, width = fields[0].shape

    def level_of(i, z):
        return (WZ * (i + first_pair) + z + WZ // 2) % level_count

    specs, values = [pl.BlockSpec(memory_space=pltpu.SMEM)], [crop_rows]
    for field in fields:
        for z in range(WZ):
            specs.append(pl.BlockSpec(
                (1, col_count, row_count, width), lambda i, z=z: (level_of(i, z), 0, 0, 0)
            ))
            values.append(field)
    for halo in halos:
        for a in range(2):
            for z in range(WZ):
                specs.append(pl.BlockSpec(
                    (1, 1) + halo.shape[2:], lambda i, a=a, z=z: (a, level_of(i, z), 0, 0)
                ))
                values.append(halo)
    specs += [whole(v.shape) for v in constants + sums]
    values += constants + sums

    cells = col_count * CELLS
    kept = sums[:2] if last else sums
    out_specs = [
        pl.BlockSpec((2, 1, count, width), lambda i: (0, i, 0, 0)) for count in (cells, EDGE)
    ] + [whole(v.shape) for v in kept]
    out_shape = [shape_of((2, pair_count, count, width), BF16) for count in (cells, EDGE)]
    out_shape += [shape_of(v.shape, F32) for v in kept]
    if straddles:
        packed = packed_rows(col_count)
        out_specs.append(pl.BlockSpec((2, WZ, packed, width), lambda i: (0, i, 0, 0)))
        out_shape.append(shape_of((2, pair_count * WZ, packed, width), BF16))
    rows = BLOCK_WINDOWS * WINDOW
    scratch = [
        pltpu.VMEM((WINDOW, SCORES), F32),
        pltpu.VMEM((cells, width), F32),
        pltpu.VMEM((cells, width), F32),
        pltpu.VMEM((rows, 3 * width), BF16),
        pltpu.VMEM((BLOCK_WINDOWS, WINDOW, SCORES), F32),
        pltpu.VMEM((rows, width), BF16),
        pltpu.VMEM((rows, 3 * width), BF16),
    ]
    if last:
        scratch.append(pltpu.VMEM((WINDOW, SCORES), F32))
    return pl.pallas_call(
        functools.partial(block_kernel, straddles, first_pair, last),
        grid=(pair_count,),
        in_specs=specs,
        out_specs=out_specs,
        out_shape=out_shape,
        scratch_shapes=scratch,
        cost_estimate=pl.CostEstimate(
            flops=pair_count * cells * 5_200_000, bytes_accessed=16 * 2**20, transcendentals=0
        ),
        compiler_params=pltpu.CompilerParams(vmem_limit_bytes=VMEM_LIMIT),
    )(*values)


def halved(rows, count):
    sizes = [rows >> (i + 1) for i in range(count)]
    return sizes, [sum(sizes[:i]) for i in range(count + 1)]


def sum_kernel(
    bits, halvings, parts, grad_ref, small_ref, out_ref, small_out_ref,
    acc_ref, send_ref, recv_ref, more_ref, small_recv_ref, sems, small_sems,
):
    axes = ("lat", "lon")
    places = {axis: lax.axis_index(axis) for axis in axes}
    own_bit, partner = {}, {}
    for axis, bit in bits:
        value = (places[axis] // 2**bit) % 2
        own_bit[axis, bit] = value
        moved = dict(places)
        moved[axis] = places[axis] + 2**bit * (1 - 2 * value)
        partner[axis, bit] = tuple(moved[name] for name in axes)

    barrier = pltpu.get_barrier_semaphore()
    for bit in bits:
        pl.semaphore_signal(barrier, inc=1, device_id=partner[bit], device_id_type=MESH)
    pl.semaphore_wait(barrier, len(bits))

    def send(source, target, pair, bit):
        copy = pltpu.make_async_remote_copy(
            src_ref=source, dst_ref=target, send_sem=pair.at[0], recv_sem=pair.at[1],
            device_id=partner[bit], device_id_type=MESH,
        )
        copy.start()
        return copy

    part_rows = grad_ref.shape[0] // parts
    sizes, starts = halved(part_rows, halvings)
    shard = sizes[-1]
    orders = []
    for p in range(parts):
        order = list(bits[:halvings])
        if p == 1 and halvings > 2:
            order[1], order[2] = order[2], order[1]
        orders.append(order)
    low = [p * part_rows for p in range(parts)]
    small_out_ref[...] = small_ref[...]
    acc_ref[...] = grad_ref[...]

    def halve(p, s):
        bit, size = orders[p][s], sizes[s]
        place = pl.ds(p * starts[-1] + starts[s], size)
        away = pl.multiple_of(low[p] + (1 - own_bit[bit]) * size, 16)
        send_ref[place, :] = acc_ref[pl.ds(away, size), :].astype(BF16)
        low[p] = low[p] + own_bit[bit] * size
        return send(send_ref.at[place], recv_ref.at[place], sems.at[p, s], bit)

    def add_half(p, s, copy):
        size = sizes[s]
        copy.wait()
        place = pl.ds(p * starts[-1] + starts[s], size)
        here = pl.ds(pl.multiple_of(low[p], 16), size)
        acc_ref[here, :] += recv_ref[place, :].astype(F32)

    copies = [halve(p, 0) for p in range(parts)]
    for s, bit in enumerate(bits):
        small_copy = send(small_out_ref, small_recv_ref.at[s], small_sems.at[s], bit)
        if s < halvings:
            for p in range(parts):
                add_half(p, s, copies[p])
                if s + 1 < halvings:
                    copies[p] = halve(p, s + 1)
        small_copy.wait()
        small_out_ref[...] += small_recv_ref[s]

    for p in range(parts):
        here = pl.ds(pl.multiple_of(low[p], 16), shard)
        out_ref[here, :] = acc_ref[here, :].astype(BF16)
        for s in range(halvings, len(bits)):
            mine = more_ref.at[0, p, s - halvings]
            theirs = more_ref.at[1, p, s - halvings]
            mine[...] = out_ref[here, :]
            send(mine, theirs, sems.at[p, s], bits[s]).wait()
            out_ref[here, :] = (mine[...].astype(F32) + theirs[...].astype(F32)).astype(BF16)

    def give(p, s):
        here = out_ref.at[pl.ds(pl.multiple_of(low[p], 16), sizes[s]), :]
        low[p] = low[p] - own_bit[orders[p][s]] * sizes[s]
        return send(here, here, sems.at[p, len(bits) + s], orders[p][s])

    copies = [give(p, halvings - 1) for p in range(parts)]
    for s in reversed(range(halvings)):
        for p in range(parts):
            copies[p].wait()
            if s:
                copies[p] = give(p, s - 1)


def sum_over_devices(grad, small):
    bits = [("lon", 0), ("lon", 1), ("lat", 0), ("lat", 1), ("lat", 2)]
    bits = [b for b in bits if 2 ** b[1] < lax.axis_size(b[0])]
    bits += [("lat", b) for b in range(3, lax.axis_size("lat").bit_length() - 1)]
    bits += [("lon", b) for b in range(2, lax.axis_size("lon").bit_length() - 1)]
    if not bits:
        return grad.astype(BF16), small
    halvings, parts = min(5, len(bits)), 2
    rows, width = grad.shape
    sizes, starts = halved(rows // parts, halvings)
    more = max(1, len(bits) - halvings)
    vmem = pl.BlockSpec(memory_space=pltpu.VMEM)
    return pl.pallas_call(
        functools.partial(sum_kernel, tuple(bits), halvings, parts),
        in_specs=[vmem, vmem],
        out_specs=[vmem, vmem],
        out_shape=[shape_of(grad.shape, BF16), shape_of(small.shape, F32)],
        scratch_shapes=[
            pltpu.VMEM(grad.shape, F32),
            pltpu.VMEM((parts * starts[-1], width), BF16),
            pltpu.VMEM((parts * starts[-1], width), BF16),
            pltpu.VMEM((2, parts, more, sizes[-1], width), BF16),
            pltpu.VMEM((len(bits),) + small.shape, F32),
            pltpu.SemaphoreType.DMA((parts, len(bits) + halvings, 2)),
            pltpu.SemaphoreType.DMA((len(bits), 2)),
        ],
        compiler_params=pltpu.CompilerParams(
            collective_id=0, has_side_effects=True, vmem_limit_bytes=VMEM_LIMIT
        ),
    )(grad, small)


def merge_kernel(
    first_ref, second_ref, straddle_ref, rows_ref, first_edge_ref, second_edge_ref,
    straddle_edge_ref, corner_ref, grad_ref, small_ref, context_ref, *out_refs,
):
    fields, grads = out_refs[:2], out_refs[2:]
    _, col_count, row_count, width = fields[0].shape
    step = pl.program_id(0)

    def piece(ref, a, first_col, count, first, size):
        block = ref[a, 0, first_col * CELLS : (first_col + count) * CELLS, :].astype(F32)
        return block.reshape(count, CELLS, width)[:, first : first + size]

    for pair, z in ((0, 0), (0, 1), (1, 0), (1, 1)):
        inner_ref = (first_ref, second_ref)[pair]
        inner_edge_ref = (first_edge_ref, second_edge_ref)[pair]

        @pl.when(step == pair * WZ + z)
        def _():
            first = z * WY
            for a, field in enumerate(fields):
                for start in range(0, col_count - HALF_X, PACKED_COLS):
                    count = min(PACKED_COLS, col_count - HALF_X - start)
                    strip = rows_ref[a, 0, start * HALF_Y : (start + count) * HALF_Y, :]
                    block = jnp.concatenate([
                        piece(straddle_ref, a, start + HALF_X, count, first + HALF_Y, HALF_Y),
                        piece(inner_ref, a, start + HALF_X, count, first, WY),
                        unpack_strip(strip.astype(F32), count),
                    ], axis=1)
                    field[0, start : start + count] = block.astype(BF16)
                block = jnp.concatenate([
                    piece(straddle_edge_ref, a, 0, HALF_X, first + HALF_Y, HALF_Y),
                    piece(inner_edge_ref, a, 0, HALF_X, first, WY),
                    piece(corner_ref, a, 0, HALF_X, first, HALF_Y),
                ], axis=1)
                field[0, col_count - HALF_X :] = block.astype(BF16)

    grad_qkv, grad_proj, grad_up, grad_down, grad_mod, *vectors = grads

    def slab(index):
        return grad_ref[index * width : (index + 1) * width, :].astype(F32)

    @pl.when(step == 0)
    def _():
        for j in range(3):
            grad_qkv[:, j * width : (j + 1) * width] = slab(j)
        grad_proj[...] = slab(3)

    @pl.when(step == 1)
    def _():
        for j in range(grad_up.shape[1] // width):
            grad_up[:, j * width : (j + 1) * width] = slab(4 + j)

    @pl.when(step == 2)
    def _():
        for j in range(grad_down.shape[0] // width):
            grad_down[j * width : (j + 1) * width, :] = slab(8 + j).T

    @pl.when(step == 3)
    def _():
        lanes = context_ref.shape[1]
        for part in range(4):
            row = small_ref[part : part + 1, :]
            for j in range(0, width, lanes):
                grad_mod[:, part * width + j : part * width + j + lanes] = (
                    context_ref[...] * row[:, j : j + lanes]
                )
        mod_bias, proj_bias, down_bias, q_bias, v_bias, up_bias = vectors
        mod_bias[...] = jnp.concatenate([small_ref[i : i + 1, :] for i in range(4)], axis=1)
        up_bias[...] = jnp.concatenate([small_ref[i : i + 1, :] for i in range(9, 13)], axis=1)
        for ref, i in ((proj_bias, 4), (down_bias, 5), (q_bias, 6), (v_bias, 8)):
            ref[...] = small_ref[i : i + 1, :]


def merge(
    field_shape, hidden_width, first, second, straddle, rows, first_edge, second_edge,
    straddle_edge, corner, grad, small, context,
):
    level_count, col_count, row_count, width = field_shape

    def level_of(i):
        return (i + WZ // 2) % level_count

    def by_pair(value):
        return pl.BlockSpec((2, 1) + value.shape[2:], lambda i: (0, i // WZ, 0, 0))

    shapes = [
        (width, 3 * width), (width, width), (width, hidden_width), (hidden_width, width),
        (width, 4 * width), (1, 4 * width), (1, width), (1, width), (1, width), (1, width),
        (1, hidden_width),
    ]
    field = pl.BlockSpec((1,) + field_shape[1:], lambda i: (level_of(i), 0, 0, 0))
    return pl.pallas_call(
        merge_kernel,
        grid=(level_count,),
        in_specs=[
            whole(first.shape), whole(second.shape), by_pair(straddle),
            pl.BlockSpec((2, 1) + rows.shape[2:], lambda i: (0, i, 0, 0)),
            whole(first_edge.shape), whole(second_edge.shape), by_pair(straddle_edge),
            by_pair(corner),
        ] + [whole(v.shape) for v in (grad, small, context)],
        out_specs=[field, field] + [whole(s) for s in shapes],
        out_shape=[shape_of(field_shape, BF16)] * 2 + [shape_of(s, F32) for s in shapes],
        compiler_params=pltpu.CompilerParams(vmem_limit_bytes=VMEM_LIMIT),
    )(
        first, second, straddle, rows, first_edge, second_edge, straddle_edge, corner, grad, small,
        context,
    )


def pass_along(block, lat_step, lon_step):
    lat, lon = lax.axis_size("lat"), lax.axis_size("lon")
    route = []
    for i in range(lat):
        for j in range(lon):
            target = ((i + lat_step) % lat) * lon + (j + lon_step) % lon
            route.append((i * lon + j, target))
    return lax.ppermute(block, ("lat", "lon"), route)


def on_device(
    tokens, cotangent, w_qkv, q_bias, v_bias, w_proj, b_proj, w_up, b_up, w_down, b_down,
    w_mod, b_mod, rel_table, crop_rows, lead_hours,
):
    width = tokens.shape[-1]
    fields = [field.transpose(0, 2, 1, 3) for field in (tokens, cotangent)]
    rows, own_cols = cut_strips(*fields)
    cols = pass_along(own_cols, 0, 1)
    rows = pass_along(rows, 1, 0)
    corner = pass_along(own_cols, 1, 1)

    table = rel_table.transpose(1, 3, 0, 2).reshape(HEADS * OFFSETS, 2 * WY - 1)
    bias, vecs, context = set_up(
        lead_hours, w_mod, b_mod, b_proj, b_down, q_bias, v_bias, b_up, table
    )
    constants = [bias, vecs, w_qkv, w_proj, w_up, w_down]
    sums = [
        jnp.zeros((4 * width + 2 * w_up.shape[1], width), F32),
        jnp.zeros((VECTORS + TABLE_ROWS, width), F32),
        jnp.zeros((WINDOW, SCORES), F32),
    ]
    first, first_edge, *sums = block_call(
        False, 0, 1, False, crop_rows, fields, [cols], constants, sums
    )
    straddle, straddle_edge, *sums, rows_back = block_call(
        True, 0, 2, False, crop_rows, fields, [cols, rows, corner], constants, sums
    )
    rows_back = pass_along(rows_back, -1, 0)
    corner_back = pass_along(straddle_edge, -1, -1)
    straddle_edge = pass_along(straddle_edge, 0, -1)
    first_edge = pass_along(first_edge, 0, -1)
    second, second_edge, grad, small = block_call(
        False, 1, 1, True, crop_rows, fields, [cols], constants, sums
    )
    second_edge = pass_along(second_edge, 0, -1)
    grad, small = sum_over_devices(grad, small)
    (
        mixed, token_grad, grad_qkv, grad_proj, grad_up, grad_down, grad_mod, grad_mod_bias,
        grad_proj_bias, grad_down_bias, grad_q_bias, grad_v_bias, grad_up_bias,
    ) = merge(
        fields[0].shape, w_up.shape[1], first, second, straddle, rows_back, first_edge, second_edge,
        straddle_edge, corner_back, grad, small, context,
    )
    table_sum = small[VECTORS : VECTORS + 2 * WY - 1, : HEADS * OFFSETS][::-1]
    grad_table = table_sum.reshape(2 * WY - 1, 2 * WZ - 1, 2 * WX - 1, HEADS).transpose(3, 1, 0, 2)
    return (
        mixed.transpose(0, 2, 1, 3),
        token_grad.transpose(0, 2, 1, 3),
        grad_qkv,
        grad_q_bias[0],
        grad_v_bias[0],
        grad_proj,
        grad_proj_bias[0],
        grad_up,
        grad_up_bias[0],
        grad_down,
        grad_down_bias[0],
        grad_mod,
        grad_mod_bias[0],
        grad_table,
    )


def solution(mesh):
    split = P(None, "lat", "lon", None)
    return jax.shard_map(
        on_device,
        mesh=mesh,
        in_specs=(split, split) + (P(),) * 14,
        out_specs=(split, split) + (P(),) * 12,
        check_vma=False,
    )
```

```python
import functools
import math

import jax
import jax.numpy as jnp
from jax import lax
from jax.experimental import pallas as pl
from jax.experimental.pallas import tpu as pltpu
from jax.sharding import PartitionSpec as P

WZ = 2
WY = 12
WX = 6
CELLS = WZ * WY
WINDOW = CELLS * WX
HEADS = 4
SCORES = HEADS * WINDOW
HALF_Y = WY // 2
HALF_X = WX // 2
BLOCK_WINDOWS = 5
OFFSETS = (2 * WZ - 1) * (2 * WX - 1)
VECTORS = 16
TABLE_ROWS = 2 * WY
EDGE = HALF_X * CELLS
PACKED_COLS = 8

NORM_EPSILON = 1e-05
MASKED_SCORE = -1000000000.0
F32 = jnp.float32
BF16 = jnp.bfloat16
MESH = pl.DeviceIdType.MESH
ANY = pl.BlockSpec(memory_space=pl.ANY)
VMEM_LIMIT = 60 * 2**20


def dot_nn(left, right):
    return lax.dot_general(left, right, (((1,), (0,)), ((), ())), preferred_element_type=F32)


def dot_nt(left, right):
    return lax.dot_general(left, right, (((1,), (1,)), ((), ())), preferred_element_type=F32)


def dot_tn(left, right):
    return lax.dot_general(left, right, (((0,), (0,)), ((), ())), preferred_element_type=F32)


def iota(shape, axis):
    return lax.broadcasted_iota(jnp.int32, shape, axis)


def whole(shape, buffers=1):
    return pl.BlockSpec(
        shape, lambda *_: (0,) * len(shape), pipeline_mode=pl.Buffered(buffers)
    )


def shape_of(shape, dtype):
    return jax.ShapeDtypeStruct(shape, dtype)


def packed_rows(col_count):
    return -(-col_count * HALF_Y // 16) * 16


def offset_pick(key_x, key_z):
    lane = iota((HEADS * OFFSETS, SCORES), 1)
    head, rest = lane // WINDOW, lane % WINDOW
    query_x, query_z = rest // CELLS, (rest % CELLS) // WY
    offset_z, offset_x = query_z - key_z + WZ - 1, query_x - key_x + WX - 1
    place = (offset_z * (2 * WX - 1) + offset_x) * HEADS + head
    return iota((HEADS * OFFSETS, SCORES), 0) == place


def setup_kernel(
    lead_ref, w_mod_ref, b_mod_ref, b_proj_ref, b_down_ref, q_bias_ref, v_bias_ref, b_up_ref,
    table_ref, bias_ref, vec_ref, context_ref,
):
    width = w_mod_ref.shape[0]
    half = width // 2
    lanes = context_ref.shape[1]
    fraction = iota((half, lanes), 0).astype(F32) / half
    angles = lead_ref[0].astype(F32) * jnp.exp(-math.log(1000.0) * fraction)
    waves = jnp.concatenate([jnp.sin(angles), jnp.cos(angles)], axis=0)
    context = waves * (1.0 / (1.0 + jnp.exp(-waves)))
    context_ref[...] = context
    for part in range(4):
        pieces = []
        for j in range(width // lanes):
            start = part * width + j * lanes
            pieces.append(
                jnp.sum(context * w_mod_ref[:, start : start + lanes].astype(F32), axis=0, keepdims=True)
            )
        vec_ref[part : part + 1, :] = jnp.concatenate(pieces, axis=1) + b_mod_ref[
            :, part * width : (part + 1) * width
        ].astype(F32)
    rows = [b_proj_ref[...], b_down_ref[...], q_bias_ref[...], jnp.zeros((1, width), BF16), v_bias_ref[...]]
    rows += [b_up_ref[:, j * width : (j + 1) * width] for j in range(4)]
    rows += [jnp.zeros((1, width), BF16)] * (VECTORS - 4 - len(rows))
    for i, row in enumerate(rows):
        vec_ref[4 + i : 5 + i, :] = row.astype(F32)

    offsets_y = 2 * WY - 1
    backwards = iota((TABLE_ROWS, offsets_y), 0) + iota((TABLE_ROWS, offsets_y), 1) == offsets_y - 1
    table = dot_nt(backwards.astype(BF16), table_ref[...]).astype(BF16)
    query_y = iota((WY, SCORES), 1) % WY
    for key_x in range(WX):
        for key_z in range(WZ):
            spread = dot_nn(table, offset_pick(key_x, key_z).astype(BF16))
            rows = spread[WY - 1 : 2 * WY - 1]
            for y in range(1, WY):
                rows = jnp.where(query_y == y, spread[WY - 1 - y : 2 * WY - 1 - y], rows)
            start = key_x * CELLS + key_z * WY
            bias_ref[start : start + WY, :] = rows


def set_up(lead_hours, w_mod, b_mod, b_proj, b_down, q_bias, v_bias, b_up, table):
    width = w_mod.shape[0]
    vmem = pl.BlockSpec(memory_space=pltpu.VMEM)
    vectors = [v[None] for v in (b_mod, b_proj, b_down, q_bias, v_bias, b_up)]
    return pl.pallas_call(
        setup_kernel,
        in_specs=[pl.BlockSpec(memory_space=pltpu.SMEM)] + [vmem] * 8,
        out_specs=[vmem] * 3,
        out_shape=[
            shape_of((WINDOW, SCORES), F32),
            shape_of((VECTORS, width), F32),
            shape_of((width, 128), F32),
        ],
        compiler_params=pltpu.CompilerParams(vmem_limit_bytes=VMEM_LIMIT),
    )(lead_hours, w_mod, *vectors, table)


def table_grad(score_sum_ref):
    query_y = iota((WY, SCORES), 1) % WY
    total = jnp.zeros((TABLE_ROWS, HEADS * OFFSETS), F32)
    for key_x in range(WX):
        for key_z in range(WZ):
            start = key_x * CELLS + key_z * WY
            rows = score_sum_ref[start : start + WY, :]
            spread = jnp.zeros((TABLE_ROWS, SCORES), F32)
            for y in range(WY):
                own = jnp.where(query_y == y, rows, 0.0)
                pads = (WY - 1 - y, TABLE_ROWS - (2 * WY - 1 - y))
                parts = [jnp.zeros((p, SCORES), F32) for p in pads]
                spread = spread + jnp.concatenate(
                    ([parts[0]] if pads[0] else []) + [own, parts[1]], axis=0
                )
            pick = offset_pick(key_x, key_z).astype(BF16)
            high = spread.astype(BF16)
            low = (spread - high.astype(F32)).astype(BF16)
            total = total + dot_nt(high, pick) + dot_nt(low, pick)
    return total


def row_mean(values):
    return jnp.mean(values, axis=-1, keepdims=True)


def norm(values):
    center = values - row_mean(values)
    inverse = lax.rsqrt(row_mean(center * center) + NORM_EPSILON)
    return center * inverse, inverse


def norm_back(grad, normed, inverse):
    return inverse * (grad - row_mean(grad) - normed * row_mean(grad * normed))


def gelu_both(values):
    gauss_cdf = 0.5 * (1.0 + lax.erf(values * math.sqrt(0.5)))
    density = jnp.exp(values * values * -0.5) * (1.0 / math.sqrt(2.0 * math.pi))
    return values * gauss_cdf, gauss_cdf + values * density


def by_head(values):
    width = values.shape[-1] // HEADS
    lane_head = iota(values.shape, 1) // width
    zero = jnp.zeros_like(values)
    return jnp.concatenate([jnp.where(lane_head == h, values, zero) for h in range(HEADS)], axis=0)


def own_head(stacked):
    cells = stacked.shape[0] // HEADS
    width = stacked.shape[-1] // HEADS
    lane_head = iota((cells, stacked.shape[-1]), 1) // width
    picked = stacked[:cells]
    for h in range(1, HEADS):
        picked = jnp.where(lane_head == h, stacked[h * cells : (h + 1) * cells], picked)
    return picked


def store_windows(field, western, out_ref):
    width = out_ref.shape[1]
    for c in range(HALF_X):
        out_ref[c * CELLS : (c + 1) * CELLS, :] = jnp.concatenate(
            [western(c, z) for z in range(WZ)], axis=0
        )
    own_cols = out_ref.shape[0] // CELLS - HALF_X
    for start in range(0, own_cols, PACKED_COLS):
        count = min(PACKED_COLS, own_cols - start)
        both = jnp.concatenate([field(start, count, z) for z in range(WZ)], axis=1)
        first = (start + HALF_X) * CELLS
        out_ref[first : first + count * CELLS, :] = both.reshape(count * CELLS, width)


def unpack_strip(rows, count):
    return jnp.stack([rows[c * HALF_Y : (c + 1) * HALF_Y] for c in range(count)], axis=0)


def mask_scores(bias, level_wraps, base, first_band, crop_own, crop_before, row_count):
    def parts(cell):
        z, row = (cell % CELLS) // WY, base + cell % WY
        part = 2 * jnp.where(z == WZ - 1, level_wraps, 0)
        part = part + jnp.where((row >= 0) & (row < HALF_Y), first_band, 0)
        crop = jnp.where(row >= 0, crop_own, crop_before)
        return part, jnp.where(row >= 0, row, row + row_count) >= row_count - crop

    key = iota(bias.shape, 0)
    query = iota(bias.shape, 1) % WINDOW
    key_part, key_valid = parts(key)
    query_part, _ = parts(query)
    allowed = (key_part == query_part) & (key_valid | (key == query))
    return jnp.where(allowed, bias, bias + MASKED_SCORE)


GROUPS = 4


def group_pair(group):
    return group // 2


def field_level(pair, z):
    return lax.rem(WZ * pair + z + WZ // 2, 2 * WZ)


def block_kernel(
    crop_ref, tokens_ref, cotangent_ref, bias_ref, vec_ref, w_qkv_ref, w_proj_ref, w_up_ref, w_down_ref,
    win_ref, rows_back_ref, edge_back_ref, corner_back_ref, grad_ref, small_ref,
    fields_ref, rows_out_ref, rows_in_ref, cols_in_ref, corner_in_ref, out_ref,
    score_bias_ref, xw_ref, gw_ref, qkv_ref, prob_ref, att_ref, dqkv_ref, score_sum_ref,
    field_sems, halo_sems, rows_sems, back_sems, edge_sems, corner_sems, out_sems,
):
    width = vec_ref.shape[1]
    hidden_width = w_up_ref.shape[1]
    _, level_count, col_count, row_count, _ = fields_ref.shape
    band_count = crop_ref.shape[0]
    score_scale = (width // HEADS) ** -0.5
    lat, lon = lax.axis_index("lat"), lax.axis_index("lon")
    lat_size, lon_size = lax.axis_size("lat"), lax.axis_size("lon")

    def device(lat_step, lon_step):
        return (
            lax.rem(lat + lat_step + lat_size, lat_size), lax.rem(lon + lon_step + lon_size, lon_size)
        )

    steps = ((1, 0), (0, 1), (1, 1))
    barrier = pltpu.get_barrier_semaphore()
    for lat_step, lon_step in steps:
        for sign in (1, -1):
            pl.semaphore_signal(
                barrier, inc=1, device_id=device(sign * lat_step, sign * lon_step), device_id_type=MESH
            )

    loads = []
    for level in (1, 2, 3, 0):
        for a, ref in enumerate((tokens_ref, cotangent_ref)):
            loads.append(pltpu.make_async_copy(
                ref.at[level], fields_ref.at[a, level], field_sems.at[len(loads)]
            ))
            loads[-1].start()

    def remote(source, target, sems, lat_step, lon_step):
        return pltpu.make_async_remote_copy(
            src_ref=source, dst_ref=target, send_sem=sems.at[0], recv_sem=sems.at[1],
            device_id=device(lat_step, lon_step), device_id_type=MESH,
        )

    last_cols = fields_ref.at[:, :, pl.ds(col_count - HALF_X, HALF_X)]
    cols_copy = remote(last_cols, cols_in_ref, halo_sems.at[0], 0, 1)
    corner_copy = remote(last_cols, corner_in_ref, halo_sems.at[1], 1, 1)

    def rows_copy(pair):
        return remote(rows_out_ref.at[pair], rows_in_ref.at[pair], rows_sems.at[pair], 1, 0)

    def back_copy(pair):
        return remote(rows_out_ref.at[pair], rows_back_ref.at[pair], back_sems.at[pair], -1, 0)

    def edge_rows(group):
        return out_ref.at[lax.rem(group, 2), :, pl.ds(0, edge_back_ref.shape[2])]

    def edge_copy(group):
        return remote(edge_rows(group), edge_back_ref.at[group], edge_sems.at[group], 0, -1)

    def corner_back_copy(group):
        pair = group_pair(group)
        return remote(edge_rows(group), corner_back_ref.at[pair], corner_sems.at[pair], -1, -1)

    def out_copy(group):
        return pltpu.make_async_copy(
            out_ref.at[lax.rem(group, 2)], win_ref.at[:, group], out_sems.at[group]
        )

    for pair in range(2):
        for z in range(WZ):
            level = (WZ * pair + z + WZ // 2) % level_count
            for a in range(2):
                loads[(pair * WZ + z) * 2 + a].wait()
                for start in range(0, col_count, PACKED_COLS):
                    count = min(PACKED_COLS, col_count - start)
                    block = fields_ref[a, level, start : start + count].astype(F32)
                    packed = [block[c, row_count - HALF_Y :] for c in range(count)]
                    rows_out_ref[
                        pair, a, z, start * HALF_Y : (start + count) * HALF_Y, :
                    ] = jnp.concatenate(packed, axis=0).astype(BF16)
        if pair == 0:
            pl.semaphore_wait(barrier, 2 * len(steps))
        rows_copy(pair).start()
    cols_copy.start()
    corner_copy.start()

    grad_ref[...] = jnp.zeros_like(grad_ref)
    small_ref[...] = jnp.zeros_like(small_ref)
    score_sum_ref[...] = jnp.zeros_like(score_sum_ref)
    rows = BLOCK_WINDOWS * WINDOW
    shift_one, scale_one, shift_two, scale_two, b_proj, b_down = [
        vec_ref[i : i + 1, :] for i in range(6)
    ]
    qkv_shift = jnp.concatenate([vec_ref[i : i + 1, :] for i in range(6, 9)], axis=1)
    b_up = jnp.concatenate([vec_ref[i : i + 1, :] for i in range(9, 13)], axis=1)

    def add_grad(first, value):
        for j in range(value.shape[1] // width):
            grad_ref[(first + j) * width : (first + j + 1) * width, :] += value[
                :, j * width : (j + 1) * width
            ]

    def column_sums(values):
        return jnp.sum(values, axis=0, keepdims=True)

    def block(index, slot):
        here = pl.ds(pl.multiple_of(index * rows, 16), rows)
        x32 = xw_ref[here, :]
        x = x32.astype(BF16)
        qkv_ref[...] = (dot_nn(x, w_qkv_ref[...]) + qkv_shift).astype(BF16)
        for w in range(BLOCK_WINDOWS):
            cells = pl.ds(w * WINDOW, WINDOW)
            queries = by_head(qkv_ref[cells, :width] * BF16(score_scale))
            scores = dot_nt(qkv_ref[cells, width : 2 * width], queries) + score_bias_ref[...]
            top = jnp.max(scores, axis=0, keepdims=True)
            exps = jnp.exp(scores - top)
            prob = exps * (1.0 / jnp.sum(exps, axis=0, keepdims=True))
            prob_ref[w] = prob
            att_ref[cells, :] = own_head(
                dot_tn(prob.astype(BF16), qkv_ref[cells, 2 * width :])
            ).astype(BF16)

        att = att_ref[...]
        branch = dot_nn(att, w_proj_ref[...]) + b_proj
        norm_one, inverse_one = norm(branch)
        middle = x32 + norm_one * (1.0 + scale_one) + shift_one
        middle_low = middle.astype(BF16)
        pre = dot_nn(middle_low, w_up_ref[...]) + b_up
        hidden, slope = gelu_both(pre)
        hidden = hidden.astype(BF16)
        second = dot_nn(hidden, w_down_ref[...]) + b_down
        norm_two, inverse_two = norm(second)
        out_ref[slot, 0, here, :] = (middle + norm_two * (1.0 + scale_two) + shift_two).astype(BF16)

        g = gw_ref[here, :]
        second_low = norm_back(g * (1.0 + scale_two), norm_two, inverse_two).astype(BF16)
        pre_grad = dot_nt(second_low, w_down_ref[...]) * slope
        add_grad(8, dot_tn(second_low, hidden))
        pre_low = pre_grad.astype(BF16)
        up_sums = column_sums(pre_grad)
        middle_grad = g + dot_nt(pre_low, w_up_ref[...])
        add_grad(4, dot_tn(middle_low, pre_low))
        branch_low = norm_back(middle_grad * (1.0 + scale_one), norm_one, inverse_one).astype(BF16)
        att_ref[...] = dot_nt(branch_low, w_proj_ref[...]).astype(BF16)
        add_grad(3, dot_tn(att, branch_low))

        for w in range(BLOCK_WINDOWS):
            cells = pl.ds(w * WINDOW, WINDOW)
            queries = by_head(qkv_ref[cells, :width] * BF16(score_scale))
            out_grad = by_head(att_ref[cells, :])
            prob = prob_ref[w]
            prob_grad = dot_nt(qkv_ref[cells, 2 * width :], out_grad)
            score_grad = prob * (prob_grad - jnp.sum(prob_grad * prob, axis=0, keepdims=True))
            score_sum_ref[...] += score_grad
            score_grad = score_grad.astype(BF16)
            dqkv_ref[cells, :width] = (
                own_head(dot_tn(score_grad, qkv_ref[cells, width : 2 * width])) * score_scale
            ).astype(BF16)
            dqkv_ref[cells, width : 2 * width] = dot_nn(score_grad, queries).astype(BF16)
            dqkv_ref[cells, 2 * width :] = dot_nn(prob.astype(BF16), out_grad).astype(BF16)

        dqkv = dqkv_ref[...]
        out_ref[slot, 1, here, :] = (middle_grad + dot_nt(dqkv, w_qkv_ref[...])).astype(BF16)
        add_grad(0, dot_tn(x, dqkv))
        qkv_sums = column_sums(dqkv.astype(F32))
        sums = [
            column_sums(middle_grad), column_sums(middle_grad * norm_one), column_sums(g),
            column_sums(g * norm_two), column_sums(branch_low.astype(F32)),
            column_sums(second_low.astype(F32)),
        ]
        sums += [qkv_sums[:, j * width : (j + 1) * width] for j in range(3)]
        sums += [up_sums[:, j * width : (j + 1) * width] for j in range(hidden_width // width)]
        sums += [jnp.zeros((VECTORS - len(sums), width), F32)]
        small_ref[:VECTORS, :] += jnp.concatenate(sums, axis=0)
        return slot

    def gather(pair, straddles):
        for a, target in enumerate((xw_ref, gw_ref)):
            def field(start, count, z, a=a):
                own = fields_ref[a, field_level(pair, z), start : start + count].astype(F32)
                if not straddles:
                    return own[:, HALF_Y : HALF_Y + WY]
                strip = rows_in_ref[pair, a, z, start * HALF_Y : (start + count) * HALF_Y, :]
                return jnp.concatenate(
                    [unpack_strip(strip.astype(F32), count), own[:, :HALF_Y]], axis=1
                )

            def western(c, z, a=a):
                own = cols_in_ref[a, field_level(pair, z), c].astype(F32)
                if not straddles:
                    return own[HALF_Y : HALF_Y + WY]
                before = corner_in_ref[a, field_level(pair, z), c].astype(F32)
                return jnp.concatenate([before[row_count - HALF_Y :], own[:HALF_Y]], axis=0)

            store_windows(field, western, target)

    def send_back(pair, slot):
        for a in range(2):
            for start in range(0, col_count - HALF_X, PACKED_COLS):
                count = min(PACKED_COLS, col_count - HALF_X - start)
                first = (start + HALF_X) * CELLS
                cells = out_ref[slot, a, first : first + count * CELLS, :].astype(F32)
                for z in range(WZ):
                    pieces = [
                        cells[c * CELLS + z * WY : c * CELLS + z * WY + HALF_Y] for c in range(count)
                    ]
                    rows_out_ref[
                        pair, a, z, start * HALF_Y : (start + count) * HALF_Y, :
                    ] = jnp.concatenate(pieces, axis=0).astype(BF16)
        back_copy(pair).start()

    def group_step(group, carry):
        pair, slot = group_pair(group), lax.rem(group, 2)
        inner = (group == 0) | (group == GROUPS - 1)

        @pl.when(group == 0)
        def _():
            cols_copy.wait_recv()

        @pl.when(group == 1)
        def _():
            corner_copy.wait_recv()

        @pl.when(group >= 2)
        def _():
            out_copy(group - 2).wait()
            edge_copy(group - 2).wait_send()

        @pl.when(group == GROUPS - 1)
        def _():
            corner_back_copy(1).wait_send()

        @pl.when(inner)
        def _():
            gather(pair, False)

        @pl.when(jnp.logical_not(inner))
        def _():
            rows_copy(pair).wait_recv()
            gather(pair, True)

        score_bias_ref[...] = mask_scores(
            bias_ref[...], pair, jnp.where(inner, HALF_Y, -HALF_Y), (lat == 0).astype(jnp.int32),
            crop_ref[lat], crop_ref[lax.rem(lat + band_count - 1, band_count)], row_count,
        )
        lax.fori_loop(0, col_count // WX // BLOCK_WINDOWS, block, slot)
        out_copy(group).start()
        edge_copy(group).start()

        @pl.when(jnp.logical_not(inner))
        def _():
            corner_back_copy(group).start()
            rows_copy(pair).wait_send()
            send_back(pair, slot)

        return carry

    lax.fori_loop(0, GROUPS, group_step, 0)
    small_ref[VECTORS:, : HEADS * OFFSETS] = table_grad(score_sum_ref)
    for group in (2, 3):
        out_copy(group).wait()
        edge_copy(group).wait_send()
    corner_back_copy(2).wait_send()
    cols_copy.wait_send()
    corner_copy.wait_send()
    for pair in range(2):
        back_copy(pair).wait()
        corner_back_copy(pair + 1).wait_recv()
    for group in range(GROUPS):
        edge_copy(group).wait_recv()


def block_call(crop_rows, tokens, cotangent, constants):
    level_count, col_count, row_count, width = tokens.shape
    vmem = pl.BlockSpec(memory_space=pltpu.VMEM)
    cells = col_count * CELLS
    rows = BLOCK_WINDOWS * WINDOW
    edge = -(-EDGE // 16) * 16
    pairs = level_count // WZ
    strips = (pairs, 2, WZ, packed_rows(col_count), width)
    grad_rows = 4 * width + 2 * constants[4].shape[1]
    sends = pltpu.SemaphoreType.DMA
    return pl.pallas_call(
        block_kernel,
        in_specs=[pl.BlockSpec(memory_space=pltpu.SMEM), ANY, ANY] + [vmem] * len(constants),
        out_specs=[ANY] * 4 + [vmem] * 2,
        out_shape=[
            shape_of((2, GROUPS, cells, width), BF16),
            shape_of(strips, BF16),
            shape_of((GROUPS, 2, edge, width), BF16),
            shape_of((pairs, 2, edge, width), BF16),
            shape_of((grad_rows, width), F32),
            shape_of((VECTORS + TABLE_ROWS, width), F32),
        ],
        scratch_shapes=[
            pltpu.VMEM((2,) + tokens.shape, BF16),
            pltpu.VMEM(strips, BF16),
            pltpu.VMEM(strips, BF16),
            pltpu.VMEM((2, level_count, HALF_X, row_count, width), BF16),
            pltpu.VMEM((2, level_count, HALF_X, row_count, width), BF16),
            pltpu.VMEM((2, 2, cells, width), BF16),
            pltpu.VMEM((WINDOW, SCORES), F32),
            pltpu.VMEM((cells, width), F32),
            pltpu.VMEM((cells, width), F32),
            pltpu.VMEM((rows, 3 * width), BF16),
            pltpu.VMEM((BLOCK_WINDOWS, WINDOW, SCORES), F32),
            pltpu.VMEM((rows, width), BF16),
            pltpu.VMEM((rows, 3 * width), BF16),
            pltpu.VMEM((WINDOW, SCORES), F32),
            sends((2 * level_count,)), sends((2, 2)), sends((pairs, 2)), sends((pairs, 2)),
            sends((GROUPS, 2)), sends((pairs, 2)), sends((GROUPS,)),
        ],
        cost_estimate=pl.CostEstimate(
            flops=GROUPS * cells * 5_200_000, bytes_accessed=32 * 2**20, transcendentals=0
        ),
        compiler_params=pltpu.CompilerParams(
            collective_id=1, has_side_effects=True, vmem_limit_bytes=VMEM_LIMIT
        ),
    )(crop_rows, tokens, cotangent, *constants)


def halved(rows, count):
    sizes = [rows >> (i + 1) for i in range(count)]
    return sizes, [sum(sizes[:i]) for i in range(count + 1)]


def sum_kernel(
    bits, halvings, parts, grad_ref, small_ref, out_ref, small_out_ref,
    acc_ref, send_ref, recv_ref, more_ref, small_recv_ref, sems, small_sems,
):
    axes = ("lat", "lon")
    places = {axis: lax.axis_index(axis) for axis in axes}
    own_bit, partner = {}, {}
    for axis, bit in bits:
        value = (places[axis] // 2**bit) % 2
        own_bit[axis, bit] = value
        moved = dict(places)
        moved[axis] = places[axis] + 2**bit * (1 - 2 * value)
        partner[axis, bit] = tuple(moved[name] for name in axes)

    barrier = pltpu.get_barrier_semaphore()
    for bit in bits:
        pl.semaphore_signal(barrier, inc=1, device_id=partner[bit], device_id_type=MESH)
    pl.semaphore_wait(barrier, len(bits))

    def send(source, target, pair, bit):
        copy = pltpu.make_async_remote_copy(
            src_ref=source, dst_ref=target, send_sem=pair.at[0], recv_sem=pair.at[1],
            device_id=partner[bit], device_id_type=MESH,
        )
        copy.start()
        return copy

    part_rows = grad_ref.shape[0] // parts
    sizes, starts = halved(part_rows, halvings)
    shard = sizes[-1]
    orders = []
    for p in range(parts):
        order = list(bits[:halvings])
        if p == 1 and halvings > 2:
            order[1], order[2] = order[2], order[1]
        orders.append(order)
    low = [p * part_rows for p in range(parts)]
    small_out_ref[...] = small_ref[...]
    acc_ref[...] = grad_ref[...]

    def halve(p, s):
        bit, size = orders[p][s], sizes[s]
        place = pl.ds(p * starts[-1] + starts[s], size)
        away = pl.multiple_of(low[p] + (1 - own_bit[bit]) * size, 16)
        send_ref[place, :] = acc_ref[pl.ds(away, size), :].astype(BF16)
        low[p] = low[p] + own_bit[bit] * size
        return send(send_ref.at[place], recv_ref.at[place], sems.at[p, s], bit)

    def add_half(p, s, copy):
        size = sizes[s]
        copy.wait()
        place = pl.ds(p * starts[-1] + starts[s], size)
        here = pl.ds(pl.multiple_of(low[p], 16), size)
        acc_ref[here, :] += recv_ref[place, :].astype(F32)

    copies = [halve(p, 0) for p in range(parts)]
    for s, bit in enumerate(bits):
        small_copy = send(small_out_ref, small_recv_ref.at[s], small_sems.at[s], bit)
        if s < halvings:
            for p in range(parts):
                add_half(p, s, copies[p])
                if s + 1 < halvings:
                    copies[p] = halve(p, s + 1)
        small_copy.wait()
        small_out_ref[...] += small_recv_ref[s]

    for p in range(parts):
        here = pl.ds(pl.multiple_of(low[p], 16), shard)
        out_ref[here, :] = acc_ref[here, :].astype(BF16)
        for s in range(halvings, len(bits)):
            mine = more_ref.at[0, p, s - halvings]
            theirs = more_ref.at[1, p, s - halvings]
            mine[...] = out_ref[here, :]
            send(mine, theirs, sems.at[p, s], bits[s]).wait()
            out_ref[here, :] = (mine[...].astype(F32) + theirs[...].astype(F32)).astype(BF16)

    def give(p, s):
        here = out_ref.at[pl.ds(pl.multiple_of(low[p], 16), sizes[s]), :]
        low[p] = low[p] - own_bit[orders[p][s]] * sizes[s]
        return send(here, here, sems.at[p, len(bits) + s], orders[p][s])

    copies = [give(p, halvings - 1) for p in range(parts)]
    for s in reversed(range(halvings)):
        for p in range(parts):
            copies[p].wait()
            if s:
                copies[p] = give(p, s - 1)


def sum_over_devices(grad, small):
    bits = [("lon", 0), ("lon", 1), ("lat", 0), ("lat", 1), ("lat", 2)]
    bits = [b for b in bits if 2 ** b[1] < lax.axis_size(b[0])]
    bits += [("lat", b) for b in range(3, lax.axis_size("lat").bit_length() - 1)]
    bits += [("lon", b) for b in range(2, lax.axis_size("lon").bit_length() - 1)]
    if not bits:
        return grad.astype(BF16), small
    halvings, parts = min(5, len(bits)), 2
    rows, width = grad.shape
    sizes, starts = halved(rows // parts, halvings)
    more = max(1, len(bits) - halvings)
    vmem = pl.BlockSpec(memory_space=pltpu.VMEM)
    return pl.pallas_call(
        functools.partial(sum_kernel, tuple(bits), halvings, parts),
        in_specs=[vmem, vmem],
        out_specs=[vmem, vmem],
        out_shape=[shape_of(grad.shape, BF16), shape_of(small.shape, F32)],
        scratch_shapes=[
            pltpu.VMEM(grad.shape, F32),
            pltpu.VMEM((parts * starts[-1], width), BF16),
            pltpu.VMEM((parts * starts[-1], width), BF16),
            pltpu.VMEM((2, parts, more, sizes[-1], width), BF16),
            pltpu.VMEM((len(bits),) + small.shape, F32),
            pltpu.SemaphoreType.DMA((parts, len(bits) + halvings, 2)),
            pltpu.SemaphoreType.DMA((len(bits), 2)),
        ],
        compiler_params=pltpu.CompilerParams(
            collective_id=0, has_side_effects=True, vmem_limit_bytes=VMEM_LIMIT
        ),
    )(grad, small)


def merge_kernel(
    inner_ref, straddle_ref, rows_ref, inner_edge_ref, straddle_edge_ref, corner_ref,
    grad_ref, small_ref, context_ref, *out_refs,
):
    fields, grads = out_refs[:2], out_refs[2:]
    _, col_count, row_count, width = fields[0].shape
    step = pl.program_id(0)

    def piece(rows_of, a, first_col, count, first, size):
        block = rows_of(a)[first_col * CELLS : (first_col + count) * CELLS, :].astype(F32)
        return block.reshape(count, CELLS, width)[:, first : first + size]

    straddle, inner = lambda a: straddle_ref.at[a, 0], lambda a: inner_ref.at[a, 0]
    straddle_edge, inner_edge, corner = (
        lambda a, ref=ref: ref.at[0, a] for ref in (straddle_edge_ref, inner_edge_ref, corner_ref)
    )
    for z in range(WZ):
        @pl.when(lax.rem(step, WZ) == z)
        def _():
            first = z * WY
            for a, field in enumerate(fields):
                for start in range(0, col_count - HALF_X, PACKED_COLS):
                    count = min(PACKED_COLS, col_count - HALF_X - start)
                    strip = rows_ref[0, a, 0, start * HALF_Y : (start + count) * HALF_Y, :]
                    block = jnp.concatenate([
                        piece(straddle, a, start + HALF_X, count, first + HALF_Y, HALF_Y),
                        piece(inner, a, start + HALF_X, count, first, WY),
                        unpack_strip(strip.astype(F32), count),
                    ], axis=1)
                    field[0, start : start + count] = block.astype(BF16)
                block = jnp.concatenate([
                    piece(straddle_edge, a, 0, HALF_X, first + HALF_Y, HALF_Y),
                    piece(inner_edge, a, 0, HALF_X, first, WY),
                    piece(corner, a, 0, HALF_X, first, HALF_Y),
                ], axis=1)
                field[0, col_count - HALF_X :] = block.astype(BF16)

    grad_qkv, grad_proj, grad_up, grad_down, grad_mod, *vectors = grads

    def slab(index):
        return grad_ref[index * width : (index + 1) * width, :].astype(F32)

    @pl.when(step == 0)
    def _():
        for j in range(3):
            grad_qkv[:, j * width : (j + 1) * width] = slab(j)
        grad_proj[...] = slab(3)

    @pl.when(step == 1)
    def _():
        for j in range(grad_up.shape[1] // width):
            grad_up[:, j * width : (j + 1) * width] = slab(4 + j)

    @pl.when(step == 2)
    def _():
        for j in range(grad_down.shape[0] // width):
            grad_down[j * width : (j + 1) * width, :] = slab(8 + j).T

    @pl.when(step == 3)
    def _():
        lanes = context_ref.shape[1]
        for part in range(4):
            row = small_ref[part : part + 1, :]
            for j in range(0, width, lanes):
                grad_mod[:, part * width + j : part * width + j + lanes] = (
                    context_ref[...] * row[:, j : j + lanes]
                )
        mod_bias, proj_bias, down_bias, q_bias, v_bias, up_bias = vectors
        mod_bias[...] = jnp.concatenate([small_ref[i : i + 1, :] for i in range(4)], axis=1)
        up_bias[...] = jnp.concatenate([small_ref[i : i + 1, :] for i in range(9, 13)], axis=1)
        for ref, i in ((proj_bias, 4), (down_bias, 5), (q_bias, 6), (v_bias, 8)):
            ref[...] = small_ref[i : i + 1, :]


def merge(field_shape, hidden_width, windows, rows_back, edge_back, corner_back, grad, small, context):
    level_count, col_count, row_count, width = field_shape

    def level_of(i):
        return (i + WZ // 2) % level_count

    def group_of(pair, straddles):
        return 1 + pair if straddles else (GROUPS - 1) * pair

    def windows_of(straddles):
        return pl.BlockSpec(
            (2, 1) + windows.shape[2:], lambda i: (0, group_of(i // WZ, straddles), 0, 0)
        )

    def edge_of(straddles):
        return pl.BlockSpec(
            (1,) + edge_back.shape[1:], lambda i: (group_of(i // WZ, straddles), 0, 0, 0)
        )

    shapes = [
        (width, 3 * width), (width, width), (width, hidden_width), (hidden_width, width),
        (width, 4 * width), (1, 4 * width), (1, width), (1, width), (1, width), (1, width),
        (1, hidden_width),
    ]
    field = pl.BlockSpec((1,) + field_shape[1:], lambda i: (level_of(i), 0, 0, 0))
    return pl.pallas_call(
        merge_kernel,
        grid=(level_count,),
        in_specs=[
            windows_of(False), windows_of(True),
            pl.BlockSpec((1, 2, 1) + rows_back.shape[3:], lambda i: (i // WZ, 0, i % WZ, 0, 0)),
            edge_of(False), edge_of(True),
            pl.BlockSpec((1,) + corner_back.shape[1:], lambda i: (i // WZ, 0, 0, 0)),
        ] + [whole(v.shape) for v in (grad, small, context)],
        out_specs=[field, field] + [whole(s) for s in shapes],
        out_shape=[shape_of(field_shape, BF16)] * 2 + [shape_of(s, F32) for s in shapes],
        compiler_params=pltpu.CompilerParams(vmem_limit_bytes=VMEM_LIMIT),
    )(windows, windows, rows_back, edge_back, edge_back, corner_back, grad, small, context)


def on_device(
    tokens, cotangent, w_qkv, q_bias, v_bias, w_proj, b_proj, w_up, b_up, w_down, b_down,
    w_mod, b_mod, rel_table, crop_rows, lead_hours,
):
    fields = [field.transpose(0, 2, 1, 3) for field in (tokens, cotangent)]
    table = rel_table.transpose(1, 3, 0, 2).reshape(HEADS * OFFSETS, 2 * WY - 1)
    bias, vecs, context = set_up(
        lead_hours, w_mod, b_mod, b_proj, b_down, q_bias, v_bias, b_up, table
    )
    constants = [bias, vecs, w_qkv, w_proj, w_up, w_down]
    windows, rows_back, edge_back, corner_back, grad, small = block_call(
        crop_rows, *fields, constants
    )
    grad, small = sum_over_devices(grad, small)
    (
        mixed, token_grad, grad_qkv, grad_proj, grad_up, grad_down, grad_mod, grad_mod_bias,
        grad_proj_bias, grad_down_bias, grad_q_bias, grad_v_bias, grad_up_bias,
    ) = merge(
        fields[0].shape, w_up.shape[1], windows, rows_back, edge_back, corner_back, grad, small, context
    )
    table_sum = small[VECTORS : VECTORS + 2 * WY - 1, : HEADS * OFFSETS][::-1]
    grad_table = table_sum.reshape(2 * WY - 1, 2 * WZ - 1, 2 * WX - 1, HEADS).transpose(3, 1, 0, 2)
    return (
        mixed.transpose(0, 2, 1, 3),
        token_grad.transpose(0, 2, 1, 3),
        grad_qkv,
        grad_q_bias[0],
        grad_v_bias[0],
        grad_proj,
        grad_proj_bias[0],
        grad_up,
        grad_up_bias[0],
        grad_down,
        grad_down_bias[0],
        grad_mod,
        grad_mod_bias[0],
        grad_table,
    )


def solution(mesh):
    split = P(None, "lat", "lon", None)
    return jax.shard_map(
        on_device,
        mesh=mesh,
        in_specs=(split, split) + (P(),) * 14,
        out_specs=(split, split) + (P(),) * 12,
        check_vma=False,
    )
```

```python
import functools
import math

import jax
import jax.numpy as jnp
from jax import lax
from jax.experimental import pallas as pl
from jax.experimental.pallas import tpu as pltpu
from jax.sharding import PartitionSpec as P

WZ = 2
WY = 12
WX = 6
CELLS = WZ * WY
WINDOW = CELLS * WX
HEADS = 4
SCORES = HEADS * WINDOW
HALF_Y = WY // 2
HALF_X = WX // 2
BLOCK_WINDOWS = 5
OFFSETS = (2 * WZ - 1) * (2 * WX - 1)
VECTORS = 16
TABLE_ROWS = 2 * WY
EDGE = HALF_X * CELLS
PACKED_COLS = 8

NORM_EPSILON = 1e-05
MASKED_SCORE = -1000000000.0
F32 = jnp.float32
BF16 = jnp.bfloat16
MESH = pl.DeviceIdType.MESH
ANY = pl.BlockSpec(memory_space=pl.ANY)
VMEM_LIMIT = 60 * 2**20


def dot_nn(left, right):
    return lax.dot_general(left, right, (((1,), (0,)), ((), ())), preferred_element_type=F32)


def dot_nt(left, right):
    return lax.dot_general(left, right, (((1,), (1,)), ((), ())), preferred_element_type=F32)


def dot_tn(left, right):
    return lax.dot_general(left, right, (((0,), (0,)), ((), ())), preferred_element_type=F32)


def iota(shape, axis):
    return lax.broadcasted_iota(jnp.int32, shape, axis)


def whole(shape, buffers=1):
    return pl.BlockSpec(
        shape, lambda *_: (0,) * len(shape), pipeline_mode=pl.Buffered(buffers)
    )


def shape_of(shape, dtype):
    return jax.ShapeDtypeStruct(shape, dtype)


def packed_rows(col_count):
    return -(-col_count * HALF_Y // 16) * 16


def offset_pick(key_x, key_z):
    lane = iota((HEADS * OFFSETS, SCORES), 1)
    head, rest = lane // WINDOW, lane % WINDOW
    query_x, query_z = rest // CELLS, (rest % CELLS) // WY
    offset_z, offset_x = query_z - key_z + WZ - 1, query_x - key_x + WX - 1
    place = (offset_z * (2 * WX - 1) + offset_x) * HEADS + head
    return iota((HEADS * OFFSETS, SCORES), 0) == place


def setup_kernel(
    lead_ref, w_mod_ref, vectors_ref, table_ref, bias_ref, vec_ref, context_ref,
):
    width = w_mod_ref.shape[0]
    half = width // 2
    lanes = context_ref.shape[1]
    fraction = iota((half, lanes), 0).astype(F32) / half
    angles = lead_ref[0].astype(F32) * jnp.exp(-math.log(1000.0) * fraction)
    waves = jnp.concatenate([jnp.sin(angles), jnp.cos(angles)], axis=0)
    context = waves * (1.0 / (1.0 + jnp.exp(-waves)))
    context_ref[...] = context
    for part in range(4):
        pieces = []
        for j in range(width // lanes):
            start = part * width + j * lanes
            pieces.append(
                jnp.sum(context * w_mod_ref[:, start : start + lanes].astype(F32), axis=0, keepdims=True)
            )
        vec_ref[part : part + 1, :] = (
            jnp.concatenate(pieces, axis=1) + vectors_ref[part : part + 1, :].astype(F32)
        )
    vec_ref[4:, :] = vectors_ref[4:, :].astype(F32)

    offsets_y = 2 * WY - 1
    backwards = iota((TABLE_ROWS, offsets_y), 0) + iota((TABLE_ROWS, offsets_y), 1) == offsets_y - 1
    table = dot_nt(backwards.astype(BF16), table_ref[...]).astype(BF16)
    query_y = iota((WY, SCORES), 1) % WY
    for key_x in range(WX):
        for key_z in range(WZ):
            spread = dot_nn(table, offset_pick(key_x, key_z).astype(BF16))
            rows = spread[WY - 1 : 2 * WY - 1]
            for y in range(1, WY):
                rows = jnp.where(query_y == y, spread[WY - 1 - y : 2 * WY - 1 - y], rows)
            start = key_x * CELLS + key_z * WY
            bias_ref[start : start + WY, :] = rows


def set_up(lead_hours, w_mod, vectors, table):
    width = w_mod.shape[0]
    vmem = pl.BlockSpec(memory_space=pltpu.VMEM)
    return pl.pallas_call(
        setup_kernel,
        in_specs=[pl.BlockSpec(memory_space=pltpu.SMEM)] + [vmem] * 3,
        out_specs=[vmem] * 3,
        out_shape=[
            shape_of((WINDOW, SCORES), F32),
            shape_of((VECTORS, width), F32),
            shape_of((width, 128), F32),
        ],
        compiler_params=pltpu.CompilerParams(vmem_limit_bytes=VMEM_LIMIT),
    )(lead_hours, w_mod, vectors, table)


def table_grad(score_sum_ref):
    query_y = iota((WY, SCORES), 1) % WY
    total = jnp.zeros((TABLE_ROWS, HEADS * OFFSETS), F32)
    for key_x in range(WX):
        for key_z in range(WZ):
            start = key_x * CELLS + key_z * WY
            rows = score_sum_ref[start : start + WY, :]
            spread = jnp.zeros((TABLE_ROWS, SCORES), F32)
            for y in range(WY):
                own = jnp.where(query_y == y, rows, 0.0)
                pads = (WY - 1 - y, TABLE_ROWS - (2 * WY - 1 - y))
                parts = [jnp.zeros((p, SCORES), F32) for p in pads]
                spread = spread + jnp.concatenate(
                    ([parts[0]] if pads[0] else []) + [own, parts[1]], axis=0
                )
            pick = offset_pick(key_x, key_z).astype(BF16)
            high = spread.astype(BF16)
            low = (spread - high.astype(F32)).astype(BF16)
            total = total + dot_nt(high, pick) + dot_nt(low, pick)
    return total


def row_mean(values):
    return jnp.mean(values, axis=-1, keepdims=True)


def norm(values):
    center = values - row_mean(values)
    inverse = lax.rsqrt(row_mean(center * center) + NORM_EPSILON)
    return center * inverse, inverse


def norm_back(grad, normed, inverse):
    return inverse * (grad - row_mean(grad) - normed * row_mean(grad * normed))


def gelu_both(values):
    gauss_cdf = 0.5 * (1.0 + lax.erf(values * math.sqrt(0.5)))
    density = jnp.exp(values * values * -0.5) * (1.0 / math.sqrt(2.0 * math.pi))
    return values * gauss_cdf, gauss_cdf + values * density


def by_head(values):
    width = values.shape[-1] // HEADS
    lane_head = iota(values.shape, 1) // width
    zero = jnp.zeros_like(values)
    return jnp.concatenate([jnp.where(lane_head == h, values, zero) for h in range(HEADS)], axis=0)


def own_head(stacked):
    cells = stacked.shape[0] // HEADS
    width = stacked.shape[-1] // HEADS
    lane_head = iota((cells, stacked.shape[-1]), 1) // width
    picked = stacked[:cells]
    for h in range(1, HEADS):
        picked = jnp.where(lane_head == h, stacked[h * cells : (h + 1) * cells], picked)
    return picked


def store_windows(field, western, out_ref):
    width = out_ref.shape[1]
    for c in range(HALF_X):
        out_ref[c * CELLS : (c + 1) * CELLS, :] = jnp.concatenate(
            [western(c, z) for z in range(WZ)], axis=0
        )
    own_cols = out_ref.shape[0] // CELLS - HALF_X
    for start in range(0, own_cols, PACKED_COLS):
        count = min(PACKED_COLS, own_cols - start)
        both = jnp.concatenate([field(start, count, z) for z in range(WZ)], axis=1)
        first = (start + HALF_X) * CELLS
        out_ref[first : first + count * CELLS, :] = both.reshape(count * CELLS, width)


def unpack_strip(rows, count):
    return jnp.stack([rows[c * HALF_Y : (c + 1) * HALF_Y] for c in range(count)], axis=0)


def mask_scores(bias, level_wraps, base, band, band_count, crop_ref, row_count):
    crops = [
        crop_ref[lax.rem(band + step + band_count, band_count)] for step in (-1, 0, 1)
    ]
    firsts = [
        (lax.rem(band + step + band_count, band_count) == 0).astype(jnp.int32) for step in (0, 1)
    ]

    def parts(cell):
        z, row = (cell % CELLS) // WY, base + cell % WY
        part = 2 * jnp.where(z == WZ - 1, level_wraps, 0)
        part = part + jnp.where((row >= 0) & (row < HALF_Y), firsts[0], 0)
        part = part + jnp.where((row >= row_count) & (row < row_count + HALF_Y), firsts[1], 0)
        crop = jnp.where(row < 0, crops[0], jnp.where(row < row_count, crops[1], crops[2]))
        return part, (row + row_count) % row_count >= row_count - crop

    key = iota(bias.shape, 0)
    query = iota(bias.shape, 1) % WINDOW
    key_part, key_valid = parts(key)
    query_part, _ = parts(query)
    allowed = (key_part == query_part) & (key_valid | (key == query))
    return jnp.where(allowed, bias, bias + MASKED_SCORE)


GROUPS = 4
TOWARD = (1, 1)


def group_pair(group):
    return group // 2


def field_level(pair, z):
    return lax.rem(WZ * pair + z + WZ // 2, 2 * WZ)


def block_kernel(
    crop_ref, tokens_ref, cotangent_ref, bias_ref, vec_ref, w_qkv_ref, w_proj_ref, w_up_ref, w_down_ref,
    win_ref, rows_back_ref, edge_back_ref, corner_back_ref, grad_ref, small_ref,
    fields_ref, rows_out_ref, rows_in_ref, cols_in_ref, corner_out_ref, corner_in_ref, out_ref,
    score_bias_ref, xw_ref, gw_ref, qkv_ref, prob_ref, att_ref, dqkv_ref, score_sum_ref,
    field_sems, halo_sems, rows_sems, back_sems, edge_sems, corner_sems, out_sems,
):
    width = vec_ref.shape[1]
    hidden_width = w_up_ref.shape[1]
    _, level_count, col_count, row_count, _ = fields_ref.shape
    band_count = crop_ref.shape[0]
    score_scale = (width // HEADS) ** -0.5
    lat, lon = lax.axis_index("lat"), lax.axis_index("lon")
    lat_size, lon_size = lax.axis_size("lat"), lax.axis_size("lon")

    def device(lat_step, lon_step):
        return (
            lax.rem(lat + lat_step + lat_size, lat_size), lax.rem(lon + lon_step + lon_size, lon_size)
        )

    steps = [(0, 1)] + [(t, lon_step) for t in sorted(set(TOWARD)) for lon_step in (0, 1)]
    barrier = pltpu.get_barrier_semaphore()
    for lat_step, lon_step in steps:
        for sign in (1, -1):
            pl.semaphore_signal(
                barrier, inc=1, device_id=device(sign * lat_step, sign * lon_step), device_id_type=MESH
            )

    loads = []
    for level in (1, 2, 3, 0):
        for a, ref in enumerate((tokens_ref, cotangent_ref)):
            loads.append(pltpu.make_async_copy(
                ref.at[level], fields_ref.at[a, level], field_sems.at[len(loads)]
            ))
            loads[-1].start()

    def remote(source, target, sems, lat_step, lon_step):
        return pltpu.make_async_remote_copy(
            src_ref=source, dst_ref=target, send_sem=sems.at[0], recv_sem=sems.at[1],
            device_id=device(lat_step, lon_step), device_id_type=MESH,
        )

    last_cols = fields_ref.at[:, :, pl.ds(col_count - HALF_X, HALF_X)]
    cols_copy = remote(last_cols, cols_in_ref, halo_sems.at[0], 0, 1)
    corner_copies = [
        remote(corner_out_ref.at[pair], corner_in_ref.at[pair], halo_sems.at[1 + pair], TOWARD[pair], 1)
        for pair in range(2)
    ]

    def rows_copy(pair):
        return remote(
            rows_out_ref.at[pair], rows_in_ref.at[pair], rows_sems.at[pair], TOWARD[pair], 0
        )

    def back_copy(pair):
        return remote(
            rows_out_ref.at[pair], rows_back_ref.at[pair], back_sems.at[pair], -TOWARD[pair], 0
        )

    def edge_rows(group):
        return out_ref.at[lax.rem(group, 2), :, pl.ds(0, edge_back_ref.shape[2])]

    def edge_copy(group):
        return remote(edge_rows(group), edge_back_ref.at[group], edge_sems.at[group], 0, -1)

    def corner_back_copy(pair):
        return remote(
            edge_rows(1 + pair), corner_back_ref.at[pair], corner_sems.at[pair], -TOWARD[pair], -1
        )

    def out_copy(group):
        return pltpu.make_async_copy(
            out_ref.at[lax.rem(group, 2)], win_ref.at[:, group], out_sems.at[group]
        )

    for pair in range(2):
        corners = []
        sent = slice(row_count - HALF_Y, row_count) if TOWARD[pair] == 1 else slice(0, HALF_Y)
        for z in range(WZ):
            level = (WZ * pair + z + WZ // 2) % level_count
            for a in range(2):
                if pair == 0:
                    loads[z * 2 + a].wait()
                for start in range(0, col_count, PACKED_COLS):
                    count = min(PACKED_COLS, col_count - start)
                    block = fields_ref[a, level, start : start + count].astype(F32)
                    packed = [block[c, sent] for c in range(count)]
                    rows_out_ref[
                        pair, a, z, start * HALF_Y : (start + count) * HALF_Y, :
                    ] = jnp.concatenate(packed, axis=0).astype(BF16)
                block = fields_ref[a, level, col_count - HALF_X :].astype(F32)
                corners += [block[c, sent] for c in range(HALF_X)]
        spare = corner_out_ref.shape[1] - HALF_Y * len(corners)
        corners.append(jnp.zeros((spare, width), F32))
        corner_out_ref[pair] = jnp.concatenate(corners, axis=0).astype(BF16)
        if pair == 0:
            pl.semaphore_wait(barrier, 2 * len(steps))
            rows_copy(0).start()
            for load in loads[2 * WZ :]:
                load.wait()
            cols_copy.start()

    grad_ref[...] = jnp.zeros_like(grad_ref)
    small_ref[...] = jnp.zeros_like(small_ref)
    score_sum_ref[...] = jnp.zeros_like(score_sum_ref)
    rows = BLOCK_WINDOWS * WINDOW
    shift_one, scale_one, shift_two, scale_two, b_proj, b_down = [
        vec_ref[i : i + 1, :] for i in range(6)
    ]
    qkv_shift = jnp.concatenate([vec_ref[i : i + 1, :] for i in range(6, 9)], axis=1)
    b_up = jnp.concatenate([vec_ref[i : i + 1, :] for i in range(9, 13)], axis=1)

    def add_grad(first, value):
        for j in range(value.shape[1] // width):
            grad_ref[(first + j) * width : (first + j + 1) * width, :] += value[
                :, j * width : (j + 1) * width
            ]

    def column_sums(values):
        return jnp.sum(values, axis=0, keepdims=True)

    def block(index, group):
        slot = lax.rem(group, 2)

        @pl.when((group == 0) & (index == 2))
        def _():
            rows_copy(1).start()
            corner_copies[1].start()

        here = pl.ds(pl.multiple_of(index * rows, 16), rows)
        x32 = xw_ref[here, :]
        x = x32.astype(BF16)
        qkv_ref[...] = (dot_nn(x, w_qkv_ref[...]) + qkv_shift).astype(BF16)
        for w in range(BLOCK_WINDOWS):
            cells = pl.ds(w * WINDOW, WINDOW)
            queries = by_head(qkv_ref[cells, :width] * BF16(score_scale))
            scores = dot_nt(qkv_ref[cells, width : 2 * width], queries) + score_bias_ref[...]
            top = jnp.max(scores, axis=0, keepdims=True)
            exps = jnp.exp(scores - top)
            prob = exps * (1.0 / jnp.sum(exps, axis=0, keepdims=True))
            prob_ref[w] = prob
            att_ref[cells, :] = own_head(
                dot_tn(prob.astype(BF16), qkv_ref[cells, 2 * width :])
            ).astype(BF16)

        att = att_ref[...]
        branch = dot_nn(att, w_proj_ref[...]) + b_proj
        norm_one, inverse_one = norm(branch)
        middle = x32 + norm_one * (1.0 + scale_one) + shift_one
        middle_low = middle.astype(BF16)
        pre = dot_nn(middle_low, w_up_ref[...]) + b_up
        hidden, slope = gelu_both(pre)
        hidden = hidden.astype(BF16)
        second = dot_nn(hidden, w_down_ref[...]) + b_down
        norm_two, inverse_two = norm(second)
        out_ref[slot, 0, here, :] = (middle + norm_two * (1.0 + scale_two) + shift_two).astype(BF16)

        g = gw_ref[here, :]
        second_low = norm_back(g * (1.0 + scale_two), norm_two, inverse_two).astype(BF16)
        pre_grad = dot_nt(second_low, w_down_ref[...]) * slope
        add_grad(8, dot_tn(second_low, hidden))
        pre_low = pre_grad.astype(BF16)
        up_sums = column_sums(pre_grad)
        middle_grad = g + dot_nt(pre_low, w_up_ref[...])
        add_grad(4, dot_tn(middle_low, pre_low))
        branch_low = norm_back(middle_grad * (1.0 + scale_one), norm_one, inverse_one).astype(BF16)
        att_ref[...] = dot_nt(branch_low, w_proj_ref[...]).astype(BF16)
        add_grad(3, dot_tn(att, branch_low))

        for w in range(BLOCK_WINDOWS):
            cells = pl.ds(w * WINDOW, WINDOW)
            queries = by_head(qkv_ref[cells, :width] * BF16(score_scale))
            out_grad = by_head(att_ref[cells, :])
            prob = prob_ref[w]
            prob_grad = dot_nt(qkv_ref[cells, 2 * width :], out_grad)
            score_grad = prob * (prob_grad - jnp.sum(prob_grad * prob, axis=0, keepdims=True))
            score_sum_ref[...] += score_grad
            score_grad = score_grad.astype(BF16)
            dqkv_ref[cells, :width] = (
                own_head(dot_tn(score_grad, qkv_ref[cells, width : 2 * width])) * score_scale
            ).astype(BF16)
            dqkv_ref[cells, width : 2 * width] = dot_nn(score_grad, queries).astype(BF16)
            dqkv_ref[cells, 2 * width :] = dot_nn(prob.astype(BF16), out_grad).astype(BF16)

        dqkv = dqkv_ref[...]
        out_ref[slot, 1, here, :] = (middle_grad + dot_nt(dqkv, w_qkv_ref[...])).astype(BF16)
        add_grad(0, dot_tn(x, dqkv))
        qkv_sums = column_sums(dqkv.astype(F32))
        sums = [
            column_sums(middle_grad), column_sums(middle_grad * norm_one), column_sums(g),
            column_sums(g * norm_two), column_sums(branch_low.astype(F32)),
            column_sums(second_low.astype(F32)),
        ]
        sums += [qkv_sums[:, j * width : (j + 1) * width] for j in range(3)]
        sums += [up_sums[:, j * width : (j + 1) * width] for j in range(hidden_width // width)]
        sums += [jnp.zeros((VECTORS - len(sums), width), F32)]
        small_ref[:VECTORS, :] += jnp.concatenate(sums, axis=0)
        return group

    def gather(pair, group):
        def assemble(own, strip, axis):
            if group in (0, GROUPS - 1):
                return lax.slice_in_dim(own, HALF_Y, HALF_Y + WY, axis=axis)
            if TOWARD[pair] == 1:
                return jnp.concatenate([strip, lax.slice_in_dim(own, 0, HALF_Y, axis=axis)], axis=axis)
            return jnp.concatenate(
                [lax.slice_in_dim(own, row_count - HALF_Y, row_count, axis=axis), strip], axis=axis
            )

        for a, target in enumerate((xw_ref, gw_ref)):
            def field(start, count, z, a=a):
                own = fields_ref[a, field_level(pair, z), start : start + count].astype(F32)
                strip = None
                if group in (1, 2):
                    strip = rows_in_ref[pair, a, z, start * HALF_Y : (start + count) * HALF_Y, :]
                    strip = unpack_strip(strip.astype(F32), count)
                return assemble(own, strip, 1)

            def western(c, z, a=a):
                own = cols_in_ref[a, field_level(pair, z), c].astype(F32)
                strip = None
                if group in (1, 2):
                    place = ((z * 2 + a) * HALF_X + c) * HALF_Y
                    strip = corner_in_ref[pair].astype(F32)[place : place + HALF_Y]
                return assemble(own, strip, 0)

            store_windows(field, western, target)

    def send_back(pair, slot):
        sent = 0 if TOWARD[pair] == 1 else HALF_Y
        for a in range(2):
            for start in range(0, col_count - HALF_X, PACKED_COLS):
                count = min(PACKED_COLS, col_count - HALF_X - start)
                first = (start + HALF_X) * CELLS
                cells = out_ref[slot, a, first : first + count * CELLS, :].astype(F32)
                for z in range(WZ):
                    places = [c * CELLS + z * WY + sent for c in range(count)]
                    rows_out_ref[
                        pair, a, z, start * HALF_Y : (start + count) * HALF_Y, :
                    ] = jnp.concatenate(
                        [cells[p : p + HALF_Y] for p in places], axis=0
                    ).astype(BF16)
        back_copy(pair).start()

    def group_step(group, carry):
        pair, slot = group_pair(group), lax.rem(group, 2)
        inner = (group == 0) | (group == GROUPS - 1)

        @pl.when(group == 0)
        def _():
            corner_copies[0].start()
            cols_copy.wait_recv()

        @pl.when(group >= 2)
        def _():
            out_copy(group - 2).wait()
            edge_copy(group - 2).wait_send()

        @pl.when(group == GROUPS - 1)
        def _():
            corner_back_copy(0).wait_send()

        @pl.when(inner)
        def _():
            gather(pair, 0)

        for straddling in range(2):
            @pl.when(group == 1 + straddling)
            def _():
                rows_copy(straddling).wait_recv()
                corner_copies[straddling].wait_recv()
                gather(straddling, 1 + straddling)

        bases = [-HALF_Y if step == 1 else row_count - HALF_Y for step in TOWARD]
        base = jnp.where(inner, HALF_Y, jnp.where(group == 1, bases[0], bases[1]))
        score_bias_ref[...] = mask_scores(
            bias_ref[...], pair, base, lat, band_count, crop_ref, row_count
        )
        lax.fori_loop(0, col_count // WX // BLOCK_WINDOWS, block, group)
        out_copy(group).start()
        edge_copy(group).start()

        for straddling in range(2):
            @pl.when(group == 1 + straddling)
            def _():
                corner_back_copy(straddling).start()
                rows_copy(straddling).wait_send()
                send_back(straddling, slot)

        return carry

    lax.fori_loop(0, GROUPS, group_step, 0)
    small_ref[VECTORS:, : HEADS * OFFSETS] = table_grad(score_sum_ref)
    for group in (2, 3):
        out_copy(group).wait()
        edge_copy(group).wait_send()
    corner_back_copy(1).wait_send()
    cols_copy.wait_send()
    for copy in corner_copies:
        copy.wait_send()
    for pair in range(2):
        back_copy(pair).wait()
        corner_back_copy(pair).wait_recv()
    for group in range(GROUPS):
        edge_copy(group).wait_recv()


def block_call(crop_rows, tokens, cotangent, constants):
    level_count, col_count, row_count, width = tokens.shape
    vmem = pl.BlockSpec(memory_space=pltpu.VMEM)
    cells = col_count * CELLS
    rows = BLOCK_WINDOWS * WINDOW
    edge = -(-EDGE // 16) * 16
    pairs = level_count // WZ
    strips = (pairs, 2, WZ, packed_rows(col_count), width)
    grad_rows = 4 * width + 2 * constants[4].shape[1]
    sends = pltpu.SemaphoreType.DMA
    return pl.pallas_call(
        block_kernel,
        in_specs=[pl.BlockSpec(memory_space=pltpu.SMEM), ANY, ANY] + [vmem] * len(constants),
        out_specs=[ANY] * 4 + [vmem] * 2,
        out_shape=[
            shape_of((2, GROUPS, cells, width), BF16),
            shape_of(strips, BF16),
            shape_of((GROUPS, 2, edge, width), BF16),
            shape_of((pairs, 2, edge, width), BF16),
            shape_of((grad_rows, width), F32),
            shape_of((VECTORS + TABLE_ROWS, width), F32),
        ],
        scratch_shapes=[
            pltpu.VMEM((2,) + tokens.shape, BF16),
            pltpu.VMEM(strips, BF16),
            pltpu.VMEM(strips, BF16),
            pltpu.VMEM((2, level_count, HALF_X, row_count, width), BF16),
            pltpu.VMEM((pairs, edge, width), BF16),
            pltpu.VMEM((pairs, edge, width), BF16),
            pltpu.VMEM((2, 2, cells, width), BF16),
            pltpu.VMEM((WINDOW, SCORES), F32),
            pltpu.VMEM((cells, width), F32),
            pltpu.VMEM((cells, width), F32),
            pltpu.VMEM((rows, 3 * width), BF16),
            pltpu.VMEM((BLOCK_WINDOWS, WINDOW, SCORES), F32),
            pltpu.VMEM((rows, width), BF16),
            pltpu.VMEM((rows, 3 * width), BF16),
            pltpu.VMEM((WINDOW, SCORES), F32),
            sends((2 * level_count,)), sends((3, 2)), sends((pairs, 2)), sends((pairs, 2)),
            sends((GROUPS, 2)), sends((pairs, 2)), sends((GROUPS,)),
        ],
        cost_estimate=pl.CostEstimate(
            flops=GROUPS * cells * 5_200_000, bytes_accessed=32 * 2**20, transcendentals=0
        ),
        compiler_params=pltpu.CompilerParams(
            collective_id=1, has_side_effects=True, vmem_limit_bytes=VMEM_LIMIT
        ),
    )(crop_rows, tokens, cotangent, *constants)


def halved(rows, count):
    sizes = [rows >> (i + 1) for i in range(count)]
    return sizes, [sum(sizes[:i]) for i in range(count + 1)]


def sum_kernel(
    bits, halvings, parts, grad_ref, small_ref, out_ref, small_out_ref,
    acc_ref, send_ref, recv_ref, more_ref, small_recv_ref, sems, small_sems,
):
    axes = ("lat", "lon")
    places = {axis: lax.axis_index(axis) for axis in axes}
    own_bit, partner = {}, {}
    for axis, bit in bits:
        value = (places[axis] // 2**bit) % 2
        own_bit[axis, bit] = value
        moved = dict(places)
        moved[axis] = places[axis] + 2**bit * (1 - 2 * value)
        partner[axis, bit] = tuple(moved[name] for name in axes)

    barrier = pltpu.get_barrier_semaphore()
    for bit in bits:
        pl.semaphore_signal(barrier, inc=1, device_id=partner[bit], device_id_type=MESH)
    pl.semaphore_wait(barrier, len(bits))

    def send(source, target, pair, bit):
        copy = pltpu.make_async_remote_copy(
            src_ref=source, dst_ref=target, send_sem=pair.at[0], recv_sem=pair.at[1],
            device_id=partner[bit], device_id_type=MESH,
        )
        copy.start()
        return copy

    part_rows = grad_ref.shape[0] // parts
    sizes, starts = halved(part_rows, halvings)
    shard = sizes[-1]
    orders = []
    for p in range(parts):
        order = list(bits[:halvings])
        if p == 1 and halvings > 2:
            order[1], order[2] = order[2], order[1]
        orders.append(order)
    low = [p * part_rows for p in range(parts)]
    small_out_ref[...] = small_ref[...]
    acc_ref[...] = grad_ref[...]

    def halve(p, s):
        bit, size = orders[p][s], sizes[s]
        place = pl.ds(p * starts[-1] + starts[s], size)
        away = pl.multiple_of(low[p] + (1 - own_bit[bit]) * size, 16)
        send_ref[place, :] = acc_ref[pl.ds(away, size), :].astype(BF16)
        low[p] = low[p] + own_bit[bit] * size
        return send(send_ref.at[place], recv_ref.at[place], sems.at[p, s], bit)

    def add_half(p, s, copy):
        size = sizes[s]
        copy.wait()
        place = pl.ds(p * starts[-1] + starts[s], size)
        here = pl.ds(pl.multiple_of(low[p], 16), size)
        acc_ref[here, :] += recv_ref[place, :].astype(F32)

    copies = [halve(p, 0) for p in range(parts)]
    for s, bit in enumerate(bits):
        small_copy = send(small_out_ref, small_recv_ref.at[s], small_sems.at[s], bit)
        if s < halvings:
            for p in range(parts):
                add_half(p, s, copies[p])
                if s + 1 < halvings:
                    copies[p] = halve(p, s + 1)
        small_copy.wait()
        small_out_ref[...] += small_recv_ref[s]

    for p in range(parts):
        here = pl.ds(pl.multiple_of(low[p], 16), shard)
        out_ref[here, :] = acc_ref[here, :].astype(BF16)
        for s in range(halvings, len(bits)):
            mine = more_ref.at[0, p, s - halvings]
            theirs = more_ref.at[1, p, s - halvings]
            mine[...] = out_ref[here, :]
            send(mine, theirs, sems.at[p, s], bits[s]).wait()
            out_ref[here, :] = (mine[...].astype(F32) + theirs[...].astype(F32)).astype(BF16)

    def give(p, s):
        here = out_ref.at[pl.ds(pl.multiple_of(low[p], 16), sizes[s]), :]
        low[p] = low[p] - own_bit[orders[p][s]] * sizes[s]
        return send(here, here, sems.at[p, len(bits) + s], orders[p][s])

    copies = [give(p, halvings - 1) for p in range(parts)]
    for s in reversed(range(halvings)):
        for p in range(parts):
            copies[p].wait()
            if s:
                copies[p] = give(p, s - 1)


def sum_over_devices(grad, small):
    bits = [("lon", 0), ("lon", 1), ("lat", 0), ("lat", 1), ("lat", 2)]
    bits = [b for b in bits if 2 ** b[1] < lax.axis_size(b[0])]
    bits += [("lat", b) for b in range(3, lax.axis_size("lat").bit_length() - 1)]
    bits += [("lon", b) for b in range(2, lax.axis_size("lon").bit_length() - 1)]
    if not bits:
        return grad.astype(BF16), small
    halvings, parts = min(5, len(bits)), 2
    rows, width = grad.shape
    sizes, starts = halved(rows // parts, halvings)
    more = max(1, len(bits) - halvings)
    vmem = pl.BlockSpec(memory_space=pltpu.VMEM)
    return pl.pallas_call(
        functools.partial(sum_kernel, tuple(bits), halvings, parts),
        in_specs=[vmem, vmem],
        out_specs=[vmem, vmem],
        out_shape=[shape_of(grad.shape, BF16), shape_of(small.shape, F32)],
        scratch_shapes=[
            pltpu.VMEM(grad.shape, F32),
            pltpu.VMEM((parts * starts[-1], width), BF16),
            pltpu.VMEM((parts * starts[-1], width), BF16),
            pltpu.VMEM((2, parts, more, sizes[-1], width), BF16),
            pltpu.VMEM((len(bits),) + small.shape, F32),
            pltpu.SemaphoreType.DMA((parts, len(bits) + halvings, 2)),
            pltpu.SemaphoreType.DMA((len(bits), 2)),
        ],
        compiler_params=pltpu.CompilerParams(
            collective_id=0, has_side_effects=True, vmem_limit_bytes=VMEM_LIMIT
        ),
    )(grad, small)


def merge_kernel(
    inner_ref, straddle_ref, rows_ref, inner_edge_ref, straddle_edge_ref, corner_ref,
    grad_ref, small_ref, context_ref, *out_refs,
):
    fields, grads = out_refs[:2], out_refs[2:]
    _, col_count, row_count, width = fields[0].shape
    step = pl.program_id(0)

    def piece(rows_of, a, first_col, count, first, size):
        block = rows_of(a)[first_col * CELLS : (first_col + count) * CELLS, :].astype(F32)
        return block.reshape(count, CELLS, width)[:, first : first + size]

    straddle, inner = lambda a: straddle_ref.at[a, 0], lambda a: inner_ref.at[a, 0]
    straddle_edge, inner_edge, corner = (
        lambda a, ref=ref: ref.at[0, a] for ref in (straddle_edge_ref, inner_edge_ref, corner_ref)
    )
    for pair, z in ((0, 0), (0, 1), (1, 0), (1, 1)):
        @pl.when(step == pair * WZ + z)
        def _():
            first = z * WY
            kept, sent = (HALF_Y, 0) if TOWARD[pair] == 1 else (0, HALF_Y)

            def in_order(own, inner_rows, back):
                parts = [own, inner_rows, back] if TOWARD[pair] == 1 else [back, inner_rows, own]
                return jnp.concatenate(parts, axis=1).astype(BF16)

            for a, field in enumerate(fields):
                for start in range(0, col_count - HALF_X, PACKED_COLS):
                    count = min(PACKED_COLS, col_count - HALF_X - start)
                    strip = rows_ref[0, a, 0, start * HALF_Y : (start + count) * HALF_Y, :]
                    field[0, start : start + count] = in_order(
                        piece(straddle, a, start + HALF_X, count, first + kept, HALF_Y),
                        piece(inner, a, start + HALF_X, count, first, WY),
                        unpack_strip(strip.astype(F32), count),
                    )
                field[0, col_count - HALF_X :] = in_order(
                    piece(straddle_edge, a, 0, HALF_X, first + kept, HALF_Y),
                    piece(inner_edge, a, 0, HALF_X, first, WY),
                    piece(corner, a, 0, HALF_X, first + sent, HALF_Y),
                )

    grad_qkv, grad_proj, grad_up, grad_down, grad_mod, *vectors = grads

    def slab(index):
        return grad_ref[index * width : (index + 1) * width, :].astype(F32)

    @pl.when(step == 0)
    def _():
        for j in range(3):
            grad_qkv[:, j * width : (j + 1) * width] = slab(j)
        grad_proj[...] = slab(3)

    @pl.when(step == 1)
    def _():
        for j in range(grad_up.shape[1] // width):
            grad_up[:, j * width : (j + 1) * width] = slab(4 + j)

    @pl.when(step == 2)
    def _():
        for j in range(grad_down.shape[0] // width):
            grad_down[j * width : (j + 1) * width, :] = slab(8 + j).T

    @pl.when(step == 3)
    def _():
        lanes = context_ref.shape[1]
        for part in range(4):
            row = small_ref[part : part + 1, :]
            for j in range(0, width, lanes):
                grad_mod[:, part * width + j : part * width + j + lanes] = (
                    context_ref[...] * row[:, j : j + lanes]
                )
        mod_bias, proj_bias, down_bias, q_bias, v_bias, up_bias = vectors
        mod_bias[...] = jnp.concatenate([small_ref[i : i + 1, :] for i in range(4)], axis=1)
        up_bias[...] = jnp.concatenate([small_ref[i : i + 1, :] for i in range(9, 13)], axis=1)
        for ref, i in ((proj_bias, 4), (down_bias, 5), (q_bias, 6), (v_bias, 8)):
            ref[...] = small_ref[i : i + 1, :]


def merge(field_shape, hidden_width, windows, rows_back, edge_back, corner_back, grad, small, context):
    level_count, col_count, row_count, width = field_shape

    def level_of(i):
        return (i + WZ // 2) % level_count

    def group_of(pair, straddles):
        return 1 + pair if straddles else (GROUPS - 1) * pair

    def windows_of(straddles):
        return pl.BlockSpec(
            (2, 1) + windows.shape[2:], lambda i: (0, group_of(i // WZ, straddles), 0, 0)
        )

    def edge_of(straddles):
        return pl.BlockSpec(
            (1,) + edge_back.shape[1:], lambda i: (group_of(i // WZ, straddles), 0, 0, 0)
        )

    shapes = [
        (width, 3 * width), (width, width), (width, hidden_width), (hidden_width, width),
        (width, 4 * width), (1, 4 * width), (1, width), (1, width), (1, width), (1, width),
        (1, hidden_width),
    ]
    field = pl.BlockSpec((1,) + field_shape[1:], lambda i: (level_of(i), 0, 0, 0))
    return pl.pallas_call(
        merge_kernel,
        grid=(level_count,),
        in_specs=[
            windows_of(False), windows_of(True),
            pl.BlockSpec((1, 2, 1) + rows_back.shape[3:], lambda i: (i // WZ, 0, i % WZ, 0, 0)),
            edge_of(False), edge_of(True),
            pl.BlockSpec((1,) + corner_back.shape[1:], lambda i: (i // WZ, 0, 0, 0)),
        ] + [whole(v.shape) for v in (grad, small, context)],
        out_specs=[field, field] + [whole(s) for s in shapes],
        out_shape=[shape_of(field_shape, BF16)] * 2 + [shape_of(s, F32) for s in shapes],
        compiler_params=pltpu.CompilerParams(vmem_limit_bytes=VMEM_LIMIT),
    )(windows, windows, rows_back, edge_back, edge_back, corner_back, grad, small, context)


def on_device(
    tokens, cotangent, w_qkv, q_bias, v_bias, w_proj, b_proj, w_up, b_up, w_down, b_down,
    w_mod, b_mod, rel_table, crop_rows, lead_hours,
):
    fields = [field.transpose(0, 2, 1, 3) for field in (tokens, cotangent)]
    table = rel_table.transpose(1, 3, 0, 2).reshape(HEADS * OFFSETS, 2 * WY - 1)
    nothing = jnp.zeros_like(q_bias)
    vectors = jnp.concatenate(
        [b_mod, b_proj, b_down, q_bias, nothing, v_bias, b_up] + [nothing] * 3
    ).reshape(VECTORS, -1)
    bias, vecs, context = set_up(lead_hours, w_mod, vectors, table)
    constants = [bias, vecs, w_qkv, w_proj, w_up, w_down]
    windows, rows_back, edge_back, corner_back, grad, small = block_call(
        crop_rows, *fields, constants
    )
    grad, small = sum_over_devices(grad, small)
    (
        mixed, token_grad, grad_qkv, grad_proj, grad_up, grad_down, grad_mod, grad_mod_bias,
        grad_proj_bias, grad_down_bias, grad_q_bias, grad_v_bias, grad_up_bias,
    ) = merge(
        fields[0].shape, w_up.shape[1], windows, rows_back, edge_back, corner_back, grad, small, context
    )
    table_sum = small[VECTORS : VECTORS + 2 * WY - 1, : HEADS * OFFSETS][::-1]
    grad_table = table_sum.reshape(2 * WY - 1, 2 * WZ - 1, 2 * WX - 1, HEADS).transpose(3, 1, 0, 2)
    return (
        mixed.transpose(0, 2, 1, 3),
        token_grad.transpose(0, 2, 1, 3),
        grad_qkv,
        grad_q_bias[0],
        grad_v_bias[0],
        grad_proj,
        grad_proj_bias[0],
        grad_up,
        grad_up_bias[0],
        grad_down,
        grad_down_bias[0],
        grad_mod,
        grad_mod_bias[0],
        grad_table,
    )


def solution(mesh):
    split = P(None, "lat", "lon", None)
    return jax.shard_map(
        on_device,
        mesh=mesh,
        in_specs=(split, split) + (P(),) * 14,
        out_specs=(split, split) + (P(),) * 12,
        check_vma=False,
    )
```

```python
import functools
import math

import jax
import jax.numpy as jnp
from jax import lax
from jax.experimental import pallas as pl
from jax.experimental.pallas import tpu as pltpu
from jax.sharding import PartitionSpec as P

WZ = 2
WY = 12
WX = 6
CELLS = WZ * WY
WINDOW = CELLS * WX
HEADS = 4
SCORES = HEADS * WINDOW
HALF_Y = WY // 2
HALF_X = WX // 2
BLOCK_WINDOWS = 5
OFFSETS = (2 * WZ - 1) * (2 * WX - 1)
VECTORS = 16
LANES = 128
TABLE_ROWS = 2 * WY
EDGE = HALF_X * CELLS
PACKED_COLS = 8

NORM_EPSILON = 1e-05
MASKED_SCORE = -1000000000.0
F32 = jnp.float32
BF16 = jnp.bfloat16
MESH = pl.DeviceIdType.MESH
ANY = pl.BlockSpec(memory_space=pl.ANY)
VMEM_LIMIT = 60 * 2**20


def dot_nn(left, right):
    return lax.dot_general(left, right, (((1,), (0,)), ((), ())), preferred_element_type=F32)


def dot_nt(left, right):
    return lax.dot_general(left, right, (((1,), (1,)), ((), ())), preferred_element_type=F32)


def dot_tn(left, right):
    return lax.dot_general(left, right, (((0,), (0,)), ((), ())), preferred_element_type=F32)


def iota(shape, axis):
    return lax.broadcasted_iota(jnp.int32, shape, axis)


def whole(shape, buffers=1):
    return pl.BlockSpec(
        shape, lambda *_: (0,) * len(shape), pipeline_mode=pl.Buffered(buffers)
    )


def shape_of(shape, dtype):
    return jax.ShapeDtypeStruct(shape, dtype)


def packed_rows(col_count):
    return -(-col_count * HALF_Y // 16) * 16


def offset_pick(key_x, key_z):
    lane = iota((HEADS * OFFSETS, SCORES), 1)
    head, rest = lane // WINDOW, lane % WINDOW
    query_x, query_z = rest // CELLS, (rest % CELLS) // WY
    offset_z, offset_x = query_z - key_z + WZ - 1, query_x - key_x + WX - 1
    place = (offset_z * (2 * WX - 1) + offset_x) * HEADS + head
    return iota((HEADS * OFFSETS, SCORES), 0) == place


def setup_kernel(
    lead_ref, w_mod_ref, b_mod_ref, b_proj_ref, b_down_ref, q_bias_ref, v_bias_ref, b_up_ref,
    table_ref, bias_ref, vec_ref, context_ref,
):
    width = w_mod_ref.shape[0]
    half = width // 2
    lanes = context_ref.shape[1]
    fraction = iota((half, lanes), 0).astype(F32) / half
    angles = lead_ref[0].astype(F32) * jnp.exp(-math.log(1000.0) * fraction)
    waves = jnp.concatenate([jnp.sin(angles), jnp.cos(angles)], axis=0)
    context = waves * (1.0 / (1.0 + jnp.exp(-waves)))
    context_ref[...] = context
    for part in range(4):
        pieces = []
        for j in range(width // lanes):
            start = part * width + j * lanes
            pieces.append(
                jnp.sum(context * w_mod_ref[:, start : start + lanes].astype(F32), axis=0, keepdims=True)
            )
        vec_ref[part : part + 1, :] = (
            jnp.concatenate(pieces, axis=1)
            + b_mod_ref[part * width : (part + 1) * width].astype(F32)[None]
        )
    vec_ref[4:, :] = jnp.zeros((VECTORS - 4, width), F32)
    for i, ref in ((4, b_proj_ref), (5, b_down_ref), (6, q_bias_ref), (8, v_bias_ref)):
        vec_ref[i : i + 1, :] = ref[...].astype(F32)[None]
    for j in range(b_up_ref.shape[0] // width):
        vec_ref[9 + j : 10 + j, :] = b_up_ref[j * width : (j + 1) * width].astype(F32)[None]

    offsets_y = 2 * WY - 1
    backwards = iota((TABLE_ROWS, offsets_y), 0) + iota((TABLE_ROWS, offsets_y), 1) == offsets_y - 1
    table = jnp.concatenate(
        [table_ref[z, x].astype(F32) for z in range(2 * WZ - 1) for x in range(2 * WX - 1)], axis=0
    ).astype(BF16)
    table = dot_nt(backwards.astype(BF16), table).astype(BF16)
    query_y = iota((WY, SCORES), 1) % WY
    for key_x in range(WX):
        for key_z in range(WZ):
            spread = dot_nn(table, offset_pick(key_x, key_z).astype(BF16))
            rows = spread[WY - 1 : 2 * WY - 1]
            for y in range(1, WY):
                rows = jnp.where(query_y == y, spread[WY - 1 - y : 2 * WY - 1 - y], rows)
            start = key_x * CELLS + key_z * WY
            bias_ref[start : start + WY, :] = rows


def set_up(lead_hours, w_mod, vectors, table):
    width = w_mod.shape[0]
    vmem = pl.BlockSpec(memory_space=pltpu.VMEM)
    return pl.pallas_call(
        setup_kernel,
        in_specs=[pl.BlockSpec(memory_space=pltpu.SMEM)] + [vmem] * (2 + len(vectors)),
        out_specs=[vmem] * 3,
        out_shape=[
            shape_of((WINDOW, SCORES), F32),
            shape_of((VECTORS, width), F32),
            shape_of((width, 128), F32),
        ],
        compiler_params=pltpu.CompilerParams(vmem_limit_bytes=VMEM_LIMIT),
    )(lead_hours, w_mod, *vectors, table)


def table_grad(score_sum_ref):
    query_y = iota((WY, SCORES), 1) % WY
    total = jnp.zeros((TABLE_ROWS, HEADS * OFFSETS), F32)
    for key_x in range(WX):
        for key_z in range(WZ):
            start = key_x * CELLS + key_z * WY
            rows = score_sum_ref[start : start + WY, :]
            spread = jnp.zeros((TABLE_ROWS, SCORES), F32)
            for y in range(WY):
                own = jnp.where(query_y == y, rows, 0.0)
                pads = (WY - 1 - y, TABLE_ROWS - (2 * WY - 1 - y))
                parts = [jnp.zeros((p, SCORES), F32) for p in pads]
                spread = spread + jnp.concatenate(
                    ([parts[0]] if pads[0] else []) + [own, parts[1]], axis=0
                )
            pick = offset_pick(key_x, key_z).astype(BF16)
            high = spread.astype(BF16)
            low = (spread - high.astype(F32)).astype(BF16)
            total = total + dot_nt(high, pick) + dot_nt(low, pick)
    return total


def halved(rows, count):
    sizes = [rows >> (i + 1) for i in range(count)]
    return sizes, [sum(sizes[:i]) for i in range(count + 1)]


def sum_bits():
    bits = [("lon", 0), ("lon", 1), ("lat", 0), ("lat", 1), ("lat", 2)]
    bits = [b for b in bits if 2 ** b[1] < lax.axis_size(b[0])]
    bits += [("lat", b) for b in range(3, lax.axis_size("lat").bit_length() - 1)]
    bits += [("lon", b) for b in range(2, lax.axis_size("lon").bit_length() - 1)]
    return bits, min(5, len(bits))


def peer_sizes():
    lons, lats = lax.axis_size("lon") // 2, min(8, lax.axis_size("lat"))
    return lons, lats, lons * lats


def sum_parts(width, hidden_width):
    qkv_rows = 3 * width * (width // LANES)
    rest = (width + 2 * hidden_width) * (width // LANES)
    first = -(-rest // 1024) * 512
    return [(qkv_rows, first), (qkv_rows + first, rest - first), (0, qkv_rows)]


def row_mean(values):
    return jnp.mean(values, axis=-1, keepdims=True)


def norm(values):
    center = values - row_mean(values)
    inverse = lax.rsqrt(row_mean(center * center) + NORM_EPSILON)
    return center * inverse, inverse


def norm_back(grad, normed, inverse):
    return inverse * (grad - row_mean(grad) - normed * row_mean(grad * normed))


def gelu_both(values):
    gauss_cdf = 0.5 * (1.0 + lax.erf(values * math.sqrt(0.5)))
    density = jnp.exp(values * values * -0.5) * (1.0 / math.sqrt(2.0 * math.pi))
    return values * gauss_cdf, gauss_cdf + values * density


def by_head(values):
    width = values.shape[-1] // HEADS
    lane_head = iota(values.shape, 1) // width
    zero = jnp.zeros_like(values)
    return jnp.concatenate([jnp.where(lane_head == h, values, zero) for h in range(HEADS)], axis=0)


def own_head(stacked):
    cells = stacked.shape[0] // HEADS
    width = stacked.shape[-1] // HEADS
    lane_head = iota((cells, stacked.shape[-1]), 1) // width
    picked = stacked[:cells]
    for h in range(1, HEADS):
        picked = jnp.where(lane_head == h, stacked[h * cells : (h + 1) * cells], picked)
    return picked


def store_windows(field, western, out_ref):
    width = out_ref.shape[1]
    for c in range(HALF_X):
        out_ref[c * CELLS : (c + 1) * CELLS, :] = jnp.concatenate(
            [western(c, z) for z in range(WZ)], axis=0
        )
    own_cols = out_ref.shape[0] // CELLS - HALF_X
    for start in range(0, own_cols, PACKED_COLS):
        count = min(PACKED_COLS, own_cols - start)
        both = jnp.concatenate([field(start, count, z) for z in range(WZ)], axis=1)
        first = (start + HALF_X) * CELLS
        out_ref[first : first + count * CELLS, :] = both.reshape(count * CELLS, width)


def unpack_strip(rows, count):
    return jnp.stack([rows[c * HALF_Y : (c + 1) * HALF_Y] for c in range(count)], axis=0)


def mask_scores(bias, level_wraps, base, band, band_count, crop_ref, row_count):
    crops = [
        crop_ref[lax.rem(band + step + band_count, band_count)] for step in (-1, 0, 1)
    ]
    firsts = [
        (lax.rem(band + step + band_count, band_count) == 0).astype(jnp.int32) for step in (0, 1)
    ]

    def parts(cell):
        z, row = (cell % CELLS) // WY, base + cell % WY
        part = 2 * jnp.where(z == WZ - 1, level_wraps, 0)
        part = part + jnp.where((row >= 0) & (row < HALF_Y), firsts[0], 0)
        part = part + jnp.where((row >= row_count) & (row < row_count + HALF_Y), firsts[1], 0)
        crop = jnp.where(row < 0, crops[0], jnp.where(row < row_count, crops[1], crops[2]))
        return part, (row + row_count) % row_count >= row_count - crop

    key = iota(bias.shape, 0)
    query = iota(bias.shape, 1) % WINDOW
    key_part, key_valid = parts(key)
    query_part, _ = parts(query)
    allowed = (key_part == query_part) & (key_valid | (key == query))
    return jnp.where(allowed, bias, bias + MASKED_SCORE)


GROUPS = 4
TOWARD = (1, 1)


def group_pair(group):
    return group // 2


def field_level(pair, z):
    return lax.rem(WZ * pair + z + WZ // 2, 2 * WZ)


def block_kernel(
    crop_ref, tokens_ref, cotangent_ref, bias_ref, vec_ref, w_qkv_ref, w_proj_ref, w_up_ref, w_down_ref,
    win_ref, rows_back_ref, edge_back_ref, corner_back_ref, sum_ref, small_ref,
    grad_ref, send_ref, recv_ref, more_ref, small_recv_ref, scatter_ref, pieces_ref, fields_ref, rows_out_ref, rows_in_ref, cols_in_ref, corner_out_ref, corner_in_ref, out_ref,
    score_bias_ref, xw_ref, gw_ref, qkv_ref, prob_ref, att_ref, middle_grad_ref, dqkv_ref,
    score_sum_ref,
    field_sems, halo_sems, rows_sems, back_sems, edge_sems, corner_sems, out_sems, sum_sems, small_sems,
    peer_sems,
):
    width = vec_ref.shape[1]
    hidden_width = w_up_ref.shape[1]
    _, level_count, col_count, row_count, _ = fields_ref.shape
    band_count = crop_ref.shape[0]
    score_scale = (width // HEADS) ** -0.5
    lat, lon = lax.axis_index("lat"), lax.axis_index("lon")
    lat_size, lon_size = lax.axis_size("lat"), lax.axis_size("lon")

    def device(lat_step, lon_step):
        return (
            lax.rem(lat + lat_step + lat_size, lat_size), lax.rem(lon + lon_step + lon_size, lon_size)
        )

    steps = [(0, 1)] + [(t, lon_step) for t in sorted(set(TOWARD)) for lon_step in (0, 1)]
    barrier = pltpu.get_barrier_semaphore()
    for lat_step, lon_step in steps:
        for sign in (1, -1):
            pl.semaphore_signal(
                barrier, inc=1, device_id=device(sign * lat_step, sign * lon_step), device_id_type=MESH
            )

    bits, halvings = sum_bits()
    own_bit, partner = {}, {}
    for axis, bit in bits:
        place = lat if axis == "lat" else lon
        own_bit[axis, bit] = (place // 2**bit) % 2
        moved = place + 2**bit * (1 - 2 * own_bit[axis, bit])
        partner[axis, bit] = (moved, lon) if axis == "lat" else (lat, moved)
        pl.semaphore_signal(barrier, inc=1, device_id=partner[axis, bit], device_id_type=MESH)
    peer_lons, peer_lats, peer_count = peer_sizes()
    my_peer = lon // 2 + peer_lons * (lat % peer_lats)

    def peer(step):
        index = (my_peer + step) % peer_count
        return index, (
            (lat // peer_lats) * peer_lats + index // peer_lons, 2 * (index % peer_lons) + lon % 2
        )

    for step in range(1, peer_count):
        pl.semaphore_signal(barrier, inc=1, device_id=peer(step)[1], device_id_type=MESH)

    loads = []
    for level in (1, 2, 3, 0):
        for a, ref in enumerate((tokens_ref, cotangent_ref)):
            loads.append(pltpu.make_async_copy(
                ref.at[level], fields_ref.at[a, level], field_sems.at[len(loads)]
            ))
            loads[-1].start()

    def remote(source, target, sems, lat_step, lon_step):
        return pltpu.make_async_remote_copy(
            src_ref=source, dst_ref=target, send_sem=sems.at[0], recv_sem=sems.at[1],
            device_id=device(lat_step, lon_step), device_id_type=MESH,
        )

    last_cols = fields_ref.at[:, :, pl.ds(col_count - HALF_X, HALF_X)]
    cols_copy = remote(last_cols, cols_in_ref, halo_sems.at[0], 0, 1)
    corner_copies = [
        remote(corner_out_ref.at[pair], corner_in_ref.at[pair], halo_sems.at[1 + pair], TOWARD[pair], 1)
        for pair in range(2)
    ]

    def rows_copy(pair):
        return remote(
            rows_out_ref.at[pair], rows_in_ref.at[pair], rows_sems.at[pair], TOWARD[pair], 0
        )

    def back_copy(pair):
        return remote(
            rows_out_ref.at[pair], rows_back_ref.at[pair], back_sems.at[pair], -TOWARD[pair], 0
        )

    def edge_rows(group):
        return out_ref.at[lax.rem(group, 2), :, pl.ds(0, edge_back_ref.shape[2])]

    def edge_copy(group):
        return remote(edge_rows(group), edge_back_ref.at[group], edge_sems.at[group], 0, -1)

    def corner_back_copy(pair):
        return remote(
            edge_rows(1 + pair), corner_back_ref.at[pair], corner_sems.at[pair], -TOWARD[pair], -1
        )

    def out_copy(group):
        return pltpu.make_async_copy(
            out_ref.at[lax.rem(group, 2)], win_ref.at[:, group], out_sems.at[group]
        )

    for pair in range(2):
        corners = []
        sent = slice(row_count - HALF_Y, row_count) if TOWARD[pair] == 1 else slice(0, HALF_Y)
        for z in range(WZ):
            level = (WZ * pair + z + WZ // 2) % level_count
            for a in range(2):
                if pair == 0:
                    loads[z * 2 + a].wait()
                for start in range(0, col_count, PACKED_COLS):
                    count = min(PACKED_COLS, col_count - start)
                    block = fields_ref[a, level, start : start + count].astype(F32)
                    packed = [block[c, sent] for c in range(count)]
                    rows_out_ref[
                        pair, a, z, start * HALF_Y : (start + count) * HALF_Y, :
                    ] = jnp.concatenate(packed, axis=0).astype(BF16)
                block = fields_ref[a, level, col_count - HALF_X :].astype(F32)
                corners += [block[c, sent] for c in range(HALF_X)]
        spare = corner_out_ref.shape[1] - HALF_Y * len(corners)
        corners.append(jnp.zeros((spare, width), F32))
        corner_out_ref[pair] = jnp.concatenate(corners, axis=0).astype(BF16)
        if pair == 0:
            pl.semaphore_wait(barrier, 2 * len(steps) + len(bits) + peer_count - 1)
            rows_copy(0).start()
            for load in loads[2 * WZ :]:
                load.wait()
            cols_copy.start()

    grad_ref[...] = jnp.zeros_like(grad_ref)
    small_ref[...] = jnp.zeros_like(small_ref)
    score_sum_ref[...] = jnp.zeros_like(score_sum_ref)
    rows = BLOCK_WINDOWS * WINDOW
    shift_one, scale_one, shift_two, scale_two, b_proj, b_down = [
        vec_ref[i : i + 1, :] for i in range(6)
    ]
    qkv_shift = jnp.concatenate([vec_ref[i : i + 1, :] for i in range(6, 9)], axis=1)
    b_up = jnp.concatenate([vec_ref[i : i + 1, :] for i in range(9, 13)], axis=1)

    def add_grad(first, value):
        for j in range(value.shape[1] // LANES):
            grad_ref[(first + j) * width : (first + j + 1) * width, :] += value[
                :, j * LANES : (j + 1) * LANES
            ]

    parts = sum_parts(width, hidden_width)
    sizes, send_starts = zip(*[halved(count, halvings) for _, count in parts])
    orders, lows = [], []
    for p, (first, _) in enumerate(parts):
        order = list(bits[:halvings])
        if p == 1 and halvings > 2:
            order[1], order[2] = order[2], order[1]
        orders.append(order)
        lows.append([first])
        for s, bit in enumerate(order):
            lows[p].append(lows[p][s] + own_bit[bit] * sizes[p][s])

    def to_partner(source, target, sems, bit):
        return pltpu.make_async_remote_copy(
            src_ref=source, dst_ref=target, send_sem=sems.at[0], recv_sem=sems.at[1],
            device_id=partner[bit], device_id_type=MESH,
        )

    def half_place(p, s):
        return pl.ds(sum(starts[-1] for starts in send_starts[:p]) + send_starts[p][s], sizes[p][s])

    def half_copy(p, s):
        place = half_place(p, s)
        return to_partner(send_ref.at[place], recv_ref.at[place], sum_sems.at[p, s], orders[p][s])

    def halve(p, s):
        size, bit = sizes[p][s], orders[p][s]
        away = pl.multiple_of(lows[p][s] + (1 - own_bit[bit]) * size, 16)
        send_ref[half_place(p, s), :] = grad_ref[pl.ds(away, size), :].astype(BF16)
        half_copy(p, s).start()

    def add_half(p, s):
        half_copy(p, s).wait()
        here = pl.ds(pl.multiple_of(lows[p][s + 1], 16), sizes[p][s])
        grad_ref[here, :] += recv_ref[half_place(p, s), :].astype(F32)

    def shard_done(p):
        here = pl.ds(pl.multiple_of(lows[p][halvings], 16), sizes[p][-1])
        sum_ref[here, :] = grad_ref[here, :].astype(BF16)
        exchange_shard(p, here, sizes[p][-1])

    def exchange_shard(p, here, count):
        for s in range(halvings, len(bits)):
            mine = more_ref.at[0, p, s - halvings, pl.ds(0, count)]
            theirs = more_ref.at[1, p, s - halvings, pl.ds(0, count)]
            mine[...] = sum_ref[here, :]
            copy = to_partner(mine, theirs, sum_sems.at[p, s], bits[s])
            copy.start()
            copy.wait()
            sum_ref[here, :] = (mine[...].astype(F32) + theirs[...].astype(F32)).astype(BF16)

    def give_copy(p, s):
        here = sum_ref.at[pl.ds(pl.multiple_of(lows[p][s + 1], 16), sizes[p][s]), :]
        return to_partner(here, here, sum_sems.at[p, len(bits) + s], orders[p][s])

    def sum_step(p, k):
        if 1 <= k <= halvings:
            add_half(p, k - 1)
        if k < halvings:
            halve(p, k)
        if k == halvings:
            shard_done(p)
        if halvings < k <= 2 * halvings:
            give_copy(p, 2 * halvings - k).wait()
        if halvings <= k < 2 * halvings:
            give_copy(p, 2 * halvings - 1 - k).start()

    early, late = (0, 1), 2
    hidden_steps = min(4, halvings)

    piece = sizes[late][0] // peer_count

    def piece_place(index):
        return pl.ds(pl.multiple_of(lows[late][1] + index * piece, 16), piece)

    def scatter_copy(step):
        index, there = peer(step)
        return pltpu.make_async_remote_copy(
            src_ref=scatter_ref.at[pl.ds(pl.multiple_of(index * piece, 16), piece), :],
            dst_ref=pieces_ref.at[step], send_sem=peer_sems.at[0, step, 0],
            recv_sem=peer_sems.at[0, step, 1], device_id=there, device_id_type=MESH,
        )

    def gather_copy(step):
        mine = sum_ref.at[piece_place(my_peer), :]
        return pltpu.make_async_remote_copy(
            src_ref=mine, dst_ref=mine, send_sem=peer_sems.at[1, step, 0],
            recv_sem=peer_sems.at[1, step, 1], device_id=peer(step)[1], device_id_type=MESH,
        )

    def late_step(k):
        others = range(1, peer_count)
        if k == 0:
            halve(late, 0)
        elif k == 1:
            add_half(late, 0)
            half = pl.ds(pl.multiple_of(lows[late][1], 16), sizes[late][0])
            scatter_ref[...] = grad_ref[half, :].astype(BF16)
            for step in others:
                scatter_copy(step).start()
        elif k == 2:
            total = grad_ref[piece_place(my_peer), :]
            for step in others:
                scatter_copy(step).wait()
                total = total + pieces_ref[step].astype(F32)
            sum_ref[piece_place(my_peer), :] = total.astype(BF16)
            exchange_shard(late, piece_place(my_peer), piece)
            for step in others:
                gather_copy(step).start()
        elif k == 3:
            for step in others:
                gather_copy(step).wait()
            give_copy(late, 0).start()
        elif k == 4:
            give_copy(late, 0).wait()

    def column_sums(values):
        return jnp.sum(values, axis=0, keepdims=True)

    def forward(index, group, kept):
        slot = lax.rem(group, 2)
        here = pl.ds(pl.multiple_of(index * rows, 16), rows)
        x32 = xw_ref[here, :]
        x = x32.astype(BF16)
        qkv_ref[kept] = (dot_nn(x, w_qkv_ref[...]) + qkv_shift).astype(BF16)
        for w in range(BLOCK_WINDOWS):
            cells = pl.ds(w * WINDOW, WINDOW)
            queries = by_head(qkv_ref[kept, cells, :width] * BF16(score_scale))
            scores = dot_nt(qkv_ref[kept, cells, width : 2 * width], queries) + score_bias_ref[...]
            top = jnp.max(scores, axis=0, keepdims=True)
            exps = jnp.exp(scores - top)
            prob = exps * (1.0 / jnp.sum(exps, axis=0, keepdims=True))
            prob_ref[kept, w] = prob
            att_ref[kept, cells, :] = own_head(
                dot_tn(prob.astype(BF16), qkv_ref[kept, cells, 2 * width :])
            ).astype(BF16)
            yield

        att = att_ref[kept]
        branch = dot_nn(att, w_proj_ref[...]) + b_proj
        yield
        norm_one, inverse_one = norm(branch)
        middle = x32 + norm_one * (1.0 + scale_one) + shift_one
        middle_low = middle.astype(BF16)
        pre = dot_nn(middle_low, w_up_ref[...]) + b_up
        yield
        hidden, slope = gelu_both(pre)
        hidden = hidden.astype(BF16)
        second = dot_nn(hidden, w_down_ref[...]) + b_down
        yield
        norm_two, inverse_two = norm(second)
        out_ref[slot, 0, here, :] = (middle + norm_two * (1.0 + scale_two) + shift_two).astype(BF16)

        g = gw_ref[here, :]
        yield
        second_low = norm_back(g * (1.0 + scale_two), norm_two, inverse_two).astype(BF16)
        pre_grad = dot_nt(second_low, w_down_ref[...]) * slope
        yield
        add_grad(16, dot_tn(second_low, hidden))
        yield
        pre_low = pre_grad.astype(BF16)
        up_sums = column_sums(pre_grad)
        middle_grad = g + dot_nt(pre_low, w_up_ref[...])
        yield
        add_grad(8, dot_tn(middle_low, pre_low))
        yield
        branch_low = norm_back(middle_grad * (1.0 + scale_one), norm_one, inverse_one).astype(BF16)
        att_ref[kept] = dot_nt(branch_low, w_proj_ref[...]).astype(BF16)
        yield
        add_grad(6, dot_tn(att, branch_low))
        middle_grad_ref[kept] = middle_grad
        sums = [
            column_sums(middle_grad), column_sums(middle_grad * norm_one), column_sums(g),
            column_sums(g * norm_two), column_sums(branch_low.astype(F32)),
            column_sums(second_low.astype(F32)),
        ]
        sums += [jnp.zeros((1, width), F32)] * 3
        sums += [up_sums[:, j * width : (j + 1) * width] for j in range(hidden_width // width)]
        sums += [jnp.zeros((VECTORS - len(sums), width), F32)]
        small_ref[:VECTORS, :] += jnp.concatenate(sums, axis=0)

    def backward(index, group, kept):
        slot = lax.rem(group, 2)
        here = pl.ds(pl.multiple_of(index * rows, 16), rows)

        for w in range(BLOCK_WINDOWS):
            cells = pl.ds(w * WINDOW, WINDOW)
            queries = by_head(qkv_ref[kept, cells, :width] * BF16(score_scale))
            out_grad = by_head(att_ref[kept, cells, :])
            prob = prob_ref[kept, w]
            prob_grad = dot_nt(qkv_ref[kept, cells, 2 * width :], out_grad)
            score_grad = prob * (prob_grad - jnp.sum(prob_grad * prob, axis=0, keepdims=True))
            score_sum_ref[...] += score_grad
            score_grad = score_grad.astype(BF16)
            dqkv_ref[cells, :width] = (
                own_head(dot_tn(score_grad, qkv_ref[kept, cells, width : 2 * width])) * score_scale
            ).astype(BF16)
            dqkv_ref[cells, width : 2 * width] = dot_nn(score_grad, queries).astype(BF16)
            dqkv_ref[cells, 2 * width :] = dot_nn(prob.astype(BF16), out_grad).astype(BF16)
            yield

        dqkv = dqkv_ref[...]
        out_ref[slot, 1, here, :] = (
            middle_grad_ref[kept] + dot_nt(dqkv, w_qkv_ref[...])
        ).astype(BF16)
        add_grad(0, dot_tn(xw_ref[here, :].astype(BF16), dqkv))
        qkv_sums = column_sums(dqkv.astype(F32))
        sums = [qkv_sums[:, j * width : (j + 1) * width] for j in range(3)]
        small_ref[6:9, :] += jnp.concatenate(sums, axis=0)

    def together(*stages):
        stages = list(stages)
        while stages:
            for stage in list(stages):
                try:
                    next(stage)
                except StopIteration:
                    stages.remove(stage)

    blocks = col_count // WX // BLOCK_WINDOWS

    def plain_blocks(group):
        def block(index, carry):
            @pl.when((group == 0) & (index == 2))
            def _():
                rows_copy(1).start()
                corner_copies[1].start()

            together(forward(index, group, 0))
            together(backward(index, group, 0))
            return carry

        lax.fori_loop(0, blocks, block, 0)

    def last_blocks(group):
        def forwards(index, carry):
            together(forward(index, group, index))
            return carry

        def backwards(index, carry):
            stage = backward(index, group, index)
            for _ in range(BLOCK_WINDOWS // 2 + 1):
                next(stage)
            for step in range(hidden_steps):
                @pl.when(index == step)
                def _():
                    for p in early:
                        sum_step(p, step + 1)

            together(stage)
            return carry

        lax.fori_loop(0, blocks, forwards, 0)
        for p in early:
            sum_step(p, 0)
        lax.fori_loop(0, blocks, backwards, 0)
        for step in range(blocks, hidden_steps):
            for p in early:
                sum_step(p, step + 1)

    def gather(pair, group):
        def assemble(own, strip, axis):
            if group in (0, GROUPS - 1):
                return lax.slice_in_dim(own, HALF_Y, HALF_Y + WY, axis=axis)
            if TOWARD[pair] == 1:
                return jnp.concatenate([strip, lax.slice_in_dim(own, 0, HALF_Y, axis=axis)], axis=axis)
            return jnp.concatenate(
                [lax.slice_in_dim(own, row_count - HALF_Y, row_count, axis=axis), strip], axis=axis
            )

        for a, target in enumerate((xw_ref, gw_ref)):
            def field(start, count, z, a=a):
                own = fields_ref[a, field_level(pair, z), start : start + count].astype(F32)
                strip = None
                if group in (1, 2):
                    strip = rows_in_ref[pair, a, z, start * HALF_Y : (start + count) * HALF_Y, :]
                    strip = unpack_strip(strip.astype(F32), count)
                return assemble(own, strip, 1)

            def western(c, z, a=a):
                own = cols_in_ref[a, field_level(pair, z), c].astype(F32)
                strip = None
                if group in (1, 2):
                    place = ((z * 2 + a) * HALF_X + c) * HALF_Y
                    strip = corner_in_ref[pair].astype(F32)[place : place + HALF_Y]
                return assemble(own, strip, 0)

            store_windows(field, western, target)

    def send_back(pair, slot):
        sent = 0 if TOWARD[pair] == 1 else HALF_Y
        for a in range(2):
            for start in range(0, col_count - HALF_X, PACKED_COLS):
                count = min(PACKED_COLS, col_count - HALF_X - start)
                first = (start + HALF_X) * CELLS
                cells = out_ref[slot, a, first : first + count * CELLS, :].astype(F32)
                for z in range(WZ):
                    places = [c * CELLS + z * WY + sent for c in range(count)]
                    rows_out_ref[
                        pair, a, z, start * HALF_Y : (start + count) * HALF_Y, :
                    ] = jnp.concatenate(
                        [cells[p : p + HALF_Y] for p in places], axis=0
                    ).astype(BF16)
        back_copy(pair).start()

    def group_step(group, carry):
        pair, slot = group_pair(group), lax.rem(group, 2)
        inner = (group == 0) | (group == GROUPS - 1)

        @pl.when(group == 0)
        def _():
            corner_copies[0].start()
            cols_copy.wait_recv()

        @pl.when(group >= 2)
        def _():
            out_copy(group - 2).wait()
            edge_copy(group - 2).wait_send()

        @pl.when(group == GROUPS - 1)
        def _():
            corner_back_copy(0).wait_send()

        @pl.when(inner)
        def _():
            gather(pair, 0)

        for straddling in range(2):
            @pl.when(group == 1 + straddling)
            def _():
                rows_copy(straddling).wait_recv()
                corner_copies[straddling].wait_recv()
                gather(straddling, 1 + straddling)

        bases = [-HALF_Y if step == 1 else row_count - HALF_Y for step in TOWARD]
        base = jnp.where(inner, HALF_Y, jnp.where(group == 1, bases[0], bases[1]))
        score_bias_ref[...] = mask_scores(
            bias_ref[...], pair, base, lat, band_count, crop_ref, row_count
        )
        @pl.when(group < GROUPS - 1)
        def _():
            plain_blocks(group)

        @pl.when(group == GROUPS - 1)
        def _():
            last_blocks(group)

        out_copy(group).start()
        edge_copy(group).start()

        for straddling in range(2):
            @pl.when(group == 1 + straddling)
            def _():
                corner_back_copy(straddling).start()
                rows_copy(straddling).wait_send()
                send_back(straddling, slot)

        return carry

    lax.fori_loop(0, GROUPS, group_step, 0)
    late_step(0)
    small_ref[VECTORS:, : HEADS * OFFSETS] = table_grad(score_sum_ref)
    early_steps = 2 * halvings - hidden_steps
    for k in range(max(early_steps, 4, len(bits))):
        if k < len(bits):
            small_copy = to_partner(small_ref, small_recv_ref.at[k], small_sems.at[k], bits[k])
            small_copy.start()
        if k < early_steps:
            for p in early:
                sum_step(p, hidden_steps + 1 + k)
        late_step(k + 1)
        if k < len(bits):
            small_copy.wait()
            small_ref[...] += small_recv_ref[k]
    for group in (2, 3):
        out_copy(group).wait()
        edge_copy(group).wait_send()
    corner_back_copy(1).wait_send()
    cols_copy.wait_send()
    for copy in corner_copies:
        copy.wait_send()
    for pair in range(2):
        back_copy(pair).wait()
        corner_back_copy(pair).wait_recv()
    for group in range(GROUPS):
        edge_copy(group).wait_recv()


def block_call(crop_rows, tokens, cotangent, constants):
    level_count, col_count, row_count, width = tokens.shape
    vmem = pl.BlockSpec(memory_space=pltpu.VMEM)
    cells = col_count * CELLS
    rows = BLOCK_WINDOWS * WINDOW
    edge = -(-EDGE // 16) * 16
    blocks = col_count // WX // BLOCK_WINDOWS
    pairs = level_count // WZ
    strips = (pairs, 2, WZ, packed_rows(col_count), width)
    grad_rows = (4 * width + 2 * constants[4].shape[1]) * (width // LANES)
    bits, halvings = sum_bits()
    parts = sum_parts(width, constants[4].shape[1])
    more = max(1, len(bits) - halvings)
    late_rows = parts[2][1] // 2
    shard = max([count >> halvings for _, count in parts] + [late_rows // peer_sizes()[2]])
    half_rows = sum(halved(count, halvings)[1][-1] for _, count in parts)
    sends = pltpu.SemaphoreType.DMA
    return pl.pallas_call(
        block_kernel,
        in_specs=[pl.BlockSpec(memory_space=pltpu.SMEM), ANY, ANY] + [vmem] * len(constants),
        out_specs=[ANY] * 4 + [vmem] * 2,
        out_shape=[
            shape_of((2, GROUPS, cells, width), BF16),
            shape_of(strips, BF16),
            shape_of((GROUPS, 2, edge, width), BF16),
            shape_of((pairs, 2, edge, width), BF16),
            shape_of((grad_rows, LANES), BF16),
            shape_of((VECTORS + TABLE_ROWS, width), F32),
        ],
        scratch_shapes=[
            pltpu.VMEM((grad_rows, LANES), F32),
            pltpu.VMEM((half_rows, LANES), BF16),
            pltpu.VMEM((half_rows, LANES), BF16),
            pltpu.VMEM((2, len(parts), more, shard, LANES), BF16),
            pltpu.VMEM((max(1, len(bits)), VECTORS + TABLE_ROWS, width), F32),
            pltpu.VMEM((late_rows, LANES), BF16),
            pltpu.VMEM((peer_sizes()[2], late_rows // peer_sizes()[2], LANES), BF16),
            pltpu.VMEM((2,) + tokens.shape, BF16),
            pltpu.VMEM(strips, BF16),
            pltpu.VMEM(strips, BF16),
            pltpu.VMEM((2, level_count, HALF_X, row_count, width), BF16),
            pltpu.VMEM((pairs, edge, width), BF16),
            pltpu.VMEM((pairs, edge, width), BF16),
            pltpu.VMEM((2, 2, cells, width), BF16),
            pltpu.VMEM((WINDOW, SCORES), F32),
            pltpu.VMEM((cells, width), F32),
            pltpu.VMEM((cells, width), F32),
            pltpu.VMEM((blocks, rows, 3 * width), BF16),
            pltpu.VMEM((blocks, BLOCK_WINDOWS, WINDOW, SCORES), F32),
            pltpu.VMEM((blocks, rows, width), BF16),
            pltpu.VMEM((blocks, rows, width), F32),
            pltpu.VMEM((rows, 3 * width), BF16),
            pltpu.VMEM((WINDOW, SCORES), F32),
            sends((2 * level_count,)), sends((3, 2)), sends((pairs, 2)), sends((pairs, 2)),
            sends((GROUPS, 2)), sends((pairs, 2)), sends((GROUPS,)),
            sends((len(parts), len(bits) + halvings, 2)), sends((max(1, len(bits)), 2)),
            sends((2, peer_sizes()[2], 2)),
        ],
        cost_estimate=pl.CostEstimate(
            flops=GROUPS * cells * 5_200_000, bytes_accessed=32 * 2**20, transcendentals=0
        ),
        compiler_params=pltpu.CompilerParams(
            collective_id=1, has_side_effects=True, vmem_limit_bytes=VMEM_LIMIT
        ),
    )(crop_rows, tokens, cotangent, *constants)


def merge_kernel(
    inner_ref, straddle_ref, rows_ref, inner_edge_ref, straddle_edge_ref, corner_ref,
    grad_ref, small_ref, context_ref, *out_refs,
):
    fields, grads = out_refs[:2], out_refs[2:]
    _, col_count, row_count, width = fields[0].shape
    step = pl.program_id(0)

    def piece(rows_of, a, first_col, count, first, size):
        block = rows_of(a)[first_col * CELLS : (first_col + count) * CELLS, :].astype(F32)
        return block.reshape(count, CELLS, width)[:, first : first + size]

    straddle, inner = lambda a: straddle_ref.at[a, 0], lambda a: inner_ref.at[a, 0]
    straddle_edge, inner_edge, corner = (
        lambda a, ref=ref: ref.at[0, a] for ref in (straddle_edge_ref, inner_edge_ref, corner_ref)
    )
    for pair, z in ((0, 0), (0, 1), (1, 0), (1, 1)):
        @pl.when(step == pair * WZ + z)
        def _():
            first = z * WY
            kept, sent = (HALF_Y, 0) if TOWARD[pair] == 1 else (0, HALF_Y)

            def in_order(own, inner_rows, back):
                parts = [own, inner_rows, back] if TOWARD[pair] == 1 else [back, inner_rows, own]
                return jnp.concatenate(parts, axis=1).astype(BF16)

            for a, field in enumerate(fields):
                for start in range(0, col_count - HALF_X, PACKED_COLS):
                    count = min(PACKED_COLS, col_count - HALF_X - start)
                    strip = rows_ref[0, a, 0, start * HALF_Y : (start + count) * HALF_Y, :]
                    field[0, start : start + count] = in_order(
                        piece(straddle, a, start + HALF_X, count, first + kept, HALF_Y),
                        piece(inner, a, start + HALF_X, count, first, WY),
                        unpack_strip(strip.astype(F32), count),
                    )
                field[0, col_count - HALF_X :] = in_order(
                    piece(straddle_edge, a, 0, HALF_X, first + kept, HALF_Y),
                    piece(inner_edge, a, 0, HALF_X, first, WY),
                    piece(corner, a, 0, HALF_X, first + sent, HALF_Y),
                )

    grad_qkv, grad_proj, grad_up, grad_down, grad_mod, *vectors = grads

    def slab(index):
        per_slab = width // LANES
        return jnp.concatenate([
            grad_ref[j * width : (j + 1) * width, :].astype(F32)
            for j in range(index * per_slab, (index + 1) * per_slab)
        ], axis=1)

    @pl.when(step == 0)
    def _():
        for j in range(3):
            grad_qkv[:, j * width : (j + 1) * width] = slab(j)
        grad_proj[...] = slab(3)

    @pl.when(step == 1)
    def _():
        for j in range(grad_up.shape[1] // width):
            grad_up[:, j * width : (j + 1) * width] = slab(4 + j)

    @pl.when(step == 2)
    def _():
        for j in range(grad_down.shape[0] // width):
            grad_down[j * width : (j + 1) * width, :] = slab(8 + j).T

    @pl.when(step == 3)
    def _():
        lanes = context_ref.shape[1]
        for part in range(4):
            row = small_ref[part : part + 1, :]
            for j in range(0, width, lanes):
                grad_mod[:, part * width + j : part * width + j + lanes] = (
                    context_ref[...] * row[:, j : j + lanes]
                )
        mod_bias, proj_bias, down_bias, q_bias, v_bias, up_bias = vectors
        mod_bias[...] = jnp.concatenate([small_ref[i : i + 1, :] for i in range(4)], axis=1)
        up_bias[...] = jnp.concatenate([small_ref[i : i + 1, :] for i in range(9, 13)], axis=1)
        for ref, i in ((proj_bias, 4), (down_bias, 5), (q_bias, 6), (v_bias, 8)):
            ref[...] = small_ref[i : i + 1, :]


def merge(field_shape, hidden_width, windows, rows_back, edge_back, corner_back, grad, small, context):
    level_count, col_count, row_count, width = field_shape

    def level_of(i):
        return (i + WZ // 2) % level_count

    def group_of(pair, straddles):
        return 1 + pair if straddles else (GROUPS - 1) * pair

    def windows_of(straddles):
        return pl.BlockSpec(
            (2, 1) + windows.shape[2:], lambda i: (0, group_of(i // WZ, straddles), 0, 0)
        )

    def edge_of(straddles):
        return pl.BlockSpec(
            (1,) + edge_back.shape[1:], lambda i: (group_of(i // WZ, straddles), 0, 0, 0)
        )

    shapes = [
        (width, 3 * width), (width, width), (width, hidden_width), (hidden_width, width),
        (width, 4 * width), (1, 4 * width), (1, width), (1, width), (1, width), (1, width),
        (1, hidden_width),
    ]
    field = pl.BlockSpec((1,) + field_shape[1:], lambda i: (level_of(i), 0, 0, 0))
    return pl.pallas_call(
        merge_kernel,
        grid=(level_count,),
        in_specs=[
            windows_of(False), windows_of(True),
            pl.BlockSpec((1, 2, 1) + rows_back.shape[3:], lambda i: (i // WZ, 0, i % WZ, 0, 0)),
            edge_of(False), edge_of(True),
            pl.BlockSpec((1,) + corner_back.shape[1:], lambda i: (i // WZ, 0, 0, 0)),
        ] + [whole(v.shape) for v in (grad, small, context)],
        out_specs=[field, field] + [whole(s) for s in shapes],
        out_shape=[shape_of(field_shape, BF16)] * 2 + [shape_of(s, F32) for s in shapes],
        compiler_params=pltpu.CompilerParams(vmem_limit_bytes=VMEM_LIMIT),
    )(windows, windows, rows_back, edge_back, edge_back, corner_back, grad, small, context)


def on_device(
    tokens, cotangent, w_qkv, q_bias, v_bias, w_proj, b_proj, w_up, b_up, w_down, b_down,
    w_mod, b_mod, rel_table, crop_rows, lead_hours,
):
    fields = [field.transpose(0, 2, 1, 3) for field in (tokens, cotangent)]
    table = rel_table.transpose(1, 3, 0, 2)
    vectors = (b_mod, b_proj, b_down, q_bias, v_bias, b_up)
    bias, vecs, context = set_up(lead_hours, w_mod, vectors, table)
    constants = [bias, vecs, w_qkv, w_proj, w_up, w_down]
    windows, rows_back, edge_back, corner_back, grad, small = block_call(
        crop_rows, *fields, constants
    )
    (
        mixed, token_grad, grad_qkv, grad_proj, grad_up, grad_down, grad_mod, grad_mod_bias,
        grad_proj_bias, grad_down_bias, grad_q_bias, grad_v_bias, grad_up_bias,
    ) = merge(
        fields[0].shape, w_up.shape[1], windows, rows_back, edge_back, corner_back, grad, small, context
    )
    table_sum = small[VECTORS : VECTORS + 2 * WY - 1, : HEADS * OFFSETS][::-1]
    grad_table = table_sum.reshape(2 * WY - 1, 2 * WZ - 1, 2 * WX - 1, HEADS).transpose(3, 1, 0, 2)
    return (
        mixed.transpose(0, 2, 1, 3),
        token_grad.transpose(0, 2, 1, 3),
        grad_qkv,
        grad_q_bias[0],
        grad_v_bias[0],
        grad_proj,
        grad_proj_bias[0],
        grad_up,
        grad_up_bias[0],
        grad_down,
        grad_down_bias[0],
        grad_mod,
        grad_mod_bias[0],
        grad_table,
    )


def solution(mesh):
    split = P(None, "lat", "lon", None)
    return jax.shard_map(
        on_device,
        mesh=mesh,
        in_specs=(split, split) + (P(),) * 14,
        out_specs=(split, split) + (P(),) * 12,
        check_vma=False,
    )
```

```python
import functools
import math

import jax
import jax.numpy as jnp
from jax import lax
from jax.experimental import pallas as pl
from jax.experimental.pallas import tpu as pltpu
from jax.sharding import PartitionSpec as P

WZ = 2
WY = 12
WX = 6
CELLS = WZ * WY
WINDOW = CELLS * WX
HEADS = 4
SCORES = HEADS * WINDOW
HALF_Y = WY // 2
HALF_X = WX // 2
BLOCK_WINDOWS = 5
OFFSETS = (2 * WZ - 1) * (2 * WX - 1)
VECTORS = 16
LANES = 128
TABLE_ROWS = 2 * WY
EDGE = HALF_X * CELLS
PACKED_COLS = 8

NORM_EPSILON = 1e-05
MASKED_SCORE = -1000000000.0
F32 = jnp.float32
BF16 = jnp.bfloat16
MESH = pl.DeviceIdType.MESH
ANY = pl.BlockSpec(memory_space=pl.ANY)
VMEM_LIMIT = 60 * 2**20


def dot_nn(left, right):
    return lax.dot_general(left, right, (((1,), (0,)), ((), ())), preferred_element_type=F32)


def dot_nt(left, right):
    return lax.dot_general(left, right, (((1,), (1,)), ((), ())), preferred_element_type=F32)


def dot_tn(left, right):
    return lax.dot_general(left, right, (((0,), (0,)), ((), ())), preferred_element_type=F32)


def iota(shape, axis):
    return lax.broadcasted_iota(jnp.int32, shape, axis)


def whole(shape, buffers=1):
    return pl.BlockSpec(
        shape, lambda *_: (0,) * len(shape), pipeline_mode=pl.Buffered(buffers)
    )


def shape_of(shape, dtype):
    return jax.ShapeDtypeStruct(shape, dtype)


def packed_rows(col_count):
    return -(-col_count * HALF_Y // 16) * 16


def offset_pick(key_x, key_z):
    lane = iota((HEADS * OFFSETS, SCORES), 1)
    head, rest = lane // WINDOW, lane % WINDOW
    query_x, query_z = rest // CELLS, (rest % CELLS) // WY
    offset_z, offset_x = query_z - key_z + WZ - 1, query_x - key_x + WX - 1
    place = (offset_z * (2 * WX - 1) + offset_x) * HEADS + head
    return iota((HEADS * OFFSETS, SCORES), 0) == place


def set_up(
    lead_ref, w_mod_ref, b_mod_ref, b_proj_ref, b_down_ref, q_bias_ref, v_bias_ref, b_up_ref,
    table_ref, bias_ref, vec_ref, context_ref,
):
    width = w_mod_ref.shape[0]
    half = width // 2
    lanes = context_ref.shape[1]
    fraction = iota((half, lanes), 0).astype(F32) / half
    angles = lead_ref[0].astype(F32) * jnp.exp(-math.log(1000.0) * fraction)
    waves = jnp.concatenate([jnp.sin(angles), jnp.cos(angles)], axis=0)
    context = waves * (1.0 / (1.0 + jnp.exp(-waves)))
    context_ref[...] = context
    for part in range(4):
        pieces = []
        for j in range(width // lanes):
            start = part * width + j * lanes
            pieces.append(
                jnp.sum(context * w_mod_ref[:, start : start + lanes].astype(F32), axis=0, keepdims=True)
            )
        vec_ref[part : part + 1, :] = (
            jnp.concatenate(pieces, axis=1)
            + b_mod_ref[part * width : (part + 1) * width].astype(F32)[None]
        )
    vec_ref[4:, :] = jnp.zeros((VECTORS - 4, width), F32)
    for i, ref in ((4, b_proj_ref), (5, b_down_ref), (6, q_bias_ref), (8, v_bias_ref)):
        vec_ref[i : i + 1, :] = ref[...].astype(F32)[None]
    for j in range(b_up_ref.shape[0] // width):
        vec_ref[9 + j : 10 + j, :] = b_up_ref[j * width : (j + 1) * width].astype(F32)[None]

    offsets_y = 2 * WY - 1
    backwards = iota((TABLE_ROWS, offsets_y), 0) + iota((TABLE_ROWS, offsets_y), 1) == offsets_y - 1
    table = jnp.concatenate(
        [table_ref[z, x].astype(F32) for z in range(2 * WZ - 1) for x in range(2 * WX - 1)], axis=0
    ).astype(BF16)
    table = dot_nt(backwards.astype(BF16), table).astype(BF16)
    query_y = iota((WY, SCORES), 1) % WY
    for key_x in range(WX):
        for key_z in range(WZ):
            spread = dot_nn(table, offset_pick(key_x, key_z).astype(BF16))
            rows = spread[WY - 1 : 2 * WY - 1]
            for y in range(1, WY):
                rows = jnp.where(query_y == y, spread[WY - 1 - y : 2 * WY - 1 - y], rows)
            start = key_x * CELLS + key_z * WY
            bias_ref[start : start + WY, :] = rows


def table_grad(score_sum_ref):
    query_y = iota((WY, SCORES), 1) % WY
    total = jnp.zeros((TABLE_ROWS, HEADS * OFFSETS), F32)
    for key_x in range(WX):
        for key_z in range(WZ):
            start = key_x * CELLS + key_z * WY
            rows = score_sum_ref[start : start + WY, :]
            spread = jnp.zeros((TABLE_ROWS, SCORES), F32)
            for y in range(WY):
                own = jnp.where(query_y == y, rows, 0.0)
                pads = (WY - 1 - y, TABLE_ROWS - (2 * WY - 1 - y))
                parts = [jnp.zeros((p, SCORES), F32) for p in pads]
                spread = spread + jnp.concatenate(
                    ([parts[0]] if pads[0] else []) + [own, parts[1]], axis=0
                )
            pick = offset_pick(key_x, key_z).astype(BF16)
            high = spread.astype(BF16)
            low = (spread - high.astype(F32)).astype(BF16)
            total = total + dot_nt(high, pick) + dot_nt(low, pick)
    return total


def halved(rows, count):
    sizes = [rows >> (i + 1) for i in range(count)]
    return sizes, [sum(sizes[:i]) for i in range(count + 1)]


def sum_bits():
    bits = [("lon", 0), ("lon", 1), ("lat", 0), ("lat", 1), ("lat", 2)]
    bits = [b for b in bits if 2 ** b[1] < lax.axis_size(b[0])]
    bits += [("lat", b) for b in range(3, lax.axis_size("lat").bit_length() - 1)]
    bits += [("lon", b) for b in range(2, lax.axis_size("lon").bit_length() - 1)]
    return bits, min(5, len(bits))


def peer_sizes():
    lons, lats = lax.axis_size("lon") // 2, min(8, lax.axis_size("lat"))
    return lons, lats, lons * lats


def sum_parts(width, hidden_width):
    qkv_rows = 3 * width * (width // LANES)
    rest = (width + 2 * hidden_width) * (width // LANES)
    first = -(-rest // 1024) * 512
    return [(qkv_rows, first), (qkv_rows + first, rest - first), (0, qkv_rows)]


def row_mean(values):
    return jnp.mean(values, axis=-1, keepdims=True)


def norm(values):
    center = values - row_mean(values)
    inverse = lax.rsqrt(row_mean(center * center) + NORM_EPSILON)
    return center * inverse, inverse


def norm_back(grad, normed, inverse):
    return inverse * (grad - row_mean(grad) - normed * row_mean(grad * normed))


def gelu_both(values):
    gauss_cdf = 0.5 * (1.0 + lax.erf(values * math.sqrt(0.5)))
    density = jnp.exp(values * values * -0.5) * (1.0 / math.sqrt(2.0 * math.pi))
    return values * gauss_cdf, gauss_cdf + values * density


def by_head(values):
    width = values.shape[-1] // HEADS
    lane_head = iota(values.shape, 1) // width
    zero = jnp.zeros_like(values)
    return jnp.concatenate([jnp.where(lane_head == h, values, zero) for h in range(HEADS)], axis=0)


def own_head(stacked):
    cells = stacked.shape[0] // HEADS
    width = stacked.shape[-1] // HEADS
    lane_head = iota((cells, stacked.shape[-1]), 1) // width
    picked = stacked[:cells]
    for h in range(1, HEADS):
        picked = jnp.where(lane_head == h, stacked[h * cells : (h + 1) * cells], picked)
    return picked


def store_windows(field, western, out_ref):
    width = out_ref.shape[1]
    for c in range(HALF_X):
        out_ref[c * CELLS : (c + 1) * CELLS, :] = jnp.concatenate(
            [western(c, z) for z in range(WZ)], axis=0
        )
    own_cols = out_ref.shape[0] // CELLS - HALF_X
    for start in range(0, own_cols, PACKED_COLS):
        count = min(PACKED_COLS, own_cols - start)
        both = jnp.concatenate([field(start, count, z) for z in range(WZ)], axis=1)
        first = (start + HALF_X) * CELLS
        out_ref[first : first + count * CELLS, :] = both.reshape(count * CELLS, width)


def unpack_strip(rows, count):
    return jnp.stack([rows[c * HALF_Y : (c + 1) * HALF_Y] for c in range(count)], axis=0)


def mask_scores(bias, level_wraps, base, band, band_count, crop_ref, row_count):
    crops = [
        crop_ref[lax.rem(band + step + band_count, band_count)] for step in (-1, 0, 1)
    ]
    firsts = [
        (lax.rem(band + step + band_count, band_count) == 0).astype(jnp.int32) for step in (0, 1)
    ]

    def parts(cell):
        z, row = (cell % CELLS) // WY, base + cell % WY
        part = 2 * jnp.where(z == WZ - 1, level_wraps, 0)
        part = part + jnp.where((row >= 0) & (row < HALF_Y), firsts[0], 0)
        part = part + jnp.where((row >= row_count) & (row < row_count + HALF_Y), firsts[1], 0)
        crop = jnp.where(row < 0, crops[0], jnp.where(row < row_count, crops[1], crops[2]))
        return part, (row + row_count) % row_count >= row_count - crop

    key = iota(bias.shape, 0)
    query = iota(bias.shape, 1) % WINDOW
    key_part, key_valid = parts(key)
    query_part, _ = parts(query)
    allowed = (key_part == query_part) & (key_valid | (key == query))
    return jnp.where(allowed, bias, bias + MASKED_SCORE)


GROUPS = 4
TOWARD = (1, 1)


def group_pair(group):
    return group // 2


def field_level(pair, z):
    return lax.rem(WZ * pair + z + WZ // 2, 2 * WZ)


def block_kernel(
    crop_ref, lead_ref, tokens_ref, cotangent_ref, w_mod_ref, b_mod_ref, b_proj_ref, b_down_ref,
    q_bias_ref, v_bias_ref, b_up_ref, table_ref, w_qkv_ref, w_proj_ref, w_up_ref, w_down_ref,
    win_ref, rows_back_ref, edge_back_ref, corner_back_ref, sum_ref, small_ref, context_ref,
    bias_ref, vec_ref,
    grad_ref, send_ref, recv_ref, more_ref, small_recv_ref, scatter_ref, pieces_ref, fields_ref, rows_out_ref, rows_in_ref, cols_in_ref, corner_out_ref, corner_in_ref, out_ref,
    score_bias_ref, xw_ref, gw_ref, qkv_ref, prob_ref, att_ref, middle_grad_ref, dqkv_ref,
    score_sum_ref,
    field_sems, halo_sems, rows_sems, back_sems, edge_sems, corner_sems, out_sems, sum_sems, small_sems,
    peer_sems,
):
    width = vec_ref.shape[1]
    hidden_width = w_up_ref.shape[1]
    _, level_count, col_count, row_count, _ = fields_ref.shape
    band_count = crop_ref.shape[0]
    score_scale = (width // HEADS) ** -0.5
    lat, lon = lax.axis_index("lat"), lax.axis_index("lon")
    lat_size, lon_size = lax.axis_size("lat"), lax.axis_size("lon")

    def device(lat_step, lon_step):
        return (
            lax.rem(lat + lat_step + lat_size, lat_size), lax.rem(lon + lon_step + lon_size, lon_size)
        )

    steps = [(0, 1)] + [(t, lon_step) for t in sorted(set(TOWARD)) for lon_step in (0, 1)]
    barrier = pltpu.get_barrier_semaphore()
    for lat_step, lon_step in steps:
        for sign in (1, -1):
            pl.semaphore_signal(
                barrier, inc=1, device_id=device(sign * lat_step, sign * lon_step), device_id_type=MESH
            )

    bits, halvings = sum_bits()
    own_bit, partner = {}, {}
    for axis, bit in bits:
        place = lat if axis == "lat" else lon
        own_bit[axis, bit] = (place // 2**bit) % 2
        moved = place + 2**bit * (1 - 2 * own_bit[axis, bit])
        partner[axis, bit] = (moved, lon) if axis == "lat" else (lat, moved)
        pl.semaphore_signal(barrier, inc=1, device_id=partner[axis, bit], device_id_type=MESH)
    peer_lons, peer_lats, peer_count = peer_sizes()
    my_peer = lon // 2 + peer_lons * (lat % peer_lats)

    def peer(step):
        index = (my_peer + step) % peer_count
        return index, (
            (lat // peer_lats) * peer_lats + index // peer_lons, 2 * (index % peer_lons) + lon % 2
        )

    for step in range(1, peer_count):
        pl.semaphore_signal(barrier, inc=1, device_id=peer(step)[1], device_id_type=MESH)

    loads = []
    for level in (1, 2, 3, 0):
        for a, ref in enumerate((tokens_ref, cotangent_ref)):
            loads.append(pltpu.make_async_copy(
                ref.at[level], fields_ref.at[a, level], field_sems.at[len(loads)]
            ))
            loads[-1].start()

    set_up(
        lead_ref, w_mod_ref, b_mod_ref, b_proj_ref, b_down_ref, q_bias_ref, v_bias_ref, b_up_ref,
        table_ref, bias_ref, vec_ref, context_ref,
    )

    def remote(source, target, sems, lat_step, lon_step):
        return pltpu.make_async_remote_copy(
            src_ref=source, dst_ref=target, send_sem=sems.at[0], recv_sem=sems.at[1],
            device_id=device(lat_step, lon_step), device_id_type=MESH,
        )

    last_cols = fields_ref.at[:, :, pl.ds(col_count - HALF_X, HALF_X)]
    cols_copy = remote(last_cols, cols_in_ref, halo_sems.at[0], 0, 1)
    corner_copies = [
        remote(corner_out_ref.at[pair], corner_in_ref.at[pair], halo_sems.at[1 + pair], TOWARD[pair], 1)
        for pair in range(2)
    ]

    def rows_copy(pair):
        return remote(
            rows_out_ref.at[pair], rows_in_ref.at[pair], rows_sems.at[pair], TOWARD[pair], 0
        )

    def back_copy(pair):
        return remote(
            rows_out_ref.at[pair], rows_back_ref.at[pair], back_sems.at[pair], -TOWARD[pair], 0
        )

    def edge_rows(group):
        return out_ref.at[lax.rem(group, 2), :, pl.ds(0, edge_back_ref.shape[2])]

    def edge_copy(group):
        return remote(edge_rows(group), edge_back_ref.at[group], edge_sems.at[group], 0, -1)

    def corner_back_copy(pair):
        return remote(
            edge_rows(1 + pair), corner_back_ref.at[pair], corner_sems.at[pair], -TOWARD[pair], -1
        )

    def out_copy(group):
        return pltpu.make_async_copy(
            out_ref.at[lax.rem(group, 2)], win_ref.at[:, group], out_sems.at[group]
        )

    for pair in range(2):
        corners = []
        sent = slice(row_count - HALF_Y, row_count) if TOWARD[pair] == 1 else slice(0, HALF_Y)
        for z in range(WZ):
            level = (WZ * pair + z + WZ // 2) % level_count
            for a in range(2):
                if pair == 0:
                    loads[z * 2 + a].wait()
                for start in range(0, col_count, PACKED_COLS):
                    count = min(PACKED_COLS, col_count - start)
                    block = fields_ref[a, level, start : start + count].astype(F32)
                    packed = [block[c, sent] for c in range(count)]
                    rows_out_ref[
                        pair, a, z, start * HALF_Y : (start + count) * HALF_Y, :
                    ] = jnp.concatenate(packed, axis=0).astype(BF16)
                block = fields_ref[a, level, col_count - HALF_X :].astype(F32)
                corners += [block[c, sent] for c in range(HALF_X)]
        spare = corner_out_ref.shape[1] - HALF_Y * len(corners)
        corners.append(jnp.zeros((spare, width), F32))
        corner_out_ref[pair] = jnp.concatenate(corners, axis=0).astype(BF16)
        if pair == 0:
            pl.semaphore_wait(barrier, 2 * len(steps) + len(bits) + peer_count - 1)
            rows_copy(0).start()
            for load in loads[2 * WZ :]:
                load.wait()
            cols_copy.start()

    grad_ref[...] = jnp.zeros_like(grad_ref)
    small_ref[...] = jnp.zeros_like(small_ref)
    score_sum_ref[...] = jnp.zeros_like(score_sum_ref)
    rows = BLOCK_WINDOWS * WINDOW
    shift_one, scale_one, shift_two, scale_two, b_proj, b_down = [
        vec_ref[i : i + 1, :] for i in range(6)
    ]
    qkv_shift = jnp.concatenate([vec_ref[i : i + 1, :] for i in range(6, 9)], axis=1)
    b_up = jnp.concatenate([vec_ref[i : i + 1, :] for i in range(9, 13)], axis=1)

    def add_grad(first, value):
        for j in range(value.shape[1] // LANES):
            grad_ref[(first + j) * width : (first + j + 1) * width, :] += value[
                :, j * LANES : (j + 1) * LANES
            ]

    parts = sum_parts(width, hidden_width)
    sizes, send_starts = zip(*[halved(count, halvings) for _, count in parts])
    orders, lows = [], []
    for p, (first, _) in enumerate(parts):
        order = list(bits[:halvings])
        if p == 1 and halvings > 2:
            order[1], order[2] = order[2], order[1]
        orders.append(order)
        lows.append([first])
        for s, bit in enumerate(order):
            lows[p].append(lows[p][s] + own_bit[bit] * sizes[p][s])

    def to_partner(source, target, sems, bit):
        return pltpu.make_async_remote_copy(
            src_ref=source, dst_ref=target, send_sem=sems.at[0], recv_sem=sems.at[1],
            device_id=partner[bit], device_id_type=MESH,
        )

    def half_place(p, s):
        return pl.ds(sum(starts[-1] for starts in send_starts[:p]) + send_starts[p][s], sizes[p][s])

    def half_copy(p, s):
        place = half_place(p, s)
        return to_partner(send_ref.at[place], recv_ref.at[place], sum_sems.at[p, s], orders[p][s])

    def halve(p, s):
        size, bit = sizes[p][s], orders[p][s]
        away = pl.multiple_of(lows[p][s] + (1 - own_bit[bit]) * size, 16)
        send_ref[half_place(p, s), :] = grad_ref[pl.ds(away, size), :].astype(BF16)
        half_copy(p, s).start()

    def add_half(p, s):
        half_copy(p, s).wait()
        here = pl.ds(pl.multiple_of(lows[p][s + 1], 16), sizes[p][s])
        grad_ref[here, :] += recv_ref[half_place(p, s), :].astype(F32)

    def shard_done(p):
        here = pl.ds(pl.multiple_of(lows[p][halvings], 16), sizes[p][-1])
        sum_ref[here, :] = grad_ref[here, :].astype(BF16)
        exchange_shard(p, here, sizes[p][-1])

    def exchange_shard(p, here, count):
        for s in range(halvings, len(bits)):
            mine = more_ref.at[0, p, s - halvings, pl.ds(0, count)]
            theirs = more_ref.at[1, p, s - halvings, pl.ds(0, count)]
            mine[...] = sum_ref[here, :]
            copy = to_partner(mine, theirs, sum_sems.at[p, s], bits[s])
            copy.start()
            copy.wait()
            sum_ref[here, :] = (mine[...].astype(F32) + theirs[...].astype(F32)).astype(BF16)

    def give_copy(p, s):
        here = sum_ref.at[pl.ds(pl.multiple_of(lows[p][s + 1], 16), sizes[p][s]), :]
        return to_partner(here, here, sum_sems.at[p, len(bits) + s], orders[p][s])

    def sum_step(p, k):
        if 1 <= k <= halvings:
            add_half(p, k - 1)
        if k < halvings:
            halve(p, k)
        if k == halvings:
            shard_done(p)
        if halvings < k <= 2 * halvings:
            give_copy(p, 2 * halvings - k).wait()
        if halvings <= k < 2 * halvings:
            give_copy(p, 2 * halvings - 1 - k).start()

    early, late = (0, 1), 2
    hidden_steps = min(4, halvings)

    piece = sizes[late][0] // peer_count

    def piece_place(index):
        return pl.ds(pl.multiple_of(lows[late][1] + index * piece, 16), piece)

    def scatter_copy(step):
        index, there = peer(step)
        return pltpu.make_async_remote_copy(
            src_ref=scatter_ref.at[pl.ds(pl.multiple_of(index * piece, 16), piece), :],
            dst_ref=pieces_ref.at[step], send_sem=peer_sems.at[0, step, 0],
            recv_sem=peer_sems.at[0, step, 1], device_id=there, device_id_type=MESH,
        )

    def gather_copy(step):
        mine = sum_ref.at[piece_place(my_peer), :]
        return pltpu.make_async_remote_copy(
            src_ref=mine, dst_ref=mine, send_sem=peer_sems.at[1, step, 0],
            recv_sem=peer_sems.at[1, step, 1], device_id=peer(step)[1], device_id_type=MESH,
        )

    def late_step(k):
        others = range(1, peer_count)
        if k == 0:
            halve(late, 0)
        elif k == 1:
            add_half(late, 0)
            half = pl.ds(pl.multiple_of(lows[late][1], 16), sizes[late][0])
            scatter_ref[...] = grad_ref[half, :].astype(BF16)
            for step in others:
                scatter_copy(step).start()
        elif k == 2:
            total = grad_ref[piece_place(my_peer), :]
            for step in others:
                scatter_copy(step).wait()
                total = total + pieces_ref[step].astype(F32)
            sum_ref[piece_place(my_peer), :] = total.astype(BF16)
            exchange_shard(late, piece_place(my_peer), piece)
            for step in others:
                gather_copy(step).start()
        elif k == 3:
            for step in others:
                gather_copy(step).wait()
            give_copy(late, 0).start()
        elif k == 4:
            give_copy(late, 0).wait()

    def column_sums(values):
        return jnp.sum(values, axis=0, keepdims=True)

    def forward(index, group, kept):
        slot = lax.rem(group, 2)
        here = pl.ds(pl.multiple_of(index * rows, 16), rows)
        x32 = xw_ref[here, :]
        x = x32.astype(BF16)
        qkv_ref[kept] = (dot_nn(x, w_qkv_ref[...]) + qkv_shift).astype(BF16)
        for w in range(BLOCK_WINDOWS):
            cells = pl.ds(w * WINDOW, WINDOW)
            queries = by_head(qkv_ref[kept, cells, :width] * BF16(score_scale))
            scores = dot_nt(qkv_ref[kept, cells, width : 2 * width], queries) + score_bias_ref[...]
            top = jnp.max(scores, axis=0, keepdims=True)
            exps = jnp.exp(scores - top)
            prob = exps * (1.0 / jnp.sum(exps, axis=0, keepdims=True))
            prob_ref[kept, w] = prob
            att_ref[kept, cells, :] = own_head(
                dot_tn(prob.astype(BF16), qkv_ref[kept, cells, 2 * width :])
            ).astype(BF16)
            yield

        att = att_ref[kept]
        branch = dot_nn(att, w_proj_ref[...]) + b_proj
        yield
        norm_one, inverse_one = norm(branch)
        middle = x32 + norm_one * (1.0 + scale_one) + shift_one
        middle_low = middle.astype(BF16)
        pre = dot_nn(middle_low, w_up_ref[...]) + b_up
        yield
        hidden, slope = gelu_both(pre)
        hidden = hidden.astype(BF16)
        second = dot_nn(hidden, w_down_ref[...]) + b_down
        yield
        norm_two, inverse_two = norm(second)
        out_ref[slot, 0, here, :] = (middle + norm_two * (1.0 + scale_two) + shift_two).astype(BF16)

        g = gw_ref[here, :]
        yield
        second_low = norm_back(g * (1.0 + scale_two), norm_two, inverse_two).astype(BF16)
        pre_grad = dot_nt(second_low, w_down_ref[...]) * slope
        yield
        add_grad(16, dot_tn(second_low, hidden))
        yield
        pre_low = pre_grad.astype(BF16)
        up_sums = column_sums(pre_grad)
        middle_grad = g + dot_nt(pre_low, w_up_ref[...])
        yield
        add_grad(8, dot_tn(middle_low, pre_low))
        yield
        branch_low = norm_back(middle_grad * (1.0 + scale_one), norm_one, inverse_one).astype(BF16)
        att_ref[kept] = dot_nt(branch_low, w_proj_ref[...]).astype(BF16)
        yield
        add_grad(6, dot_tn(att, branch_low))
        middle_grad_ref[kept] = middle_grad
        sums = [
            column_sums(middle_grad), column_sums(middle_grad * norm_one), column_sums(g),
            column_sums(g * norm_two), column_sums(branch_low.astype(F32)),
            column_sums(second_low.astype(F32)),
        ]
        sums += [jnp.zeros((1, width), F32)] * 3
        sums += [up_sums[:, j * width : (j + 1) * width] for j in range(hidden_width // width)]
        sums += [jnp.zeros((VECTORS - len(sums), width), F32)]
        small_ref[:VECTORS, :] += jnp.concatenate(sums, axis=0)

    def backward(index, group, kept):
        slot = lax.rem(group, 2)
        here = pl.ds(pl.multiple_of(index * rows, 16), rows)

        for w in range(BLOCK_WINDOWS):
            cells = pl.ds(w * WINDOW, WINDOW)
            queries = by_head(qkv_ref[kept, cells, :width] * BF16(score_scale))
            out_grad = by_head(att_ref[kept, cells, :])
            prob = prob_ref[kept, w]
            prob_grad = dot_nt(qkv_ref[kept, cells, 2 * width :], out_grad)
            score_grad = prob * (prob_grad - jnp.sum(prob_grad * prob, axis=0, keepdims=True))
            score_sum_ref[...] += score_grad
            score_grad = score_grad.astype(BF16)
            dqkv_ref[cells, :width] = (
                own_head(dot_tn(score_grad, qkv_ref[kept, cells, width : 2 * width])) * score_scale
            ).astype(BF16)
            dqkv_ref[cells, width : 2 * width] = dot_nn(score_grad, queries).astype(BF16)
            dqkv_ref[cells, 2 * width :] = dot_nn(prob.astype(BF16), out_grad).astype(BF16)
            yield

        dqkv = dqkv_ref[...]
        out_ref[slot, 1, here, :] = (
            middle_grad_ref[kept] + dot_nt(dqkv, w_qkv_ref[...])
        ).astype(BF16)
        add_grad(0, dot_tn(xw_ref[here, :].astype(BF16), dqkv))
        qkv_sums = column_sums(dqkv.astype(F32))
        sums = [qkv_sums[:, j * width : (j + 1) * width] for j in range(3)]
        small_ref[6:9, :] += jnp.concatenate(sums, axis=0)

    def together(*stages):
        stages = list(stages)
        while stages:
            for stage in list(stages):
                try:
                    next(stage)
                except StopIteration:
                    stages.remove(stage)

    blocks = col_count // WX // BLOCK_WINDOWS

    def plain_blocks(group):
        def block(index, carry):
            @pl.when((group == 0) & (index == 2))
            def _():
                rows_copy(1).start()
                corner_copies[1].start()

            together(forward(index, group, 0))
            together(backward(index, group, 0))
            return carry

        lax.fori_loop(0, blocks, block, 0)

    def last_blocks(group):
        def forwards(index, carry):
            together(forward(index, group, index))
            return carry

        def backwards(index, carry):
            stage = backward(index, group, index)
            for _ in range(BLOCK_WINDOWS // 2 + 1):
                next(stage)
            for step in range(hidden_steps):
                @pl.when(index == step)
                def _():
                    for p in early:
                        sum_step(p, step + 1)

            together(stage)
            return carry

        lax.fori_loop(0, blocks, forwards, 0)
        for p in early:
            sum_step(p, 0)
        lax.fori_loop(0, blocks, backwards, 0)
        for step in range(blocks, hidden_steps):
            for p in early:
                sum_step(p, step + 1)

    def gather(pair, group):
        def assemble(own, strip, axis):
            if group in (0, GROUPS - 1):
                return lax.slice_in_dim(own, HALF_Y, HALF_Y + WY, axis=axis)
            if TOWARD[pair] == 1:
                return jnp.concatenate([strip, lax.slice_in_dim(own, 0, HALF_Y, axis=axis)], axis=axis)
            return jnp.concatenate(
                [lax.slice_in_dim(own, row_count - HALF_Y, row_count, axis=axis), strip], axis=axis
            )

        for a, target in enumerate((xw_ref, gw_ref)):
            def field(start, count, z, a=a):
                own = fields_ref[a, field_level(pair, z), start : start + count].astype(F32)
                strip = None
                if group in (1, 2):
                    strip = rows_in_ref[pair, a, z, start * HALF_Y : (start + count) * HALF_Y, :]
                    strip = unpack_strip(strip.astype(F32), count)
                return assemble(own, strip, 1)

            def western(c, z, a=a):
                own = cols_in_ref[a, field_level(pair, z), c].astype(F32)
                strip = None
                if group in (1, 2):
                    place = ((z * 2 + a) * HALF_X + c) * HALF_Y
                    strip = corner_in_ref[pair].astype(F32)[place : place + HALF_Y]
                return assemble(own, strip, 0)

            store_windows(field, western, target)

    def send_back(pair, slot):
        sent = 0 if TOWARD[pair] == 1 else HALF_Y
        for a in range(2):
            for start in range(0, col_count - HALF_X, PACKED_COLS):
                count = min(PACKED_COLS, col_count - HALF_X - start)
                first = (start + HALF_X) * CELLS
                cells = out_ref[slot, a, first : first + count * CELLS, :].astype(F32)
                for z in range(WZ):
                    places = [c * CELLS + z * WY + sent for c in range(count)]
                    rows_out_ref[
                        pair, a, z, start * HALF_Y : (start + count) * HALF_Y, :
                    ] = jnp.concatenate(
                        [cells[p : p + HALF_Y] for p in places], axis=0
                    ).astype(BF16)
        back_copy(pair).start()

    def group_step(group, carry):
        pair, slot = group_pair(group), lax.rem(group, 2)
        inner = (group == 0) | (group == GROUPS - 1)

        @pl.when(group == 0)
        def _():
            corner_copies[0].start()
            cols_copy.wait_recv()

        @pl.when(group >= 2)
        def _():
            out_copy(group - 2).wait()
            edge_copy(group - 2).wait_send()

        @pl.when(group == GROUPS - 1)
        def _():
            corner_back_copy(0).wait_send()

        @pl.when(inner)
        def _():
            gather(pair, 0)

        for straddling in range(2):
            @pl.when(group == 1 + straddling)
            def _():
                rows_copy(straddling).wait_recv()
                corner_copies[straddling].wait_recv()
                gather(straddling, 1 + straddling)

        bases = [-HALF_Y if step == 1 else row_count - HALF_Y for step in TOWARD]
        base = jnp.where(inner, HALF_Y, jnp.where(group == 1, bases[0], bases[1]))
        score_bias_ref[...] = mask_scores(
            bias_ref[...], pair, base, lat, band_count, crop_ref, row_count
        )
        @pl.when(group < GROUPS - 1)
        def _():
            plain_blocks(group)

        @pl.when(group == GROUPS - 1)
        def _():
            last_blocks(group)

        out_copy(group).start()
        edge_copy(group).start()

        for straddling in range(2):
            @pl.when(group == 1 + straddling)
            def _():
                corner_back_copy(straddling).start()
                rows_copy(straddling).wait_send()
                send_back(straddling, slot)

        return carry

    lax.fori_loop(0, GROUPS, group_step, 0)
    late_step(0)
    small_ref[VECTORS:, : HEADS * OFFSETS] = table_grad(score_sum_ref)
    early_steps = 2 * halvings - hidden_steps
    for k in range(max(early_steps, 4, len(bits))):
        if k < len(bits):
            small_copy = to_partner(small_ref, small_recv_ref.at[k], small_sems.at[k], bits[k])
            small_copy.start()
        if k < early_steps:
            for p in early:
                sum_step(p, hidden_steps + 1 + k)
        late_step(k + 1)
        if k < len(bits):
            small_copy.wait()
            small_ref[...] += small_recv_ref[k]
    for group in (2, 3):
        out_copy(group).wait()
        edge_copy(group).wait_send()
    corner_back_copy(1).wait_send()
    cols_copy.wait_send()
    for copy in corner_copies:
        copy.wait_send()
    for pair in range(2):
        back_copy(pair).wait()
        corner_back_copy(pair).wait_recv()
    for group in range(GROUPS):
        edge_copy(group).wait_recv()


def block_call(crop_rows, lead_hours, tokens, cotangent, constants):
    level_count, col_count, row_count, width = tokens.shape
    vmem = pl.BlockSpec(memory_space=pltpu.VMEM)
    cells = col_count * CELLS
    rows = BLOCK_WINDOWS * WINDOW
    edge = -(-EDGE // 16) * 16
    blocks = col_count // WX // BLOCK_WINDOWS
    pairs = level_count // WZ
    strips = (pairs, 2, WZ, packed_rows(col_count), width)
    grad_rows = (4 * width + 2 * constants[-2].shape[1]) * (width // LANES)
    bits, halvings = sum_bits()
    parts = sum_parts(width, constants[-2].shape[1])
    more = max(1, len(bits) - halvings)
    late_rows = parts[2][1] // 2
    shard = max([count >> halvings for _, count in parts] + [late_rows // peer_sizes()[2]])
    half_rows = sum(halved(count, halvings)[1][-1] for _, count in parts)
    sends = pltpu.SemaphoreType.DMA
    return pl.pallas_call(
        block_kernel,
        in_specs=[pl.BlockSpec(memory_space=pltpu.SMEM)] * 2 + [ANY, ANY] + [vmem] * len(constants),
        out_specs=[ANY] * 4 + [vmem] * 3,
        out_shape=[
            shape_of((2, GROUPS, cells, width), BF16),
            shape_of(strips, BF16),
            shape_of((GROUPS, 2, edge, width), BF16),
            shape_of((pairs, 2, edge, width), BF16),
            shape_of((grad_rows, LANES), BF16),
            shape_of((VECTORS + TABLE_ROWS, width), F32),
            shape_of((width, LANES), F32),
        ],
        scratch_shapes=[
            pltpu.VMEM((WINDOW, SCORES), F32),
            pltpu.VMEM((VECTORS, width), F32),
            pltpu.VMEM((grad_rows, LANES), F32),
            pltpu.VMEM((half_rows, LANES), BF16),
            pltpu.VMEM((half_rows, LANES), BF16),
            pltpu.VMEM((2, len(parts), more, shard, LANES), BF16),
            pltpu.VMEM((max(1, len(bits)), VECTORS + TABLE_ROWS, width), F32),
            pltpu.VMEM((late_rows, LANES), BF16),
            pltpu.VMEM((peer_sizes()[2], late_rows // peer_sizes()[2], LANES), BF16),
            pltpu.VMEM((2,) + tokens.shape, BF16),
            pltpu.VMEM(strips, BF16),
            pltpu.VMEM(strips, BF16),
            pltpu.VMEM((2, level_count, HALF_X, row_count, width), BF16),
            pltpu.VMEM((pairs, edge, width), BF16),
            pltpu.VMEM((pairs, edge, width), BF16),
            pltpu.VMEM((2, 2, cells, width), BF16),
            pltpu.VMEM((WINDOW, SCORES), F32),
            pltpu.VMEM((cells, width), F32),
            pltpu.VMEM((cells, width), F32),
            pltpu.VMEM((blocks, rows, 3 * width), BF16),
            pltpu.VMEM((blocks, BLOCK_WINDOWS, WINDOW, SCORES), F32),
            pltpu.VMEM((blocks, rows, width), BF16),
            pltpu.VMEM((blocks, rows, width), F32),
            pltpu.VMEM((rows, 3 * width), BF16),
            pltpu.VMEM((WINDOW, SCORES), F32),
            sends((2 * level_count,)), sends((3, 2)), sends((pairs, 2)), sends((pairs, 2)),
            sends((GROUPS, 2)), sends((pairs, 2)), sends((GROUPS,)),
            sends((len(parts), len(bits) + halvings, 2)), sends((max(1, len(bits)), 2)),
            sends((2, peer_sizes()[2], 2)),
        ],
        cost_estimate=pl.CostEstimate(
            flops=GROUPS * cells * 5_200_000, bytes_accessed=32 * 2**20, transcendentals=0
        ),
        compiler_params=pltpu.CompilerParams(
            collective_id=1, has_side_effects=True, vmem_limit_bytes=VMEM_LIMIT
        ),
    )(crop_rows, lead_hours, tokens, cotangent, *constants)


def merge_kernel(
    inner_ref, straddle_ref, rows_ref, inner_edge_ref, straddle_edge_ref, corner_ref,
    grad_ref, small_ref, context_ref, *out_refs,
):
    fields, grads, vectors, sems = out_refs[:2], out_refs[2:7], out_refs[7:13], out_refs[-1]
    staged = out_refs[13:-1]
    _, col_count, row_count, width = fields[0].shape
    step = pl.program_id(0)

    def piece(rows_of, a, first_col, count, first, size):
        block = rows_of(a)[first_col * CELLS : (first_col + count) * CELLS, :].astype(F32)
        return block.reshape(count, CELLS, width)[:, first : first + size]

    straddle, inner = lambda a: straddle_ref.at[a, 0], lambda a: inner_ref.at[a, 0]
    straddle_edge, inner_edge, corner = (
        lambda a, ref=ref: ref.at[0, a] for ref in (straddle_edge_ref, inner_edge_ref, corner_ref)
    )
    for pair, z in ((0, 0), (0, 1), (1, 0), (1, 1)):
        @pl.when(step == pair * WZ + z)
        def _():
            first = z * WY
            kept, sent = (HALF_Y, 0) if TOWARD[pair] == 1 else (0, HALF_Y)

            def in_order(own, inner_rows, back):
                parts = [own, inner_rows, back] if TOWARD[pair] == 1 else [back, inner_rows, own]
                return jnp.concatenate(parts, axis=1).astype(BF16)

            for a, field in enumerate(fields):
                for start in range(0, col_count - HALF_X, PACKED_COLS):
                    count = min(PACKED_COLS, col_count - HALF_X - start)
                    strip = rows_ref[0, a, 0, start * HALF_Y : (start + count) * HALF_Y, :]
                    field[0, start : start + count] = in_order(
                        piece(straddle, a, start + HALF_X, count, first + kept, HALF_Y),
                        piece(inner, a, start + HALF_X, count, first, WY),
                        unpack_strip(strip.astype(F32), count),
                    )
                field[0, col_count - HALF_X :] = in_order(
                    piece(straddle_edge, a, 0, HALF_X, first + kept, HALF_Y),
                    piece(inner_edge, a, 0, HALF_X, first, WY),
                    piece(corner, a, 0, HALF_X, first + sent, HALF_Y),
                )

    grad_qkv, grad_proj, grad_up, grad_down, grad_mod = staged

    def leave(index):
        return pltpu.make_async_copy(staged[index], grads[index], sems.at[index])

    def slab(index):
        per_slab = width // LANES
        return jnp.concatenate([
            grad_ref[j * width : (j + 1) * width, :].astype(F32)
            for j in range(index * per_slab, (index + 1) * per_slab)
        ], axis=1)

    @pl.when(step == 0)
    def _():
        for j in range(3):
            grad_qkv[:, j * width : (j + 1) * width] = slab(j)
        grad_proj[...] = slab(3)
        leave(0).start()
        leave(1).start()
        for part in range(4):
            row = small_ref[part : part + 1, :]
            for j in range(0, width, LANES):
                grad_mod[:, part * width + j : part * width + j + LANES] = (
                    context_ref[...] * row[:, j : j + LANES]
                )
        leave(4).start()

    @pl.when(step == 1)
    def _():
        for j in range(grad_up.shape[1] // width):
            grad_up[:, j * width : (j + 1) * width] = slab(4 + j)
        leave(2).start()

    @pl.when(step == 2)
    def _():
        for j in range(grad_down.shape[0] // width):
            grad_down[j * width : (j + 1) * width, :] = slab(8 + j).T
        leave(3).start()

    @pl.when(step == 3)
    def _():
        mod_bias, proj_bias, down_bias, q_bias, v_bias, up_bias = vectors
        mod_bias[...] = jnp.concatenate([small_ref[i : i + 1, :] for i in range(4)], axis=1)
        up_bias[...] = jnp.concatenate([small_ref[i : i + 1, :] for i in range(9, 13)], axis=1)
        for ref, i in ((proj_bias, 4), (down_bias, 5), (q_bias, 6), (v_bias, 8)):
            ref[...] = small_ref[i : i + 1, :]
        for index in range(len(staged)):
            leave(index).wait()


def merge(field_shape, hidden_width, windows, rows_back, edge_back, corner_back, grad, small, context):
    level_count, col_count, row_count, width = field_shape

    def level_of(i):
        return (i + WZ // 2) % level_count

    def group_of(pair, straddles):
        return 1 + pair if straddles else (GROUPS - 1) * pair

    def windows_of(straddles):
        return pl.BlockSpec(
            (2, 1) + windows.shape[2:], lambda i: (0, group_of(i // WZ, straddles), 0, 0)
        )

    def edge_of(straddles):
        return pl.BlockSpec(
            (1,) + edge_back.shape[1:], lambda i: (group_of(i // WZ, straddles), 0, 0, 0)
        )

    shapes = [
        (width, 3 * width), (width, width), (width, hidden_width), (hidden_width, width),
        (width, 4 * width),
    ]
    vectors = [(1, 4 * width), (1, width), (1, width), (1, width), (1, width), (1, hidden_width)]
    field = pl.BlockSpec((1,) + field_shape[1:], lambda i: (level_of(i), 0, 0, 0))
    return pl.pallas_call(
        merge_kernel,
        grid=(level_count,),
        in_specs=[
            windows_of(False), windows_of(True),
            pl.BlockSpec((1, 2, 1) + rows_back.shape[3:], lambda i: (i // WZ, 0, i % WZ, 0, 0)),
            edge_of(False), edge_of(True),
            pl.BlockSpec((1,) + corner_back.shape[1:], lambda i: (i // WZ, 0, 0, 0)),
        ] + [whole(v.shape) for v in (grad, small, context)],
        out_specs=[field, field] + [ANY] * len(shapes) + [whole(s) for s in vectors],
        out_shape=[shape_of(field_shape, BF16)] * 2 + [shape_of(s, F32) for s in shapes + vectors],
        scratch_shapes=[pltpu.VMEM(s, F32) for s in shapes] + [
            pltpu.SemaphoreType.DMA((len(shapes),))
        ],
        compiler_params=pltpu.CompilerParams(vmem_limit_bytes=VMEM_LIMIT),
    )(windows, windows, rows_back, edge_back, edge_back, corner_back, grad, small, context)


def on_device(
    tokens, cotangent, w_qkv, q_bias, v_bias, w_proj, b_proj, w_up, b_up, w_down, b_down,
    w_mod, b_mod, rel_table, crop_rows, lead_hours,
):
    fields = [field.transpose(0, 2, 1, 3) for field in (tokens, cotangent)]
    table = rel_table.transpose(1, 3, 0, 2)
    windows, rows_back, edge_back, corner_back, grad, small, context = block_call(
        crop_rows, lead_hours, *fields, (
            w_mod, b_mod, b_proj, b_down, q_bias, v_bias, b_up, table, w_qkv, w_proj, w_up, w_down,
        )
    )
    (
        mixed, token_grad, grad_qkv, grad_proj, grad_up, grad_down, grad_mod, grad_mod_bias,
        grad_proj_bias, grad_down_bias, grad_q_bias, grad_v_bias, grad_up_bias,
    ) = merge(
        fields[0].shape, w_up.shape[1], windows, rows_back, edge_back, corner_back, grad, small, context
    )
    table_sum = small[VECTORS : VECTORS + 2 * WY - 1, : HEADS * OFFSETS][::-1]
    grad_table = table_sum.reshape(2 * WY - 1, 2 * WZ - 1, 2 * WX - 1, HEADS).transpose(3, 1, 0, 2)
    return (
        mixed.transpose(0, 2, 1, 3),
        token_grad.transpose(0, 2, 1, 3),
        grad_qkv,
        grad_q_bias[0],
        grad_v_bias[0],
        grad_proj,
        grad_proj_bias[0],
        grad_up,
        grad_up_bias[0],
        grad_down,
        grad_down_bias[0],
        grad_mod,
        grad_mod_bias[0],
        grad_table,
    )


def solution(mesh):
    split = P(None, "lat", "lon", None)
    return jax.shard_map(
        on_device,
        mesh=mesh,
        in_specs=(split, split) + (P(),) * 14,
        out_specs=(split, split) + (P(),) * 12,
        check_vma=False,
    )
```

```python
import functools
import math

import jax
import jax.numpy as jnp
from jax import lax
from jax.experimental import pallas as pl
from jax.experimental.pallas import tpu as pltpu
from jax.sharding import PartitionSpec as P

WZ = 2
WY = 12
WX = 6
CELLS = WZ * WY
WINDOW = CELLS * WX
HEADS = 4
SCORES = HEADS * WINDOW
HALF_Y = WY // 2
HALF_X = WX // 2
BLOCK_WINDOWS = 5
OFFSETS = (2 * WZ - 1) * (2 * WX - 1)
VECTORS = 16
LANES = 128
TABLE_ROWS = 2 * WY
EDGE = HALF_X * CELLS
PACKED_COLS = 8

NORM_EPSILON = 1e-05
MASKED_SCORE = -1000000000.0
F32 = jnp.float32
BF16 = jnp.bfloat16
MESH = pl.DeviceIdType.MESH
ANY = pl.BlockSpec(memory_space=pl.ANY)
VMEM_LIMIT = 60 * 2**20


def dot_nn(left, right):
    return lax.dot_general(left, right, (((1,), (0,)), ((), ())), preferred_element_type=F32)


def dot_nt(left, right):
    return lax.dot_general(left, right, (((1,), (1,)), ((), ())), preferred_element_type=F32)


def dot_tn(left, right):
    return lax.dot_general(left, right, (((0,), (0,)), ((), ())), preferred_element_type=F32)


def iota(shape, axis):
    return lax.broadcasted_iota(jnp.int32, shape, axis)


def whole(shape, buffers=1):
    return pl.BlockSpec(
        shape, lambda *_: (0,) * len(shape), pipeline_mode=pl.Buffered(buffers)
    )


def shape_of(shape, dtype):
    return jax.ShapeDtypeStruct(shape, dtype)


def packed_rows(col_count):
    return -(-col_count * HALF_Y // 16) * 16


def offset_pick(key_x, key_z):
    lane = iota((HEADS * OFFSETS, SCORES), 1)
    head, rest = lane // WINDOW, lane % WINDOW
    query_x, query_z = rest // CELLS, (rest % CELLS) // WY
    offset_z, offset_x = query_z - key_z + WZ - 1, query_x - key_x + WX - 1
    place = (offset_z * (2 * WX - 1) + offset_x) * HEADS + head
    return iota((HEADS * OFFSETS, SCORES), 0) == place


def setup_kernel(
    lead_ref, w_mod_ref, b_mod_ref, b_proj_ref, b_down_ref, q_bias_ref, v_bias_ref, b_up_ref,
    table_ref, bias_ref, vec_ref, context_ref,
):
    width = w_mod_ref.shape[0]
    half = width // 2
    lanes = context_ref.shape[1]
    fraction = iota((half, lanes), 0).astype(F32) / half
    angles = lead_ref[0].astype(F32) * jnp.exp(-math.log(1000.0) * fraction)
    waves = jnp.concatenate([jnp.sin(angles), jnp.cos(angles)], axis=0)
    context = waves * (1.0 / (1.0 + jnp.exp(-waves)))
    context_ref[...] = context
    for part in range(4):
        pieces = []
        for j in range(width // lanes):
            start = part * width + j * lanes
            pieces.append(
                jnp.sum(context * w_mod_ref[:, start : start + lanes].astype(F32), axis=0, keepdims=True)
            )
        vec_ref[part : part + 1, :] = (
            jnp.concatenate(pieces, axis=1)
            + b_mod_ref[part * width : (part + 1) * width].astype(F32)[None]
        )
    vec_ref[4:, :] = jnp.zeros((VECTORS - 4, width), F32)
    for i, ref in ((4, b_proj_ref), (5, b_down_ref), (6, q_bias_ref), (8, v_bias_ref)):
        vec_ref[i : i + 1, :] = ref[...].astype(F32)[None]
    for j in range(b_up_ref.shape[0] // width):
        vec_ref[9 + j : 10 + j, :] = b_up_ref[j * width : (j + 1) * width].astype(F32)[None]

    offsets_y = 2 * WY - 1
    backwards = iota((TABLE_ROWS, offsets_y), 0) + iota((TABLE_ROWS, offsets_y), 1) == offsets_y - 1
    table = jnp.concatenate(
        [table_ref[z, x].astype(F32) for z in range(2 * WZ - 1) for x in range(2 * WX - 1)], axis=0
    ).astype(BF16)
    table = dot_nt(backwards.astype(BF16), table).astype(BF16)
    query_y = iota((WY, SCORES), 1) % WY
    for key_x in range(WX):
        for key_z in range(WZ):
            spread = dot_nn(table, offset_pick(key_x, key_z).astype(BF16))
            rows = spread[WY - 1 : 2 * WY - 1]
            for y in range(1, WY):
                rows = jnp.where(query_y == y, spread[WY - 1 - y : 2 * WY - 1 - y], rows)
            start = key_x * CELLS + key_z * WY
            bias_ref[start : start + WY, :] = rows


def set_up(lead_hours, w_mod, vectors, table):
    width = w_mod.shape[0]
    vmem = pl.BlockSpec(memory_space=pltpu.VMEM)
    return pl.pallas_call(
        setup_kernel,
        in_specs=[pl.BlockSpec(memory_space=pltpu.SMEM)] + [vmem] * (2 + len(vectors)),
        out_specs=[vmem] * 3,
        out_shape=[
            shape_of((WINDOW, SCORES), F32),
            shape_of((VECTORS, width), F32),
            shape_of((width, 128), F32),
        ],
        compiler_params=pltpu.CompilerParams(vmem_limit_bytes=VMEM_LIMIT),
    )(lead_hours, w_mod, *vectors, table)


def table_grad(score_sum_ref):
    query_y = iota((WY, SCORES), 1) % WY
    total = jnp.zeros((TABLE_ROWS, HEADS * OFFSETS), F32)
    for key_x in range(WX):
        for key_z in range(WZ):
            start = key_x * CELLS + key_z * WY
            rows = score_sum_ref[start : start + WY, :]
            spread = jnp.zeros((TABLE_ROWS, SCORES), F32)
            for y in range(WY):
                own = jnp.where(query_y == y, rows, 0.0)
                pads = (WY - 1 - y, TABLE_ROWS - (2 * WY - 1 - y))
                parts = [jnp.zeros((p, SCORES), F32) for p in pads]
                spread = spread + jnp.concatenate(
                    ([parts[0]] if pads[0] else []) + [own, parts[1]], axis=0
                )
            pick = offset_pick(key_x, key_z).astype(BF16)
            high = spread.astype(BF16)
            low = (spread - high.astype(F32)).astype(BF16)
            total = total + dot_nt(high, pick) + dot_nt(low, pick)
    return total


def halved(rows, count):
    sizes = [rows >> (i + 1) for i in range(count)]
    return sizes, [sum(sizes[:i]) for i in range(count + 1)]


def sum_bits():
    bits = [("lon", 0), ("lon", 1), ("lat", 0), ("lat", 1), ("lat", 2)]
    bits = [b for b in bits if 2 ** b[1] < lax.axis_size(b[0])]
    bits += [("lat", b) for b in range(3, lax.axis_size("lat").bit_length() - 1)]
    bits += [("lon", b) for b in range(2, lax.axis_size("lon").bit_length() - 1)]
    return bits, min(5, len(bits))


def peer_sizes():
    lons, lats = lax.axis_size("lon") // 2, min(8, lax.axis_size("lat"))
    return lons, lats, lons * lats


def sum_parts(width, hidden_width):
    qkv_rows = 3 * width * (width // LANES)
    rest = (width + 2 * hidden_width) * (width // LANES)
    first = -(-rest // 1024) * 512
    return [(qkv_rows, first), (qkv_rows + first, rest - first), (0, qkv_rows)]


def row_mean(values):
    return jnp.mean(values, axis=-1, keepdims=True)


def centered(values):
    return values - row_mean(values)


def norm_centered(center):
    inverse = lax.rsqrt(row_mean(center * center) + NORM_EPSILON)
    return center * inverse, inverse


def norm_back(grad, normed, inverse):
    return inverse * (grad - row_mean(grad) - normed * row_mean(grad * normed))


def gelu_both(values):
    gauss_cdf = 0.5 * (1.0 + lax.erf(values * math.sqrt(0.5)))
    density = jnp.exp(values * values * -0.5) * (1.0 / math.sqrt(2.0 * math.pi))
    return values * gauss_cdf, gauss_cdf + values * density


def by_head(values):
    width = values.shape[-1] // HEADS
    lane_head = iota(values.shape, 1) // width
    zero = jnp.zeros_like(values)
    return jnp.concatenate([jnp.where(lane_head == h, values, zero) for h in range(HEADS)], axis=0)


def own_head(stacked):
    cells = stacked.shape[0] // HEADS
    width = stacked.shape[-1] // HEADS
    lane_head = iota((cells, stacked.shape[-1]), 1) // width
    picked = stacked[:cells]
    for h in range(1, HEADS):
        picked = jnp.where(lane_head == h, stacked[h * cells : (h + 1) * cells], picked)
    return picked


def store_windows(field, western, out_ref):
    width = out_ref.shape[1]
    for c in range(HALF_X):
        out_ref[c * CELLS : (c + 1) * CELLS, :] = jnp.concatenate(
            [western(c, z) for z in range(WZ)], axis=0
        )
    own_cols = out_ref.shape[0] // CELLS - HALF_X
    for start in range(0, own_cols, PACKED_COLS):
        count = min(PACKED_COLS, own_cols - start)
        both = jnp.concatenate([field(start, count, z) for z in range(WZ)], axis=1)
        first = (start + HALF_X) * CELLS
        out_ref[first : first + count * CELLS, :] = both.reshape(count * CELLS, width)


def unpack_strip(rows, count):
    return jnp.stack([rows[c * HALF_Y : (c + 1) * HALF_Y] for c in range(count)], axis=0)


def mask_scores(bias, level_wraps, base, band, band_count, crop_ref, row_count):
    crops = [
        crop_ref[lax.rem(band + step + band_count, band_count)] for step in (-1, 0, 1)
    ]
    firsts = [
        (lax.rem(band + step + band_count, band_count) == 0).astype(jnp.int32) for step in (0, 1)
    ]

    def parts(cell):
        z, row = (cell % CELLS) // WY, base + cell % WY
        part = 2 * jnp.where(z == WZ - 1, level_wraps, 0)
        part = part + jnp.where((row >= 0) & (row < HALF_Y), firsts[0], 0)
        part = part + jnp.where((row >= row_count) & (row < row_count + HALF_Y), firsts[1], 0)
        crop = jnp.where(row < 0, crops[0], jnp.where(row < row_count, crops[1], crops[2]))
        return part, (row + row_count) % row_count >= row_count - crop

    key = iota(bias.shape, 0)
    query = iota(bias.shape, 1) % WINDOW
    key_part, key_valid = parts(key)
    query_part, _ = parts(query)
    allowed = (key_part == query_part) & (key_valid | (key == query))
    return jnp.where(allowed, bias, bias + MASKED_SCORE)


GROUPS = 4
TOWARD = (1, 1)


def group_pair(group):
    return group // 2


def field_level(pair, z):
    return lax.rem(WZ * pair + z + WZ // 2, 2 * WZ)


def block_kernel(
    crop_ref, tokens_ref, cotangent_ref, bias_ref, vec_ref, w_qkv_ref, w_proj_ref, w_up_ref, w_down_ref,
    win_ref, rows_back_ref, edge_back_ref, corner_back_ref, sum_ref, small_ref,
    grad_ref, send_ref, recv_ref, more_ref, small_recv_ref, scatter_ref, pieces_ref, proj_centered_ref,
    down_centered_ref, fields_ref, rows_out_ref, rows_in_ref, cols_in_ref, corner_out_ref, corner_in_ref, out_ref,
    score_bias_ref, xw_ref, gw_ref, qkv_ref, prob_ref, att_ref, middle_grad_ref, dqkv_ref,
    score_sum_ref,
    field_sems, halo_sems, rows_sems, back_sems, edge_sems, corner_sems, out_sems, sum_sems, small_sems,
    peer_sems,
):
    width = vec_ref.shape[1]
    hidden_width = w_up_ref.shape[1]
    _, level_count, col_count, row_count, _ = fields_ref.shape
    band_count = crop_ref.shape[0]
    score_scale = (width // HEADS) ** -0.5
    lat, lon = lax.axis_index("lat"), lax.axis_index("lon")
    lat_size, lon_size = lax.axis_size("lat"), lax.axis_size("lon")

    def device(lat_step, lon_step):
        return (
            lax.rem(lat + lat_step + lat_size, lat_size), lax.rem(lon + lon_step + lon_size, lon_size)
        )

    steps = [(0, 1)] + [(t, lon_step) for t in sorted(set(TOWARD)) for lon_step in (0, 1)]
    barrier = pltpu.get_barrier_semaphore()
    for lat_step, lon_step in steps:
        for sign in (1, -1):
            pl.semaphore_signal(
                barrier, inc=1, device_id=device(sign * lat_step, sign * lon_step), device_id_type=MESH
            )

    bits, halvings = sum_bits()
    own_bit, partner = {}, {}
    for axis, bit in bits:
        place = lat if axis == "lat" else lon
        own_bit[axis, bit] = (place // 2**bit) % 2
        moved = place + 2**bit * (1 - 2 * own_bit[axis, bit])
        partner[axis, bit] = (moved, lon) if axis == "lat" else (lat, moved)
        pl.semaphore_signal(barrier, inc=1, device_id=partner[axis, bit], device_id_type=MESH)
    peer_lons, peer_lats, peer_count = peer_sizes()
    my_peer = lon // 2 + peer_lons * (lat % peer_lats)

    def peer(step):
        index = (my_peer + step) % peer_count
        return index, (
            (lat // peer_lats) * peer_lats + index // peer_lons, 2 * (index % peer_lons) + lon % 2
        )

    for step in range(1, peer_count):
        pl.semaphore_signal(barrier, inc=1, device_id=peer(step)[1], device_id_type=MESH)

    loads = []
    for level in (1, 2, 3, 0):
        for a, ref in enumerate((tokens_ref, cotangent_ref)):
            loads.append(pltpu.make_async_copy(
                ref.at[level], fields_ref.at[a, level], field_sems.at[len(loads)]
            ))
            loads[-1].start()

    def remote(source, target, sems, lat_step, lon_step):
        return pltpu.make_async_remote_copy(
            src_ref=source, dst_ref=target, send_sem=sems.at[0], recv_sem=sems.at[1],
            device_id=device(lat_step, lon_step), device_id_type=MESH,
        )

    last_cols = fields_ref.at[:, :, pl.ds(col_count - HALF_X, HALF_X)]
    cols_copy = remote(last_cols, cols_in_ref, halo_sems.at[0], 0, 1)
    corner_copies = [
        remote(corner_out_ref.at[pair], corner_in_ref.at[pair], halo_sems.at[1 + pair], TOWARD[pair], 1)
        for pair in range(2)
    ]

    def rows_copy(pair):
        return remote(
            rows_out_ref.at[pair], rows_in_ref.at[pair], rows_sems.at[pair], TOWARD[pair], 0
        )

    def back_copy(pair):
        return remote(
            rows_out_ref.at[pair], rows_back_ref.at[pair], back_sems.at[pair], -TOWARD[pair], 0
        )

    def edge_rows(group):
        return out_ref.at[lax.rem(group, 2), :, pl.ds(0, edge_back_ref.shape[2])]

    def edge_copy(group):
        return remote(edge_rows(group), edge_back_ref.at[group], edge_sems.at[group], 0, -1)

    def corner_back_copy(pair):
        return remote(
            edge_rows(1 + pair), corner_back_ref.at[pair], corner_sems.at[pair], -TOWARD[pair], -1
        )

    def out_copy(group):
        return pltpu.make_async_copy(
            out_ref.at[lax.rem(group, 2)], win_ref.at[:, group], out_sems.at[group]
        )

    for pair in range(2):
        corners = []
        sent = slice(row_count - HALF_Y, row_count) if TOWARD[pair] == 1 else slice(0, HALF_Y)
        for z in range(WZ):
            level = (WZ * pair + z + WZ // 2) % level_count
            for a in range(2):
                if pair == 0:
                    loads[z * 2 + a].wait()
                for start in range(0, col_count, PACKED_COLS):
                    count = min(PACKED_COLS, col_count - start)
                    block = fields_ref[a, level, start : start + count].astype(F32)
                    packed = [block[c, sent] for c in range(count)]
                    rows_out_ref[
                        pair, a, z, start * HALF_Y : (start + count) * HALF_Y, :
                    ] = jnp.concatenate(packed, axis=0).astype(BF16)
                block = fields_ref[a, level, col_count - HALF_X :].astype(F32)
                corners += [block[c, sent] for c in range(HALF_X)]
        spare = corner_out_ref.shape[1] - HALF_Y * len(corners)
        corners.append(jnp.zeros((spare, width), F32))
        corner_out_ref[pair] = jnp.concatenate(corners, axis=0).astype(BF16)
        if pair == 0:
            pl.semaphore_wait(barrier, 2 * len(steps) + len(bits) + peer_count - 1)
            rows_copy(0).start()
            for load in loads[2 * WZ :]:
                load.wait()
            cols_copy.start()

    grad_ref[...] = jnp.zeros_like(grad_ref)
    small_ref[...] = jnp.zeros_like(small_ref)
    score_sum_ref[...] = jnp.zeros_like(score_sum_ref)
    rows = BLOCK_WINDOWS * WINDOW
    shift_one, scale_one, shift_two, scale_two, b_proj, b_down = [
        vec_ref[i : i + 1, :] for i in range(6)
    ]
    b_proj, b_down = centered(b_proj), centered(b_down)
    for centered_ref, ref in ((proj_centered_ref, w_proj_ref), (down_centered_ref, w_down_ref)):
        centered_ref[...] = centered(ref[...].astype(F32)).astype(BF16)
    qkv_shift = jnp.concatenate([vec_ref[i : i + 1, :] for i in range(6, 9)], axis=1)
    b_up = jnp.concatenate([vec_ref[i : i + 1, :] for i in range(9, 13)], axis=1)

    def add_grad(first, value):
        for j in range(value.shape[1] // LANES):
            grad_ref[(first + j) * width : (first + j + 1) * width, :] += value[
                :, j * LANES : (j + 1) * LANES
            ]

    parts = sum_parts(width, hidden_width)
    sizes, send_starts = zip(*[halved(count, halvings) for _, count in parts])
    orders, lows = [], []
    for p, (first, _) in enumerate(parts):
        order = list(bits[:halvings])
        if p == 1 and halvings > 2:
            order[1], order[2] = order[2], order[1]
        orders.append(order)
        lows.append([first])
        for s, bit in enumerate(order):
            lows[p].append(lows[p][s] + own_bit[bit] * sizes[p][s])

    def to_partner(source, target, sems, bit):
        return pltpu.make_async_remote_copy(
            src_ref=source, dst_ref=target, send_sem=sems.at[0], recv_sem=sems.at[1],
            device_id=partner[bit], device_id_type=MESH,
        )

    def half_place(p, s):
        return pl.ds(sum(starts[-1] for starts in send_starts[:p]) + send_starts[p][s], sizes[p][s])

    def half_copy(p, s):
        place = half_place(p, s)
        return to_partner(send_ref.at[place], recv_ref.at[place], sum_sems.at[p, s], orders[p][s])

    def halve(p, s):
        size, bit = sizes[p][s], orders[p][s]
        away = pl.multiple_of(lows[p][s] + (1 - own_bit[bit]) * size, 16)
        send_ref[half_place(p, s), :] = grad_ref[pl.ds(away, size), :].astype(BF16)
        half_copy(p, s).start()

    def add_half(p, s):
        half_copy(p, s).wait()
        here = pl.ds(pl.multiple_of(lows[p][s + 1], 16), sizes[p][s])
        grad_ref[here, :] += recv_ref[half_place(p, s), :].astype(F32)

    def shard_done(p):
        here = pl.ds(pl.multiple_of(lows[p][halvings], 16), sizes[p][-1])
        sum_ref[here, :] = grad_ref[here, :].astype(BF16)
        exchange_shard(p, here, sizes[p][-1])

    def exchange_shard(p, here, count):
        for s in range(halvings, len(bits)):
            mine = more_ref.at[0, p, s - halvings, pl.ds(0, count)]
            theirs = more_ref.at[1, p, s - halvings, pl.ds(0, count)]
            mine[...] = sum_ref[here, :]
            copy = to_partner(mine, theirs, sum_sems.at[p, s], bits[s])
            copy.start()
            copy.wait()
            sum_ref[here, :] = (mine[...].astype(F32) + theirs[...].astype(F32)).astype(BF16)

    def give_copy(p, s):
        here = sum_ref.at[pl.ds(pl.multiple_of(lows[p][s + 1], 16), sizes[p][s]), :]
        return to_partner(here, here, sum_sems.at[p, len(bits) + s], orders[p][s])

    def sum_step(p, k):
        if 1 <= k <= halvings:
            add_half(p, k - 1)
        if k < halvings:
            halve(p, k)
        if k == halvings:
            shard_done(p)
        if halvings < k <= 2 * halvings:
            give_copy(p, 2 * halvings - k).wait()
        if halvings <= k < 2 * halvings:
            give_copy(p, 2 * halvings - 1 - k).start()

    early, late = (0, 1), 2
    hidden_steps = min(4, halvings)

    piece = sizes[late][0] // peer_count

    def piece_place(index):
        return pl.ds(pl.multiple_of(lows[late][1] + index * piece, 16), piece)

    def scatter_copy(step):
        index, there = peer(step)
        return pltpu.make_async_remote_copy(
            src_ref=scatter_ref.at[pl.ds(pl.multiple_of(index * piece, 16), piece), :],
            dst_ref=pieces_ref.at[step], send_sem=peer_sems.at[0, step, 0],
            recv_sem=peer_sems.at[0, step, 1], device_id=there, device_id_type=MESH,
        )

    def gather_copy(step):
        mine = sum_ref.at[piece_place(my_peer), :]
        return pltpu.make_async_remote_copy(
            src_ref=mine, dst_ref=mine, send_sem=peer_sems.at[1, step, 0],
            recv_sem=peer_sems.at[1, step, 1], device_id=peer(step)[1], device_id_type=MESH,
        )

    def late_step(k):
        others = range(1, peer_count)
        if k == 0:
            halve(late, 0)
        elif k == 1:
            add_half(late, 0)
            half = pl.ds(pl.multiple_of(lows[late][1], 16), sizes[late][0])
            scatter_ref[...] = grad_ref[half, :].astype(BF16)
            for step in others:
                scatter_copy(step).start()
        elif k == 2:
            total = grad_ref[piece_place(my_peer), :]
            for step in others:
                scatter_copy(step).wait()
                total = total + pieces_ref[step].astype(F32)
            sum_ref[piece_place(my_peer), :] = total.astype(BF16)
            exchange_shard(late, piece_place(my_peer), piece)
            for step in others:
                gather_copy(step).start()
        elif k == 3:
            for step in others:
                gather_copy(step).wait()
            give_copy(late, 0).start()
        elif k == 4:
            give_copy(late, 0).wait()

    def column_sums(values):
        return jnp.sum(values, axis=0, keepdims=True)

    def forward(index, group, kept):
        slot = lax.rem(group, 2)
        here = pl.ds(pl.multiple_of(index * rows, 16), rows)
        x32 = xw_ref[here, :]
        x = x32.astype(BF16)
        qkv_ref[kept] = (dot_nn(x, w_qkv_ref[...]) + qkv_shift).astype(BF16)
        for w in range(BLOCK_WINDOWS):
            cells = pl.ds(w * WINDOW, WINDOW)
            queries = by_head(qkv_ref[kept, cells, :width] * BF16(score_scale))
            scores = dot_nt(qkv_ref[kept, cells, width : 2 * width], queries) + score_bias_ref[...]
            top = jnp.max(scores, axis=0, keepdims=True)
            exps = jnp.exp(scores - top)
            prob = exps * (1.0 / jnp.sum(exps, axis=0, keepdims=True))
            prob_ref[kept, w] = prob
            att_ref[kept, cells, :] = own_head(
                dot_tn(prob.astype(BF16), qkv_ref[kept, cells, 2 * width :])
            ).astype(BF16)
            yield

        att = att_ref[kept]
        branch = dot_nn(att, proj_centered_ref[...]) + b_proj
        yield
        norm_one, inverse_one = norm_centered(branch)
        middle = x32 + norm_one * (1.0 + scale_one) + shift_one
        middle_low = middle.astype(BF16)
        pre = dot_nn(middle_low, w_up_ref[...]) + b_up
        yield
        hidden, slope = gelu_both(pre)
        hidden = hidden.astype(BF16)
        second = dot_nn(hidden, down_centered_ref[...]) + b_down
        yield
        norm_two, inverse_two = norm_centered(second)
        out_ref[slot, 0, here, :] = (middle + norm_two * (1.0 + scale_two) + shift_two).astype(BF16)

        g = gw_ref[here, :]
        yield
        second_low = norm_back(g * (1.0 + scale_two), norm_two, inverse_two).astype(BF16)
        pre_grad = dot_nt(second_low, w_down_ref[...]) * slope
        yield
        add_grad(16, dot_tn(second_low, hidden))
        yield
        pre_low = pre_grad.astype(BF16)
        up_sums = column_sums(pre_grad)
        middle_grad = g + dot_nt(pre_low, w_up_ref[...])
        yield
        add_grad(8, dot_tn(middle_low, pre_low))
        yield
        branch_low = norm_back(middle_grad * (1.0 + scale_one), norm_one, inverse_one).astype(BF16)
        att_ref[kept] = dot_nt(branch_low, w_proj_ref[...]).astype(BF16)
        yield
        add_grad(6, dot_tn(att, branch_low))
        middle_grad_ref[kept] = middle_grad
        sums = [
            column_sums(middle_grad), column_sums(middle_grad * norm_one), column_sums(g),
            column_sums(g * norm_two), column_sums(branch_low.astype(F32)),
            column_sums(second_low.astype(F32)),
        ]
        sums += [jnp.zeros((1, width), F32)] * 3
        sums += [up_sums[:, j * width : (j + 1) * width] for j in range(hidden_width // width)]
        sums += [jnp.zeros((VECTORS - len(sums), width), F32)]
        small_ref[:VECTORS, :] += jnp.concatenate(sums, axis=0)

    def backward(index, group, kept):
        slot = lax.rem(group, 2)
        here = pl.ds(pl.multiple_of(index * rows, 16), rows)

        for w in range(BLOCK_WINDOWS):
            cells = pl.ds(w * WINDOW, WINDOW)
            queries = by_head(qkv_ref[kept, cells, :width] * BF16(score_scale))
            out_grad = by_head(att_ref[kept, cells, :])
            prob = prob_ref[kept, w]
            prob_grad = dot_nt(qkv_ref[kept, cells, 2 * width :], out_grad)
            score_grad = prob * (prob_grad - jnp.sum(prob_grad * prob, axis=0, keepdims=True))
            score_sum_ref[...] += score_grad
            score_grad = score_grad.astype(BF16)
            dqkv_ref[cells, :width] = (
                own_head(dot_tn(score_grad, qkv_ref[kept, cells, width : 2 * width])) * score_scale
            ).astype(BF16)
            dqkv_ref[cells, width : 2 * width] = dot_nn(score_grad, queries).astype(BF16)
            dqkv_ref[cells, 2 * width :] = dot_nn(prob.astype(BF16), out_grad).astype(BF16)
            yield

        dqkv = dqkv_ref[...]
        out_ref[slot, 1, here, :] = (
            middle_grad_ref[kept] + dot_nt(dqkv, w_qkv_ref[...])
        ).astype(BF16)
        add_grad(0, dot_tn(xw_ref[here, :].astype(BF16), dqkv))
        qkv_sums = column_sums(dqkv.astype(F32))
        sums = [qkv_sums[:, j * width : (j + 1) * width] for j in range(3)]
        small_ref[6:9, :] += jnp.concatenate(sums, axis=0)

    def together(*stages):
        stages = list(stages)
        while stages:
            for stage in list(stages):
                try:
                    next(stage)
                except StopIteration:
                    stages.remove(stage)

    blocks = col_count // WX // BLOCK_WINDOWS

    def plain_blocks(group):
        def block(index, carry):
            @pl.when((group == 0) & (index == 2))
            def _():
                rows_copy(1).start()
                corner_copies[1].start()

            together(forward(index, group, 0))
            together(backward(index, group, 0))
            return carry

        lax.fori_loop(0, blocks, block, 0)

    def last_blocks(group):
        def forwards(index, carry):
            together(forward(index, group, index))
            return carry

        def backwards(index, carry):
            stage = backward(index, group, index)
            for _ in range(BLOCK_WINDOWS // 2 + 1):
                next(stage)
            for step in range(hidden_steps):
                @pl.when(index == step)
                def _():
                    for p in early:
                        sum_step(p, step + 1)

            together(stage)
            return carry

        lax.fori_loop(0, blocks, forwards, 0)
        for p in early:
            sum_step(p, 0)
        lax.fori_loop(0, blocks, backwards, 0)
        for step in range(blocks, hidden_steps):
            for p in early:
                sum_step(p, step + 1)

    def gather(pair, group):
        def assemble(own, strip, axis):
            if group in (0, GROUPS - 1):
                return lax.slice_in_dim(own, HALF_Y, HALF_Y + WY, axis=axis)
            if TOWARD[pair] == 1:
                return jnp.concatenate([strip, lax.slice_in_dim(own, 0, HALF_Y, axis=axis)], axis=axis)
            return jnp.concatenate(
                [lax.slice_in_dim(own, row_count - HALF_Y, row_count, axis=axis), strip], axis=axis
            )

        for a, target in enumerate((xw_ref, gw_ref)):
            def field(start, count, z, a=a):
                own = fields_ref[a, field_level(pair, z), start : start + count].astype(F32)
                strip = None
                if group in (1, 2):
                    strip = rows_in_ref[pair, a, z, start * HALF_Y : (start + count) * HALF_Y, :]
                    strip = unpack_strip(strip.astype(F32), count)
                return assemble(own, strip, 1)

            def western(c, z, a=a):
                own = cols_in_ref[a, field_level(pair, z), c].astype(F32)
                strip = None
                if group in (1, 2):
                    place = ((z * 2 + a) * HALF_X + c) * HALF_Y
                    strip = corner_in_ref[pair].astype(F32)[place : place + HALF_Y]
                return assemble(own, strip, 0)

            store_windows(field, western, target)

    def send_back(pair, slot):
        sent = 0 if TOWARD[pair] == 1 else HALF_Y
        for a in range(2):
            for start in range(0, col_count - HALF_X, PACKED_COLS):
                count = min(PACKED_COLS, col_count - HALF_X - start)
                first = (start + HALF_X) * CELLS
                cells = out_ref[slot, a, first : first + count * CELLS, :].astype(F32)
                for z in range(WZ):
                    places = [c * CELLS + z * WY + sent for c in range(count)]
                    rows_out_ref[
                        pair, a, z, start * HALF_Y : (start + count) * HALF_Y, :
                    ] = jnp.concatenate(
                        [cells[p : p + HALF_Y] for p in places], axis=0
                    ).astype(BF16)
        back_copy(pair).start()

    def group_step(group, carry):
        pair, slot = group_pair(group), lax.rem(group, 2)
        inner = (group == 0) | (group == GROUPS - 1)

        @pl.when(group == 0)
        def _():
            corner_copies[0].start()
            cols_copy.wait_recv()

        @pl.when(group >= 2)
        def _():
            out_copy(group - 2).wait()
            edge_copy(group - 2).wait_send()

        @pl.when(group == GROUPS - 1)
        def _():
            corner_back_copy(0).wait_send()

        @pl.when(inner)
        def _():
            gather(pair, 0)

        for straddling in range(2):
            @pl.when(group == 1 + straddling)
            def _():
                rows_copy(straddling).wait_recv()
                corner_copies[straddling].wait_recv()
                gather(straddling, 1 + straddling)

        bases = [-HALF_Y if step == 1 else row_count - HALF_Y for step in TOWARD]
        base = jnp.where(inner, HALF_Y, jnp.where(group == 1, bases[0], bases[1]))
        score_bias_ref[...] = mask_scores(
            bias_ref[...], pair, base, lat, band_count, crop_ref, row_count
        )
        @pl.when(group < GROUPS - 1)
        def _():
            plain_blocks(group)

        @pl.when(group == GROUPS - 1)
        def _():
            last_blocks(group)

        out_copy(group).start()
        edge_copy(group).start()

        for straddling in range(2):
            @pl.when(group == 1 + straddling)
            def _():
                corner_back_copy(straddling).start()
                rows_copy(straddling).wait_send()
                send_back(straddling, slot)

        return carry

    lax.fori_loop(0, GROUPS, group_step, 0)
    late_step(0)
    small_ref[VECTORS:, : HEADS * OFFSETS] = table_grad(score_sum_ref)
    early_steps = 2 * halvings - hidden_steps
    for k in range(max(early_steps, 4, len(bits))):
        if k < len(bits):
            small_copy = to_partner(small_ref, small_recv_ref.at[k], small_sems.at[k], bits[k])
            small_copy.start()
        if k < early_steps:
            for p in early:
                sum_step(p, hidden_steps + 1 + k)
        late_step(k + 1)
        if k < len(bits):
            small_copy.wait()
            small_ref[...] += small_recv_ref[k]
    for group in (2, 3):
        out_copy(group).wait()
        edge_copy(group).wait_send()
    corner_back_copy(1).wait_send()
    cols_copy.wait_send()
    for copy in corner_copies:
        copy.wait_send()
    for pair in range(2):
        back_copy(pair).wait()
        corner_back_copy(pair).wait_recv()
    for group in range(GROUPS):
        edge_copy(group).wait_recv()


def block_call(crop_rows, tokens, cotangent, constants):
    level_count, col_count, row_count, width = tokens.shape
    vmem = pl.BlockSpec(memory_space=pltpu.VMEM)
    cells = col_count * CELLS
    rows = BLOCK_WINDOWS * WINDOW
    edge = -(-EDGE // 16) * 16
    blocks = col_count // WX // BLOCK_WINDOWS
    pairs = level_count // WZ
    strips = (pairs, 2, WZ, packed_rows(col_count), width)
    grad_rows = (4 * width + 2 * constants[4].shape[1]) * (width // LANES)
    bits, halvings = sum_bits()
    parts = sum_parts(width, constants[4].shape[1])
    more = max(1, len(bits) - halvings)
    late_rows = parts[2][1] // 2
    shard = max([count >> halvings for _, count in parts] + [late_rows // peer_sizes()[2]])
    half_rows = sum(halved(count, halvings)[1][-1] for _, count in parts)
    sends = pltpu.SemaphoreType.DMA
    return pl.pallas_call(
        block_kernel,
        in_specs=[pl.BlockSpec(memory_space=pltpu.SMEM), ANY, ANY] + [vmem] * len(constants),
        out_specs=[ANY] * 4 + [vmem] * 2,
        out_shape=[
            shape_of((2, GROUPS, cells, width), BF16),
            shape_of(strips, BF16),
            shape_of((GROUPS, 2, edge, width), BF16),
            shape_of((pairs, 2, edge, width), BF16),
            shape_of((grad_rows, LANES), BF16),
            shape_of((VECTORS + TABLE_ROWS, width), F32),
        ],
        scratch_shapes=[
            pltpu.VMEM((grad_rows, LANES), F32),
            pltpu.VMEM((half_rows, LANES), BF16),
            pltpu.VMEM((half_rows, LANES), BF16),
            pltpu.VMEM((2, len(parts), more, shard, LANES), BF16),
            pltpu.VMEM((max(1, len(bits)), VECTORS + TABLE_ROWS, width), F32),
            pltpu.VMEM((late_rows, LANES), BF16),
            pltpu.VMEM((peer_sizes()[2], late_rows // peer_sizes()[2], LANES), BF16),
            pltpu.VMEM((width, width), BF16),
            pltpu.VMEM((constants[4].shape[1], width), BF16),
            pltpu.VMEM((2,) + tokens.shape, BF16),
            pltpu.VMEM(strips, BF16),
            pltpu.VMEM(strips, BF16),
            pltpu.VMEM((2, level_count, HALF_X, row_count, width), BF16),
            pltpu.VMEM((pairs, edge, width), BF16),
            pltpu.VMEM((pairs, edge, width), BF16),
            pltpu.VMEM((2, 2, cells, width), BF16),
            pltpu.VMEM((WINDOW, SCORES), F32),
            pltpu.VMEM((cells, width), F32),
            pltpu.VMEM((cells, width), F32),
            pltpu.VMEM((blocks, rows, 3 * width), BF16),
            pltpu.VMEM((blocks, BLOCK_WINDOWS, WINDOW, SCORES), F32),
            pltpu.VMEM((blocks, rows, width), BF16),
            pltpu.VMEM((blocks, rows, width), F32),
            pltpu.VMEM((rows, 3 * width), BF16),
            pltpu.VMEM((WINDOW, SCORES), F32),
            sends((2 * level_count,)), sends((3, 2)), sends((pairs, 2)), sends((pairs, 2)),
            sends((GROUPS, 2)), sends((pairs, 2)), sends((GROUPS,)),
            sends((len(parts), len(bits) + halvings, 2)), sends((max(1, len(bits)), 2)),
            sends((2, peer_sizes()[2], 2)),
        ],
        cost_estimate=pl.CostEstimate(
            flops=GROUPS * cells * 5_200_000, bytes_accessed=32 * 2**20, transcendentals=0
        ),
        compiler_params=pltpu.CompilerParams(
            collective_id=1, has_side_effects=True, vmem_limit_bytes=VMEM_LIMIT
        ),
    )(crop_rows, tokens, cotangent, *constants)


def merge_kernel(
    inner_ref, straddle_ref, rows_ref, inner_edge_ref, straddle_edge_ref, corner_ref,
    grad_ref, small_ref, context_ref, *out_refs,
):
    fields, grads = out_refs[:2], out_refs[2:]
    _, col_count, row_count, width = fields[0].shape
    step = pl.program_id(0)

    def piece(rows_of, a, first_col, count, first, size):
        block = rows_of(a)[first_col * CELLS : (first_col + count) * CELLS, :].astype(F32)
        return block.reshape(count, CELLS, width)[:, first : first + size]

    straddle, inner = lambda a: straddle_ref.at[a, 0], lambda a: inner_ref.at[a, 0]
    straddle_edge, inner_edge, corner = (
        lambda a, ref=ref: ref.at[0, a] for ref in (straddle_edge_ref, inner_edge_ref, corner_ref)
    )
    for pair, z in ((0, 0), (0, 1), (1, 0), (1, 1)):
        @pl.when(step == pair * WZ + z)
        def _():
            first = z * WY
            kept, sent = (HALF_Y, 0) if TOWARD[pair] == 1 else (0, HALF_Y)

            def in_order(own, inner_rows, back):
                parts = [own, inner_rows, back] if TOWARD[pair] == 1 else [back, inner_rows, own]
                return jnp.concatenate(parts, axis=1).astype(BF16)

            for a, field in enumerate(fields):
                for start in range(0, col_count - HALF_X, PACKED_COLS):
                    count = min(PACKED_COLS, col_count - HALF_X - start)
                    strip = rows_ref[0, a, 0, start * HALF_Y : (start + count) * HALF_Y, :]
                    field[0, start : start + count] = in_order(
                        piece(straddle, a, start + HALF_X, count, first + kept, HALF_Y),
                        piece(inner, a, start + HALF_X, count, first, WY),
                        unpack_strip(strip.astype(F32), count),
                    )
                field[0, col_count - HALF_X :] = in_order(
                    piece(straddle_edge, a, 0, HALF_X, first + kept, HALF_Y),
                    piece(inner_edge, a, 0, HALF_X, first, WY),
                    piece(corner, a, 0, HALF_X, first + sent, HALF_Y),
                )

    grad_qkv, grad_proj, grad_up, grad_down, grad_mod, *vectors = grads

    def slab(index):
        per_slab = width // LANES
        return jnp.concatenate([
            grad_ref[j * width : (j + 1) * width, :].astype(F32)
            for j in range(index * per_slab, (index + 1) * per_slab)
        ], axis=1)

    @pl.when(step == 0)
    def _():
        for j in range(3):
            grad_qkv[:, j * width : (j + 1) * width] = slab(j)
        grad_proj[...] = slab(3)

    @pl.when(step == 1)
    def _():
        for j in range(grad_up.shape[1] // width):
            grad_up[:, j * width : (j + 1) * width] = slab(4 + j)

    @pl.when(step == 2)
    def _():
        for j in range(grad_down.shape[0] // width):
            grad_down[j * width : (j + 1) * width, :] = slab(8 + j).T

    @pl.when(step == 3)
    def _():
        lanes = context_ref.shape[1]
        for part in range(4):
            row = small_ref[part : part + 1, :]
            for j in range(0, width, lanes):
                grad_mod[:, part * width + j : part * width + j + lanes] = (
                    context_ref[...] * row[:, j : j + lanes]
                )
        mod_bias, proj_bias, down_bias, q_bias, v_bias, up_bias = vectors
        mod_bias[...] = jnp.concatenate([small_ref[i : i + 1, :] for i in range(4)], axis=1)
        up_bias[...] = jnp.concatenate([small_ref[i : i + 1, :] for i in range(9, 13)], axis=1)
        for ref, i in ((proj_bias, 4), (down_bias, 5), (q_bias, 6), (v_bias, 8)):
            ref[...] = small_ref[i : i + 1, :]


def merge(field_shape, hidden_width, windows, rows_back, edge_back, corner_back, grad, small, context):
    level_count, col_count, row_count, width = field_shape

    def level_of(i):
        return (i + WZ // 2) % level_count

    def group_of(pair, straddles):
        return 1 + pair if straddles else (GROUPS - 1) * pair

    def windows_of(straddles):
        return pl.BlockSpec(
            (2, 1) + windows.shape[2:], lambda i: (0, group_of(i // WZ, straddles), 0, 0)
        )

    def edge_of(straddles):
        return pl.BlockSpec(
            (1,) + edge_back.shape[1:], lambda i: (group_of(i // WZ, straddles), 0, 0, 0)
        )

    shapes = [
        (width, 3 * width), (width, width), (width, hidden_width), (hidden_width, width),
        (width, 4 * width), (1, 4 * width), (1, width), (1, width), (1, width), (1, width),
        (1, hidden_width),
    ]
    field = pl.BlockSpec((1,) + field_shape[1:], lambda i: (level_of(i), 0, 0, 0))
    return pl.pallas_call(
        merge_kernel,
        grid=(level_count,),
        in_specs=[
            windows_of(False), windows_of(True),
            pl.BlockSpec((1, 2, 1) + rows_back.shape[3:], lambda i: (i // WZ, 0, i % WZ, 0, 0)),
            edge_of(False), edge_of(True),
            pl.BlockSpec((1,) + corner_back.shape[1:], lambda i: (i // WZ, 0, 0, 0)),
        ] + [whole(v.shape) for v in (grad, small, context)],
        out_specs=[field, field] + [whole(s) for s in shapes],
        out_shape=[shape_of(field_shape, BF16)] * 2 + [shape_of(s, F32) for s in shapes],
        compiler_params=pltpu.CompilerParams(vmem_limit_bytes=VMEM_LIMIT),
    )(windows, windows, rows_back, edge_back, edge_back, corner_back, grad, small, context)


def on_device(
    tokens, cotangent, w_qkv, q_bias, v_bias, w_proj, b_proj, w_up, b_up, w_down, b_down,
    w_mod, b_mod, rel_table, crop_rows, lead_hours,
):
    fields = [field.transpose(0, 2, 1, 3) for field in (tokens, cotangent)]
    table = rel_table.transpose(1, 3, 0, 2)
    vectors = (b_mod, b_proj, b_down, q_bias, v_bias, b_up)
    bias, vecs, context = set_up(lead_hours, w_mod, vectors, table)
    constants = [bias, vecs, w_qkv, w_proj, w_up, w_down]
    windows, rows_back, edge_back, corner_back, grad, small = block_call(
        crop_rows, *fields, constants
    )
    (
        mixed, token_grad, grad_qkv, grad_proj, grad_up, grad_down, grad_mod, grad_mod_bias,
        grad_proj_bias, grad_down_bias, grad_q_bias, grad_v_bias, grad_up_bias,
    ) = merge(
        fields[0].shape, w_up.shape[1], windows, rows_back, edge_back, corner_back, grad, small, context
    )
    table_sum = small[VECTORS : VECTORS + 2 * WY - 1, : HEADS * OFFSETS][::-1]
    grad_table = table_sum.reshape(2 * WY - 1, 2 * WZ - 1, 2 * WX - 1, HEADS).transpose(3, 1, 0, 2)
    return (
        mixed.transpose(0, 2, 1, 3),
        token_grad.transpose(0, 2, 1, 3),
        grad_qkv,
        grad_q_bias[0],
        grad_v_bias[0],
        grad_proj,
        grad_proj_bias[0],
        grad_up,
        grad_up_bias[0],
        grad_down,
        grad_down_bias[0],
        grad_mod,
        grad_mod_bias[0],
        grad_table,
    )


def solution(mesh):
    split = P(None, "lat", "lon", None)
    return jax.shard_map(
        on_device,
        mesh=mesh,
        in_specs=(split, split) + (P(),) * 14,
        out_specs=(split, split) + (P(),) * 12,
        check_vma=False,
    )
```
